128 devices in a mesh: row: 8 (over y_hi, x), col: 16 (over z, y_lo, core).
Axes of the slice: x: 4, y: 4 (y_hi: 2, y_lo: 2; y = y_hi * 2 + y_lo), z: 4, core: 2. Of those that a mesh axis runs over, the one named last changes fastest.
Arguments:
- density: bfloat16 [2, 2944, 5888], P(None, 'row', 'col'), may hold values from -6 to 6
- pattern: int32 [2, 128, 256], P(None, 'row', 'col'), may hold values 0 or 1
- keep: int32 [2, 128, 256], P(None, 'row', 'col'), may hold values 0 or 1
- owner: int32 [128, 512, 1], P(('row', 'col')), may hold values from 0 to 127; in each aligned block of 512 rows (0 to 511, 512 to 1023, ..., all dimensions but the last counted through in order) at most 12 rows name the same one
Outputs:
- owned: bfloat16 [128, 128, 12, 529], P(('row', 'col'))
The draws below stay inside these ranges and needn't reach their ends.
Inputs may be any that keep to these rules, and one draw needn't show every extreme that they name: Within the blocks of one device, no owner is named more than 12 times.
All inputs are finite; a program needn't handle non-finite values. No bound on the sum of `pattern` or of `keep` on one device may be relied on, other than what follows from the above.
Results may differ from the reference program's by a relative error of at most 0.0022.
Values may be sent and summed in bfloat16 or wider, within the bound.
A program may use at most 64 MiB of HBM per device.

```python
import math
import jax
import jax.numpy as jnp
import numpy as np

BS = 23
PB = 16
NB = 256
ORDER = 5888
CAP = 12
N_ROW = 8
N_COL = 16


def with_ends(entries, rng, low, high):
    shape = entries.shape
    place = [jax.random.randint(jax.random.fold_in(rng, axis), (), 0, shape[axis]) for axis in range(len(shape))]
    entries = entries.at[tuple(place)].set(low)
    longest = shape.index(max(shape))
    place[longest] = (place[longest] + 1) % shape[longest]
    return entries.at[tuple(place)].set(high)


def level_of(stream_key, extent, pieces, low, largest):
    level = 1.0
    for axis_at, shards_of in pieces:
        heights = jax.random.uniform(jax.random.fold_in(jax.random.fold_in(stream_key, 6), axis_at), (shards_of,), jnp.float32, low / len(pieces), largest / len(pieces))
        level = level * jnp.repeat(jnp.exp(heights), extent[axis_at] // shards_of).reshape((-1,) + (1,) * (len(extent) - 1 - axis_at))
    return level


def routed_block(key, own, number, rows, count, top, bound, slope):
    order = jax.random.permutation(key, count)
    crowded, usual = shares(count, rows * top, bound, slope, True), shares(count, rows * top, bound, slope, False)
    places = jnp.arange(count)

    def named(tallies, turn):
        used = int((tallies > 0).sum())
        fixed = max(1, used // 4)
        passed = fixed + (places - fixed + turn * (used - fixed)) % max(1, count - fixed)
        return jnp.zeros((count,), jnp.int32).at[order[jnp.where(places < fixed, places, passed)]].set(jnp.asarray(tallies, jnp.int32))

    tallies = jnp.where(number % 4 == 0, named(crowded, number // 4), named(usual, number - number // 4 - 1))
    mixed = jax.random.permutation(jax.random.fold_in(own, 3), count)
    giver, sink = mixed[0:count // 2 * 2:2], mixed[1:count // 2 * 2:2]
    margin = jnp.minimum(tallies[giver] - 1, bound - tallies[sink]) // 2
    margin = jnp.where((giver == order[0]) | (sink == order[0]) | (tallies[sink] == 0), 0, jnp.maximum(margin, 0))
    passed = jax.random.randint(jax.random.fold_in(own, 4), (count // 2,), 0, 1 << 20) % (margin + 1)
    tallies = tallies.at[giver].add(-passed).at[sink].add(passed)
    members = jnp.searchsorted(jnp.cumsum(tallies), jnp.arange(rows * top), side="right").astype(jnp.int32)
    grid = members.reshape(top, rows).T
    grid = grid[jax.random.permutation(jax.random.fold_in(own, 1), rows)]
    turn = jax.random.randint(jax.random.fold_in(own, 2), (rows, 1), 0, top)
    return jnp.take_along_axis(grid, (jnp.arange(top)[None, :] + turn) % top, axis=1)


def shares(count, total, reach, slope, full):
    weights = [(1 << 20) // math.isqrt(standing ** slope) + 1 for standing in range(1, count + 1)]
    largest = reach if full else min(reach, max(-(-total // count), total * weights[0] // sum(weights)))
    least = 1 if total - largest >= count - 1 else 0
    given, surplus = [largest] + [least] * (count - 1), total - largest - least * (count - 1)
    while surplus > 0:
        free = [i for i in range(1, count) if given[i] < largest] or [i for i in range(1, count) if given[i] < reach]
        mass, left = sum([weights[i] for i in free]), surplus
        for i in free:
            more = min(reach - given[i], max(1, left * weights[i] // mass), surplus)
            given[i] = given[i] + more
            surplus = surplus - more
    return np.array(given)


def gaussian(key, extent, scale, most, cuts=(), kind=jnp.bfloat16):
    result = scale * jax.random.normal(key, extent, jnp.float32)
    if cuts:
        result = result * level_of(key, extent, cuts, -0.22, 0.18)
    return jnp.clip(result, -most, most).astype(kind)


def setup_inputs(seed: int = 0) -> dict:
    keys = jax.random.split(jax.random.key(seed), 5)
    density = gaussian(keys[0], (2, ORDER // 2, ORDER), 1.0, 6.0, ((1, 8), (2, 16)))
    pattern = with_ends((jax.random.randint(keys[1], (2, NB // 2, NB), 0, 4) < 3).astype(jnp.int32), jax.random.fold_in(keys[1], 1), 0, 1)
    keep = with_ends((jax.random.randint(keys[2], (2, NB // 2, NB), 0, 4) < 3).astype(jnp.int32), jax.random.fold_in(keys[2], 1), 0, 1)
    owner_keys = jax.random.split(jax.random.fold_in(keys[3], 1), (N_ROW * N_COL) * (2 * PB * PB) // (2 * PB * PB))
    owner_turns = jax.random.permutation(jax.random.fold_in(keys[3], 3), (N_ROW * N_COL) * (2 * PB * PB) // (2 * PB * PB))
    owner = jax.vmap(lambda own, number: routed_block(jax.random.fold_in(keys[3], 2), own, number, 2 * PB * PB, N_ROW * N_COL, 1, CAP, 2))(owner_keys, owner_turns).reshape((N_ROW * N_COL, 2 * PB * PB, 1))
    return {"density": density, "pattern": pattern, "keep": keep, "owner": owner}


def expand(mask):
    grown = jnp.repeat(jnp.repeat(mask, BS, axis=0), BS, axis=1)
    return grown.astype(jnp.bfloat16)


def reference(density, pattern, keep, owner):
    devices = N_ROW * N_COL
    matrix = density.reshape(ORDER, ORDER)
    mask_pat = expand(pattern.reshape(NB, NB))
    mat = matrix * mask_pat
    square = jnp.dot(mat, mat, preferred_element_type=jnp.float32) / ORDER
    square = (square * mask_pat.astype(jnp.float32)).astype(jnp.bfloat16)
    cube = jnp.dot(mat, square, preferred_element_type=jnp.float32)
    mask_keep = expand(keep.reshape(NB, NB)).astype(jnp.float32)
    update = (mask_keep * (1.5 * mat.astype(jnp.float32) - 0.5 * cube)).astype(jnp.bfloat16)
    blocks = update.reshape(2, N_ROW, PB, BS, N_COL, PB, BS)
    blocks = blocks.transpose(1, 4, 0, 2, 5, 3, 6).reshape(devices, 2 * PB * PB, BS * BS)
    targets = owner[:, :, 0].astype(jnp.int32)
    onehot = (targets[:, :, None] == jnp.arange(devices, dtype=jnp.int32)[None, None, :]).astype(jnp.int32)
    ranks = jnp.cumsum(onehot, axis=1) - onehot
    slots = jnp.sum(ranks * onehot, axis=2).astype(jnp.int32)
    sources = jnp.broadcast_to(jnp.arange(devices, dtype=jnp.int32)[:, None], targets.shape)
    owned = jnp.zeros((devices, devices, CAP, BS * BS), jnp.bfloat16)
    return owned.at[targets, sources, slots].set(blocks)
```

```python
import jax
import jax.numpy as jnp
from jax import lax
from jax.experimental import pallas as pl
from jax.experimental.pallas import tpu as pltpu
from jax.sharding import PartitionSpec as P

BS = 23
PB = 16
W = BS * PB
WP = 384
ORDER = 5888
NROW = 8
NCOL = 16
DEVICES = NROW * NCOL
CAP = 12
CAPP = 16
ENT = BS * BS
ENTP = 640
MESH = pl.DeviceIdType.MESH
F32 = jnp.float32
BF16 = jnp.bfloat16


def grow_columns(mask):
    block = lax.broadcasted_iota(jnp.int32, (PB, WP), 0)
    col = lax.broadcasted_iota(jnp.int32, (PB, WP), 1)
    spread = jnp.where((col >= block * BS) & (col < block * BS + BS), 1.0, 0.0).astype(BF16)
    return jnp.dot(mask, spread, preferred_element_type=F32).astype(BF16)


def grow(mask):
    wide = grow_columns(mask.astype(F32).astype(BF16))
    row = lax.broadcasted_iota(jnp.int32, (W, PB), 0)
    block = lax.broadcasted_iota(jnp.int32, (W, PB), 1)
    spread = jnp.where((row >= block * BS) & (row < block * BS + BS), 1.0, 0.0).astype(BF16)
    return jnp.dot(spread, wide, preferred_element_type=F32)


def products(dens, pat, keep, out, left, right, sq, relay, mask, acc, send, recv):
    r = lax.axis_index("row")
    c = lax.axis_index("col")
    x, yh = lax.rem(r, 4), lax.div(r, 4)
    z, yl, core = lax.div(c, 4), lax.rem(lax.div(c, 2), 2), lax.rem(c, 2)

    def col(dz, dyl, dcore):
        ycol = (1 - yl) if dyl else yl
        ccol = (1 - core) if dcore else core
        return lax.rem(z + dz + 4, 4) * 4 + ycol * 2 + ccol

    def row(dx, dyh):
        yrow = (1 - yh) if dyh else yh
        return yrow * 4 + lax.rem(x + dx + 4, 4)

    sib = (r, col(0, 0, 1))
    ya = (r, col(0, 1, 0))
    yb = (row(0, 1), col(0, 1, 0))
    zs = {1: (r, col(1, 0, 0)), -1: (r, col(-1, 0, 0))}
    xs = {1: (row(1, 0), c), -1: (row(-1, 0), c)}

    numbers = {}
    started = {}
    arriving = {}

    def at(buf, slot, h):
        return buf.at[slot, h, pl.ds(0, W)]

    def copy(name, src, dst, dev, here):
        k = numbers.setdefault(name, len(numbers))
        op = pltpu.make_async_remote_copy(
            src_ref=src, dst_ref=dst, send_sem=send.at[k], recv_sem=recv.at[k],
            device_id=dev, device_id_type=MESH)
        op.start()
        started[name] = op
        arriving[name] = pltpu.make_async_remote_copy(
            src_ref=here, dst_ref=here, send_sem=send.at[k], recv_sem=recv.at[k],
            device_id=dev, device_id_type=MESH)

    def got(name):
        arriving[name].wait_recv()

    barrier = pltpu.get_barrier_semaphore()
    for dev in (sib, ya, yb, zs[1], zs[-1], xs[1], xs[-1]):
        pl.semaphore_signal(barrier, inc=1, device_id=dev, device_id_type=MESH)

    for h in range(2):
        m = grow(pat[h])
        mask[h] = m.astype(BF16)
        left[c, h, :, pl.ds(256, 128)] = jnp.zeros((W, 128), BF16)
        left[c, h, :, pl.ds(0, W)] = dens[h] * m[:, :W].astype(BF16)
        right[r, h, pl.ds(0, W)] = left[c, h]
    zero = jnp.zeros((2, WP - W, WP), BF16)

    def clear(k, carry):
        right[k, :, pl.ds(W, WP - W)] = zero
        sq[k, :, pl.ds(W, WP - W)] = zero
        return carry

    lax.fori_loop(0, NROW, clear, 0)
    pl.semaphore_wait(barrier, 7)

    def send_left(name, h, dev, there, here):
        s = col(*there)
        copy((name, h), at(left, s, h), at(left, s, h), dev, at(left, col(*here), h))

    def send_sib(h, dz, dyl):
        send_left(("c", dz, dyl), h, sib, (dz, dyl, 0), (dz, dyl, 1))

    def send_row(buf, name, h, dev, there, here):
        s = row(*there)
        copy((name, h), at(buf, s, h), at(buf, s, h), dev, at(buf, row(*here), h))

    for h in range(2):
        send_left("a", h, ya, (0, 0, 0), (0, 1, 0))
        for d in (1, -1):
            send_left(("z", d), h, zs[d], (0, 0, 0), (-d, 0, 0))
            send_row(right, ("x", d), h, xs[d], (0, 0), (-d, 0))
        send_sib(h, 0, 0)

    for h in range(2):
        got(("a", h))
        copy(("b", h), at(left, col(0, 1, 0), h), at(right, r, h), yb, at(right, row(0, 1), h))
        for d in (1, -1):
            send_left(("za", d), h, zs[d], (0, 1, 0), (-d, 1, 0))
        send_sib(h, 0, 1)
        for d in (1, -1):
            got((("z", d), h))
            if (h == 0) == (d == 1):
                send_left(("f", d), h, zs[d], (-d, 0, 0), (-2 * d, 0, 0))
            send_sib(h, -d, 0)
            got((("x", d), h))
            if (h == 0) == (d == 1):
                send_row(right, ("g", d), h, xs[d], (-d, 0), (-2 * d, 0))
    for h in range(2):
        got(("b", h))
        for d in (1, -1):
            send_row(right, ("xb", d), h, xs[d], (0, 1), (-d, 1))
    for h in range(2):
        for d in (1, -1):
            got((("za", d), h))
            if (h == 0) == (d == 1):
                send_left(("fa", d), h, zs[d], (-d, 1, 0), (-2 * d, 1, 0))
            send_sib(h, -d, 1)
    for h, d in ((0, 1), (1, -1)):
        got((("f", d), h))
        send_sib(h, 2, 0)
    for h in range(2):
        for d in (1, -1):
            got((("xb", d), h))
            if (h == 0) == (d == 1):
                send_row(right, ("gb", d), h, xs[d], (-d, 1), (-2 * d, 1))
    for h, d in ((0, 1), (1, -1)):
        got((("fa", d), h))
        send_sib(h, 2, 1)
    for h, d in ((0, 1), (1, -1)):
        got((("g", d), h))
    for h, d in ((0, 1), (1, -1)):
        got((("gb", d), h))
    for dz in (0, 1, -1, 2):
        for dyl in (0, 1):
            for h in range(2):
                got((("c", dz, dyl), h))

    def first(k, carry):
        term = jnp.dot(left[k].reshape(2 * W, WP), right[lax.rem(k, NROW), lax.div(k, NROW)],
                       preferred_element_type=F32)
        acc[...] += term
        return carry

    acc[...] = jnp.zeros_like(acc)
    lax.fori_loop(0, NCOL, first, 0)

    for h in range(2):
        sq[r, h, pl.ds(0, W)] = (acc[pl.ds(h * W, W), :] / ORDER * mask[h].astype(F32)).astype(BF16)
        near, far = (ya, yb) if h == 0 else (yb, ya)
        copy(("p", h), at(sq, r, h), relay.at[h], near, relay.at[h])
        for d in (1, -1):
            send_row(sq, ("sx", d), h, xs[d], (0, 0), (-d, 0))
    for h in range(2):
        got(("p", h))
        far = yb if h == 0 else ya
        slot = r if h == 0 else row(0, 1)
        copy(("q", h), relay.at[h], at(sq, slot, h), far, at(sq, row(0, 1), h))
    for h in range(2):
        for d in (1, -1):
            got((("sx", d), h))
            if (h == 0) == (d == 1):
                send_row(sq, ("sg", d), h, xs[d], (-d, 0), (-2 * d, 0))
    for h in range(2):
        got(("q", h))
        for d in (1, -1):
            send_row(sq, ("sxb", d), h, xs[d], (0, 1), (-d, 1))

    acc[...] = jnp.zeros_like(acc)

    def second(slot):
        for h in range(2):
            acc[...] += jnp.dot(left[h * NROW + slot].reshape(2 * W, WP), sq[slot, h],
                                preferred_element_type=F32)

    for dx, dyh in ((0, 0), (1, 0), (-1, 0), (0, 1)):
        second(row(dx, dyh))
    for h in range(2):
        for d in (1, -1):
            got((("sxb", d), h))
            if (h == 0) == (d == 1):
                send_row(sq, ("sgb", d), h, xs[d], (-d, 1), (-2 * d, 1))
    for h, d in ((0, 1), (1, -1)):
        got((("sg", d), h))
    for dx, dyh in ((1, 1), (-1, 1), (2, 0)):
        second(row(dx, dyh))
    for h, d in ((0, 1), (1, -1)):
        got((("sgb", d), h))
    second(row(2, 1))

    for h in range(2):
        mat = left[c, h].astype(F32)
        new = grow(keep[h]) * (1.5 * mat - 0.5 * acc[pl.ds(h * W, W), :])
        for k in range(WP // 128):
            out[h, k] = new[:, k * 128 : k * 128 + 128]
    for op in started.values():
        op.wait_send()


N_COPIES = 60


def two_products(density, pattern, keep):
    vmem = pl.BlockSpec(memory_space=pltpu.VMEM)
    return pl.pallas_call(
        products,
        out_shape=jax.ShapeDtypeStruct((2, WP // 128, W, 128), F32),
        in_specs=[vmem] * 3,
        out_specs=vmem,
        scratch_shapes=[
            pltpu.VMEM((NCOL, 2, W, WP), BF16),
            pltpu.VMEM((NROW, 2, WP, WP), BF16),
            pltpu.VMEM((NROW, 2, WP, WP), BF16),
            pltpu.VMEM((2, W, WP), BF16),
            pltpu.VMEM((2, W, WP), BF16),
            pltpu.VMEM((2 * W, WP), F32),
            pltpu.SemaphoreType.DMA((N_COPIES,)),
            pltpu.SemaphoreType.DMA((N_COPIES,)),
        ],
        compiler_params=pltpu.CompilerParams(
            collective_id=0, has_side_effects=True, vmem_limit_bytes=48 * 1024 * 1024),
        name="two_products",
    )(density, pattern, keep)


def route(update, owner_col, owner_row, out, blocks):
    bc = lax.broadcasted_iota(jnp.int32, (PB, WP), 0)
    col = lax.broadcasted_iota(jnp.int32, (PB, WP), 1)
    pick = jnp.where((col >= bc * BS) & (col < bc * BS + BS), 1.0, 0.0)[None]
    lane = lax.broadcasted_iota(jnp.int32, (WP, 256), 0)
    shift = lax.broadcasted_iota(jnp.int32, (WP, 256), 1) - (lane - lane // BS * BS)
    for w in range(3):
        base = w * 256
        total = jnp.zeros((2 * PB * PB, 256), F32)
        for i in range(BS):
            if i * BS + BS <= base or i * BS >= base + 256:
                continue
            place = jnp.where(shift == i * BS - base, 1.0, 0.0).astype(BF16)
            rows = []
            for h in range(2):
                u = jnp.concatenate(
                    [update[h, k, pl.ds(i, PB, stride=BS), :] for k in range(WP // 128)], axis=1)
                rows.append((u[:, None, :] * pick).astype(BF16).reshape(PB * PB, WP))
            total = total + jnp.dot(jnp.concatenate(rows, axis=0), place, preferred_element_type=F32)
        n = min(256, ENTP - base)
        blocks[:, pl.ds(base, n)] = total[:, :n].astype(BF16)

    n = 2 * PB * PB
    same = owner_col[...] == owner_row[...]
    earlier = lax.broadcasted_iota(jnp.int32, (n, n), 0) < lax.broadcasted_iota(jnp.int32, (n, n), 1)
    rank = jnp.sum(jnp.where(same & earlier, 1.0, 0.0), axis=0, keepdims=True).astype(jnp.int32)
    key = owner_row[...] * CAPP + rank
    step = 512
    for k in range(0, DEVICES * CAPP, step):
        at = lax.broadcasted_iota(jnp.int32, (step, n), 0) + k
        hot = jnp.where(at == key, 1.0, 0.0).astype(BF16)
        out[pl.ds(k, step), :] = jnp.dot(hot, blocks[...], preferred_element_type=F32).astype(BF16)


def routed(update, owner):
    vmem = pl.BlockSpec(memory_space=pltpu.VMEM)
    owner = owner.reshape(-1)
    return pl.pallas_call(
        route,
        out_shape=jax.ShapeDtypeStruct((DEVICES * CAPP, ENTP), BF16),
        in_specs=[vmem] * 3,
        out_specs=vmem,
        scratch_shapes=[pltpu.VMEM((2 * PB * PB, ENTP), BF16)],
        compiler_params=pltpu.CompilerParams(vmem_limit_bytes=48 * 1024 * 1024),
        name="route",
    )(update, owner[:, None], owner[None, :])


def per_device(density, pattern, keep, owner):
    update = two_products(density, pattern, keep)
    outgoing = routed(update, owner).reshape(DEVICES, CAPP, ENTP)
    outgoing = outgoing[:, :CAP, :ENT]
    arrived = lax.all_to_all(outgoing, ("row", "col"), split_axis=0, concat_axis=0, tiled=True)
    return arrived[None]


def solution(mesh):
    placed = (
        P(None, "row", "col"),
        P(None, "row", "col"),
        P(None, "row", "col"),
        P(("row", "col"), None, None),
    )
    return jax.shard_map(
        per_device,
        mesh=mesh,
        in_specs=placed,
        out_specs=P(("row", "col"), None, None, None),
        check_vma=False,
    )
```

```python
import jax
import jax.numpy as jnp
from jax import lax
from jax.experimental import pallas as pl
from jax.experimental.pallas import tpu as pltpu
from jax.sharding import PartitionSpec as P

BS = 23
PB = 16
W = BS * PB
WP = 384
ORDER = 5888
NROW = 8
NCOL = 16
DEVICES = NROW * NCOL
CAP = 12
ENT = BS * BS
ROWS = 16
LANES = 512
MESH = pl.DeviceIdType.MESH
F32 = jnp.float32
BF16 = jnp.bfloat16


def grow_columns(mask):
    block = lax.broadcasted_iota(jnp.int32, (PB, WP), 0)
    col = lax.broadcasted_iota(jnp.int32, (PB, WP), 1)
    spread = jnp.where((col >= block * BS) & (col < block * BS + BS), 1.0, 0.0).astype(BF16)
    return jnp.dot(mask, spread, preferred_element_type=F32).astype(BF16)


def grow(mask):
    wide = grow_columns(mask.astype(F32).astype(BF16))
    row = lax.broadcasted_iota(jnp.int32, (W, PB), 0)
    block = lax.broadcasted_iota(jnp.int32, (W, PB), 1)
    spread = jnp.where((row >= block * BS) & (row < block * BS + BS), 1.0, 0.0).astype(BF16)
    return jnp.dot(spread, wide, preferred_element_type=F32)


def products(dens, pat, keep, out, left, right, sq, relay, mask, acc, send, recv):
    r = lax.axis_index("row")
    c = lax.axis_index("col")
    x, yh = lax.rem(r, 4), lax.div(r, 4)
    z, yl, core = lax.div(c, 4), lax.rem(lax.div(c, 2), 2), lax.rem(c, 2)

    def col(dz, dyl, dcore):
        ycol = (1 - yl) if dyl else yl
        ccol = (1 - core) if dcore else core
        return lax.rem(z + dz + 4, 4) * 4 + ycol * 2 + ccol

    def row(dx, dyh):
        yrow = (1 - yh) if dyh else yh
        return yrow * 4 + lax.rem(x + dx + 4, 4)

    sib = (r, col(0, 0, 1))
    ya = (r, col(0, 1, 0))
    yb = (row(0, 1), col(0, 1, 0))
    zs = {1: (r, col(1, 0, 0)), -1: (r, col(-1, 0, 0))}
    xs = {1: (row(1, 0), c), -1: (row(-1, 0), c)}

    numbers = {}
    started = {}
    arriving = {}

    def at(buf, slot, h):
        return buf.at[slot, h, pl.ds(0, W)]

    def copy(name, src, dst, dev, here):
        k = numbers.setdefault(name, len(numbers))
        op = pltpu.make_async_remote_copy(
            src_ref=src, dst_ref=dst, send_sem=send.at[k], recv_sem=recv.at[k],
            device_id=dev, device_id_type=MESH)
        op.start()
        started[name] = op
        arriving[name] = pltpu.make_async_remote_copy(
            src_ref=here, dst_ref=here, send_sem=send.at[k], recv_sem=recv.at[k],
            device_id=dev, device_id_type=MESH)

    def got(name):
        arriving[name].wait_recv()

    barrier = pltpu.get_barrier_semaphore()
    for dev in (sib, ya, yb, zs[1], zs[-1], xs[1], xs[-1]):
        pl.semaphore_signal(barrier, inc=1, device_id=dev, device_id_type=MESH)

    for h in range(2):
        m = grow(pat[h])
        mask[h] = m.astype(BF16)
        left[c, h, :, pl.ds(256, 128)] = jnp.zeros((W, 128), BF16)
        left[c, h, :, pl.ds(0, W)] = dens[h] * m[:, :W].astype(BF16)
        right[r, h, pl.ds(0, W)] = left[c, h]
    zero = jnp.zeros((2, WP - W, WP), BF16)

    def clear(k, carry):
        right[k, :, pl.ds(W, WP - W)] = zero
        sq[k, :, pl.ds(W, WP - W)] = zero
        return carry

    lax.fori_loop(0, NROW, clear, 0)
    pl.semaphore_wait(barrier, 7)

    def send_left(name, h, dev, there, here):
        s = col(*there)
        copy((name, h), at(left, s, h), at(left, s, h), dev, at(left, col(*here), h))

    def send_sib(h, dz, dyl):
        send_left(("c", dz, dyl), h, sib, (dz, dyl, 0), (dz, dyl, 1))

    def send_row(buf, name, h, dev, there, here):
        s = row(*there)
        copy((name, h), at(buf, s, h), at(buf, s, h), dev, at(buf, row(*here), h))

    for h in range(2):
        send_left("a", h, ya, (0, 0, 0), (0, 1, 0))
        for d in (1, -1):
            send_left(("z", d), h, zs[d], (0, 0, 0), (-d, 0, 0))
            send_row(right, ("x", d), h, xs[d], (0, 0), (-d, 0))
        send_sib(h, 0, 0)

    for h in range(2):
        got(("a", h))
        copy(("b", h), at(left, col(0, 1, 0), h), at(right, r, h), yb, at(right, row(0, 1), h))
        for d in (1, -1):
            send_left(("za", d), h, zs[d], (0, 1, 0), (-d, 1, 0))
        send_sib(h, 0, 1)
        for d in (1, -1):
            got((("z", d), h))
            if (h == 0) == (d == 1):
                send_left(("f", d), h, zs[d], (-d, 0, 0), (-2 * d, 0, 0))
            send_sib(h, -d, 0)
            got((("x", d), h))
            if (h == 0) == (d == 1):
                send_row(right, ("g", d), h, xs[d], (-d, 0), (-2 * d, 0))
    for h in range(2):
        got(("b", h))
        for d in (1, -1):
            send_row(right, ("xb", d), h, xs[d], (0, 1), (-d, 1))
    for h in range(2):
        for d in (1, -1):
            got((("za", d), h))
            if (h == 0) == (d == 1):
                send_left(("fa", d), h, zs[d], (-d, 1, 0), (-2 * d, 1, 0))
            send_sib(h, -d, 1)
    for h, d in ((0, 1), (1, -1)):
        got((("f", d), h))
        send_sib(h, 2, 0)
    for h in range(2):
        for d in (1, -1):
            got((("xb", d), h))
            if (h == 0) == (d == 1):
                send_row(right, ("gb", d), h, xs[d], (-d, 1), (-2 * d, 1))
    for h, d in ((0, 1), (1, -1)):
        got((("fa", d), h))
        send_sib(h, 2, 1)
    for h, d in ((0, 1), (1, -1)):
        got((("g", d), h))
    for h, d in ((0, 1), (1, -1)):
        got((("gb", d), h))
    for dz in (0, 1, -1, 2):
        for dyl in (0, 1):
            for h in range(2):
                got((("c", dz, dyl), h))

    def first(k, carry):
        term = jnp.dot(left[k].reshape(2 * W, WP), right[lax.rem(k, NROW), lax.div(k, NROW)],
                       preferred_element_type=F32)
        acc[...] += term
        return carry

    acc[...] = jnp.zeros_like(acc)
    lax.fori_loop(0, NCOL, first, 0)

    for h in range(2):
        sq[r, h, pl.ds(0, W)] = (acc[pl.ds(h * W, W), :] / ORDER * mask[h].astype(F32)).astype(BF16)
        near = ya if h == 0 else yb
        copy(("p", h), at(sq, r, h), relay.at[h], near, relay.at[h])
        for d in (1, -1):
            send_row(sq, ("sx", d), h, xs[d], (0, 0), (-d, 0))
    for h in range(2):
        got(("p", h))
        far = yb if h == 0 else ya
        slot = r if h == 0 else row(0, 1)
        copy(("q", h), relay.at[h], at(sq, slot, h), far, at(sq, row(0, 1), h))
    for h in range(2):
        for d in (1, -1):
            got((("sx", d), h))
            if (h == 0) == (d == 1):
                send_row(sq, ("sg", d), h, xs[d], (-d, 0), (-2 * d, 0))
    for h in range(2):
        got(("q", h))
        for d in (1, -1):
            send_row(sq, ("sxb", d), h, xs[d], (0, 1), (-d, 1))

    acc[...] = jnp.zeros_like(acc)

    def second(slot):
        for h in range(2):
            acc[...] += jnp.dot(left[h * NROW + slot].reshape(2 * W, WP), sq[slot, h],
                                preferred_element_type=F32)

    for dx, dyh in ((0, 0), (1, 0), (-1, 0), (0, 1)):
        second(row(dx, dyh))
    for h in range(2):
        for d in (1, -1):
            got((("sxb", d), h))
            if (h == 0) == (d == 1):
                send_row(sq, ("sgb", d), h, xs[d], (-d, 1), (-2 * d, 1))
    for h, d in ((0, 1), (1, -1)):
        got((("sg", d), h))
    for dx, dyh in ((1, 1), (-1, 1), (2, 0)):
        second(row(dx, dyh))
    for h, d in ((0, 1), (1, -1)):
        got((("sgb", d), h))
    second(row(2, 1))

    for h in range(2):
        mat = left[c, h].astype(F32)
        new = grow(keep[h]) * (1.5 * mat - 0.5 * acc[pl.ds(h * W, W), :])
        for k in range(WP // 128):
            out[h, k] = new[:, k * 128 : k * 128 + 128]
    for op in started.values():
        op.wait_send()


N_COPIES = 60


def two_products(density, pattern, keep):
    vmem = pl.BlockSpec(memory_space=pltpu.VMEM)
    return pl.pallas_call(
        products,
        out_shape=jax.ShapeDtypeStruct((2, WP // 128, W, 128), F32),
        in_specs=[vmem] * 3,
        out_specs=vmem,
        scratch_shapes=[
            pltpu.VMEM((NCOL, 2, W, WP), BF16),
            pltpu.VMEM((NROW, 2, WP, WP), BF16),
            pltpu.VMEM((NROW, 2, WP, WP), BF16),
            pltpu.VMEM((2, W, WP), BF16),
            pltpu.VMEM((2, W, WP), BF16),
            pltpu.VMEM((2 * W, WP), F32),
            pltpu.SemaphoreType.DMA((N_COPIES,)),
            pltpu.SemaphoreType.DMA((N_COPIES,)),
        ],
        compiler_params=pltpu.CompilerParams(
            collective_id=0, has_side_effects=True, vmem_limit_bytes=48 * 1024 * 1024),
        name="two_products",
    )(density, pattern, keep)


def route(update, owner_col, owner_row, out, blocks):
    n = 2 * PB * PB
    bc = lax.broadcasted_iota(jnp.int32, (PB, WP), 0)
    col = lax.broadcasted_iota(jnp.int32, (PB, WP), 1)
    pick = jnp.where((col >= bc * BS) & (col < bc * BS + BS), 1.0, 0.0)[None]
    lane = lax.broadcasted_iota(jnp.int32, (WP, 256), 0)
    shift = lax.broadcasted_iota(jnp.int32, (WP, 256), 1) - (lane - lane // BS * BS)
    same = owner_col[...] == owner_row[...]
    one = lax.broadcasted_iota(jnp.int32, (n, n), 0)
    two = lax.broadcasted_iota(jnp.int32, (n, n), 1)
    rank = jnp.sum(jnp.where(same & (one < two), 1.0, 0.0), axis=0, keepdims=True).astype(jnp.int32)
    rank_col = jnp.sum(jnp.where(same & (two < one), 1.0, 0.0), axis=1, keepdims=True).astype(jnp.int32)
    for w in range(3):
        base = w * 256
        total = jnp.zeros((n, 256), F32)
        for i in range(BS):
            if i * BS + BS <= base or i * BS >= base + 256:
                continue
            place = jnp.where(shift == i * BS - base, 1.0, 0.0).astype(BF16)
            rows = []
            for h in range(2):
                u = jnp.concatenate(
                    [update[h, k, pl.ds(i, PB, stride=BS), :] for k in range(WP // 128)], axis=1)
                rows.append((u[:, None, :] * pick).astype(BF16).reshape(PB * PB, WP))
            total = total + jnp.dot(jnp.concatenate(rows, axis=0), place, preferred_element_type=F32)
        if w < 2:
            blocks[pl.ds(0, n), pl.ds(base, 256)] = total.astype(BF16)
        else:
            for k in range(4):
                mine = (rank_col >= 3 * k) & (rank_col < 3 * k + 3)
                blocks[pl.ds(n, n), pl.ds(128 * k, 128)] = jnp.where(mine, total[:, :128], 0.0).astype(BF16)

    third = rank - lax.div(rank, 3) * 3
    key = owner_row[...] * ROWS + rank
    tail_key = owner_row[...] * ROWS + CAP + third
    step = 512
    for k in range(0, DEVICES * ROWS, step):
        at = lax.broadcasted_iota(jnp.int32, (step, n), 0) + k
        head = jnp.where(at == key, 1.0, 0.0).astype(BF16)
        tail = jnp.where(at == tail_key, 1.0, 0.0).astype(BF16)
        hot = jnp.concatenate([head, tail], axis=1)
        out[pl.ds(k, step), :] = jnp.dot(hot, blocks[...], preferred_element_type=F32).astype(BF16)


def routed(update, owner):
    vmem = pl.BlockSpec(memory_space=pltpu.VMEM)
    owner = owner.reshape(-1)
    return pl.pallas_call(
        route,
        out_shape=jax.ShapeDtypeStruct((DEVICES * ROWS, LANES), BF16),
        in_specs=[vmem] * 3,
        out_specs=vmem,
        scratch_shapes=[pltpu.VMEM((4 * PB * PB, LANES), BF16)],
        compiler_params=pltpu.CompilerParams(vmem_limit_bytes=48 * 1024 * 1024),
        name="route",
    )(update, owner[:, None], owner[None, :])


def exchange(outgoing, arrived, send, recv, own):
    r = lax.axis_index("row")
    c = lax.axis_index("col")
    x, yh = lax.rem(r, 4), lax.div(r, 4)
    z, yl, core = lax.div(c, 4), lax.rem(lax.div(c, 2), 2), lax.rem(c, 2)
    me = r * NCOL + c

    def partner(i, sign):
        dcore, dz = lax.rem(i, 2), lax.rem(lax.div(i, 2), 4)
        dyl, dyh, dx = lax.rem(lax.div(i, 8), 2), lax.rem(lax.div(i, 16), 2), lax.div(i, 32)
        row = lax.rem(yh + dyh, 2) * 4 + lax.rem(x + sign * dx + 4, 4)
        col = lax.rem(z + sign * dz + 4, 4) * 4 + lax.rem(yl + dyl, 2) * 2 + lax.rem(core + dcore, 2)
        return row, col

    def copy(i):
        row, col = partner(i, 1)
        at = pl.multiple_of((row * NCOL + col) * ROWS, ROWS)
        return pltpu.make_async_remote_copy(
            src_ref=outgoing.at[pl.ds(at, ROWS)],
            dst_ref=arrived.at[pl.ds(pl.multiple_of(me * ROWS, ROWS), ROWS)],
            send_sem=send.at[i], recv_sem=recv.at[i], device_id=(row, col), device_id_type=MESH)

    def arrival(i):
        row, col = partner(i, -1)
        here = arrived.at[pl.ds(pl.multiple_of((row * NCOL + col) * ROWS, ROWS), ROWS)]
        return pltpu.make_async_remote_copy(
            src_ref=here, dst_ref=here, send_sem=send.at[i], recv_sem=recv.at[i],
            device_id=(row, col), device_id_type=MESH)

    barrier = pltpu.get_barrier_semaphore()

    def greet(i, carry):
        pl.semaphore_signal(barrier, inc=1, device_id=partner(i, 1), device_id_type=MESH)
        return carry

    lax.fori_loop(1, DEVICES, greet, 0)
    mine = pl.ds(pl.multiple_of(me * ROWS, ROWS), ROWS)
    keep = pltpu.make_async_copy(outgoing.at[mine], arrived.at[mine], own)
    keep.start()
    pl.semaphore_wait(barrier, DEVICES - 1)

    def start(i, carry):
        copy(lax.rem(i * 45, DEVICES)).start()
        return carry

    def finish(i, carry):
        arrival(lax.rem(i * 45, DEVICES)).wait_recv()
        return carry

    def sent(i, carry):
        copy(i).wait_send()
        return carry

    lax.fori_loop(1, DEVICES, start, 0)
    keep.wait()
    lax.fori_loop(1, DEVICES, finish, 0)
    lax.fori_loop(1, DEVICES, sent, 0)


def exchanged(outgoing):
    vmem = pl.BlockSpec(memory_space=pltpu.VMEM)
    return pl.pallas_call(
        exchange,
        out_shape=jax.ShapeDtypeStruct(outgoing.shape, outgoing.dtype),
        in_specs=[vmem],
        out_specs=vmem,
        scratch_shapes=[
            pltpu.SemaphoreType.DMA((DEVICES,)),
            pltpu.SemaphoreType.DMA((DEVICES,)),
            pltpu.SemaphoreType.DMA,
        ],
        compiler_params=pltpu.CompilerParams(
            collective_id=1, has_side_effects=True, vmem_limit_bytes=32 * 1024 * 1024),
        name="exchange",
    )(outgoing)


def unpack(arrived, out, wide):
    for k in range(LANES // 128):
        wide[k] = arrived[:, pl.ds(128 * k, 128)].astype(F32)
    for s in range(CAP):
        for k in range(LANES // 128):
            part = wide[k, pl.ds(s, DEVICES, stride=ROWS), :]
            out[s, pl.ds(128 * k, 128), :] = part.T.astype(BF16)
        tail = wide[s // 3, pl.ds(CAP + s % 3, DEVICES, stride=ROWS), :]
        out[s, pl.ds(LANES, ENT - LANES), :] = tail.T[: ENT - LANES].astype(BF16)


def unpacked(arrived):
    vmem = pl.BlockSpec(memory_space=pltpu.VMEM)
    out = pl.pallas_call(
        unpack,
        out_shape=jax.ShapeDtypeStruct((CAP, ENT, DEVICES), BF16),
        in_specs=[vmem],
        out_specs=vmem,
        scratch_shapes=[pltpu.VMEM((LANES // 128, DEVICES * ROWS, 128), F32)],
        compiler_params=pltpu.CompilerParams(vmem_limit_bytes=32 * 1024 * 1024),
        name="unpack",
    )(arrived)
    return out.transpose(2, 0, 1)[None]


def per_device(density, pattern, keep, owner):
    update = two_products(density, pattern, keep)
    return unpacked(exchanged(routed(update, owner)))


def solution(mesh):
    placed = (
        P(None, "row", "col"),
        P(None, "row", "col"),
        P(None, "row", "col"),
        P(("row", "col"), None, None),
    )
    return jax.shard_map(
        per_device,
        mesh=mesh,
        in_specs=placed,
        out_specs=P(("row", "col"), None, None, None),
        check_vma=False,
    )
```

```python
import jax
import jax.numpy as jnp
from jax import lax
from jax.experimental import pallas as pl
from jax.experimental.pallas import tpu as pltpu
from jax.sharding import PartitionSpec as P

BS = 23
PB = 16
W = BS * PB
WP = 384
ORDER = 5888
NROW = 8
NCOL = 16
DEVICES = NROW * NCOL
CAP = 12
ENT = BS * BS
ROWS = 16
LANES = 512
SPLIT1 = 288
SPLIT2 = 240
MESH = pl.DeviceIdType.MESH
F32 = jnp.float32
BF16 = jnp.bfloat16


def grow_columns(mask):
    block = lax.broadcasted_iota(jnp.int32, (PB, WP), 0)
    col = lax.broadcasted_iota(jnp.int32, (PB, WP), 1)
    spread = jnp.where((col >= block * BS) & (col < block * BS + BS), 1.0, 0.0).astype(BF16)
    return jnp.dot(mask, spread, preferred_element_type=F32).astype(BF16)


def grow(mask):
    wide = grow_columns(mask.astype(F32).astype(BF16))
    row = lax.broadcasted_iota(jnp.int32, (W, PB), 0)
    block = lax.broadcasted_iota(jnp.int32, (W, PB), 1)
    spread = jnp.where((row >= block * BS) & (row < block * BS + BS), 1.0, 0.0).astype(BF16)
    return jnp.dot(spread, wide, preferred_element_type=F32)


def whole_step(
    dens_in, pat_in, keep_in, owner_in, arrived,
    dens, pat, keep, owner, left, right, sq, mask, kept, acc, update, place, hot, blocks, outgoing,
    send, recv, exchange_send, exchange_recv, local,
):
    r = lax.axis_index("row")
    c = lax.axis_index("col")
    x, yh = lax.rem(r, 4), lax.div(r, 4)
    z, yl, core = lax.div(c, 4), lax.rem(lax.div(c, 2), 2), lax.rem(c, 2)
    me = r * NCOL + c

    def col(dz, dyl, dcore=0):
        ycol = (1 - yl) if dyl else yl
        ccol = (1 - core) if dcore else core
        return lax.rem(z + dz + 4, 4) * 4 + ycol * 2 + ccol

    def row(dx, dyh):
        yrow = (1 - yh) if dyh else yh
        return yrow * 4 + lax.rem(x + dx + 4, 4)

    sib = (r, col(0, 0, 1))
    ya = (r, col(0, 1))
    yb = (row(0, 1), col(0, 1))
    yy = (row(0, 1), c)
    zs = {1: (r, col(1, 0)), -1: (r, col(-1, 0))}
    xs = {1: (row(1, 0), c), -1: (row(-1, 0), c)}

    fetches = [
        pltpu.make_async_copy(src, dst, local.at[k])
        for k, (src, dst) in enumerate(((pat_in, pat), (dens_in, dens), (keep_in, keep), (owner_in, owner)))
    ]
    for fetch in fetches:
        fetch.start()
    barrier = pltpu.get_barrier_semaphore()
    for dev in (sib, ya, yb, yy, zs[1], zs[-1], xs[1], xs[-1]):
        pl.semaphore_signal(barrier, inc=1, device_id=dev, device_id_type=MESH)

    started = []
    arriving = {}

    def start(name, src, dst, dev, here):
        k = len(started)
        op = pltpu.make_async_remote_copy(
            src_ref=src, dst_ref=dst, send_sem=send.at[k], recv_sem=recv.at[k],
            device_id=dev, device_id_type=MESH)
        op.start()
        started.append(op)
        arriving[name] = pltpu.make_async_remote_copy(
            src_ref=here, dst_ref=here, send_sem=send.at[k], recv_sem=recv.at[k],
            device_id=dev, device_id_type=MESH)

    def got(*names):
        for name in names:
            arriving[name].wait_recv()

    ALL, LO, HI = (0, W), (0, SPLIT1), (SPLIT1, W)
    LO2, HI2 = (0, SPLIT2), (SPLIT2, W)

    def part(buf, slot, h, rows):
        return buf.at[slot, h, pl.ds(rows[0], rows[1] - rows[0])]

    def go_left(name, dev, there, here, h, rows=ALL):
        s = col(*there)
        start((name, h, rows), part(left, s, h, rows), part(left, s, h, rows), dev, part(left, col(*here), h, rows))

    def go_sib(h, dz, dyl):
        go_left(("c", dz, dyl), sib, (dz, dyl, 0), (dz, dyl, 1), h)

    def go(buf, name, dev, there, here, h, rows=ALL):
        s = row(*there)
        start((name, h, rows), part(buf, s, h, rows), part(buf, s, h, rows), dev, part(buf, row(*here), h, rows))

    fetches[0].wait()
    fetches[1].wait()
    for h in range(2):
        m = grow(pat[h]).astype(BF16)
        left[c, h, :, pl.ds(256, 128)] = jnp.zeros((W, 128), BF16)
        left[c, h, :, pl.ds(0, W)] = dens[h] * m[:, :W]
        mask[h] = m
        if h == 0:
            pl.semaphore_wait(barrier, 8)
        go_left("a", ya, (0, 0), (0, 1), h)
        for d in (1, -1):
            go_left(("z", d), zs[d], (0, 0), (-d, 0), h)
            start((("x", d), h, ALL), part(left, c, h, ALL), part(right, r, h, ALL), xs[d], part(right, row(-d, 0), h, ALL))
        go_sib(h, 0, 0)

    for h in range(2):
        right[r, h, pl.ds(0, W)] = left[c, h]
    zero = jnp.zeros((2, WP - W, WP), BF16)

    def clear(k, carry):
        right[k, :, pl.ds(W, WP - W)] = zero
        sq[k, :, pl.ds(W, WP - W)] = zero
        return carry

    lax.fori_loop(0, NROW, clear, 0)
    acc[...] = jnp.zeros_like(acc)
    fetches[2].wait()
    fetches[3].wait()
    for h in range(2):
        kept[h] = grow(keep[h]).astype(BF16)

    got(("a", 0, ALL))
    start(("b", 0, ALL), part(left, col(0, 1), 0, ALL), part(right, r, 0, ALL), yb, part(right, row(0, 1), 0, ALL))
    go_left(("za", -1), zs[-1], (0, 1), (1, 1), 0)
    go_sib(0, 0, 1)
    got((("z", 1), 0, ALL))
    go_left(("ay", 1), ya, (-1, 0), (-1, 1), 0, LO)
    go_sib(0, -1, 0)
    got((("z", -1), 0, ALL))
    go_sib(0, 1, 0)
    got((("x", 1), 0, ALL))
    go(right, ("g", 1), xs[1], (-1, 0), (2, 0), 0)
    go(right, ("ys", 1), yy, (-1, 0), (-1, 1), 0, LO)
    got((("x", -1), 0, ALL))
    routing_tables(owner, place, hot)
    got(("a", 1, ALL))
    start(("b", 1, ALL), part(left, col(0, 1), 1, ALL), part(right, r, 1, ALL), yb, part(right, row(0, 1), 1, ALL))
    go_left(("za", 1), zs[1], (0, 1), (-1, 1), 1)
    go_left(("za", 1), zs[1], (0, 1), (-1, 1), 0, HI)
    go_sib(1, 0, 1)
    got((("z", 1), 1, ALL))
    go_left(("f", 1), zs[1], (-1, 0), (2, 0), 0)
    go_sib(1, -1, 0)
    got((("z", -1), 1, ALL))
    go_left(("f", -1), zs[-1], (1, 0), (2, 0), 1)
    go_left(("ay", -1), ya, (1, 0), (1, 1), 1, LO)
    go_left(("za", -1), zs[-1], (0, 1), (1, 1), 1, HI)
    go_sib(1, 1, 0)
    got(("b", 0, ALL))
    go(right, ("xb", -1), xs[-1], (0, 1), (1, 1), 0)
    go(right, ("xb", 1), xs[1], (0, 1), (-1, 1), 0, HI)
    got((("x", 1), 1, ALL), (("x", -1), 1, ALL))
    go(right, ("g", -1), xs[-1], (1, 0), (2, 0), 1)
    go(right, ("ys", -1), yy, (1, 0), (1, 1), 1, LO)
    got(("b", 1, ALL))
    go(right, ("xb", 1), xs[1], (0, 1), (-1, 1), 1, LO)
    go(right, ("xb", 1), xs[1], (0, 1), (-1, 1), 1, HI)
    go(right, ("xb", -1), xs[-1], (0, 1), (1, 1), 1, HI)
    got((("za", -1), 0, ALL))
    go_left(("fa", -1), zs[-1], (1, 1), (2, 1), 0)
    go_sib(0, 1, 1)
    got((("za", 1), 1, ALL))
    go_left(("fa", 1), zs[1], (-1, 1), (2, 1), 1)
    go_sib(1, -1, 1)
    got((("xb", -1), 0, ALL))
    go(right, ("gb", -1), xs[-1], (1, 1), (2, 1), 0)
    got((("f", 1), 0, ALL))
    go_sib(0, 2, 0)
    got((("f", -1), 1, ALL))
    go_sib(1, 2, 0)
    got((("xb", 1), 1, LO))
    go(right, ("gb", 1), xs[1], (-1, 1), (2, 1), 1, LO)
    got((("xb", 1), 1, HI))
    go(right, ("gb", 1), xs[1], (-1, 1), (2, 1), 1, HI)
    got((("za", 1), 0, HI), (("ay", 1), 0, LO))
    go_sib(0, -1, 1)
    got((("za", -1), 1, HI), (("ay", -1), 1, LO))
    go_sib(1, 1, 1)
    got((("g", 1), 0, ALL), (("g", -1), 1, ALL))
    got((("xb", 1), 0, HI), (("ys", 1), 0, LO), (("xb", -1), 1, HI), (("ys", -1), 1, LO))
    for h in range(2):
        got(*[(("c", dz, dyl), h, ALL) for dz in (0, 1, -1, 2) for dyl in (0, 1) if (dz, dyl) != (2, 1)])

    def multiply(p, buf):
        two = jnp.concatenate([left[2 * p].reshape(2 * W, WP), left[2 * p + 1].reshape(2 * W, WP)], axis=1)
        rows = buf[pl.ds(lax.rem(2 * p, NROW), 2), lax.div(p, 4)].reshape(2 * WP, WP)
        acc[...] += jnp.dot(two, rows, preferred_element_type=F32)

    def is_late(p):
        zp, yp = lax.div(p, 2), lax.rem(p, 2)
        in_left = (zp == lax.rem(z + 2, 4)) & (yp == 1 - yl)
        in_right = (lax.rem(zp, 2) == 1 - yh) & (yp == lax.div(lax.rem(x + 2, 4), 2))
        return in_left | in_right

    def early(p, carry):
        @pl.when(jnp.logical_not(is_late(p)))
        def _():
            multiply(p, right)
        return carry

    def late(p, carry):
        @pl.when(is_late(p))
        def _():
            multiply(p, right)
        return carry

    lax.fori_loop(0, NCOL // 2, early, 0)
    got((("fa", -1), 0, ALL))
    go_sib(0, 2, 1)
    got((("fa", 1), 1, ALL))
    go_sib(1, 2, 1)
    got((("gb", -1), 0, ALL), (("gb", 1), 1, LO), (("gb", 1), 1, HI))
    got((("c", 2, 1), 0, ALL), (("c", 2, 1), 1, ALL))
    lax.fori_loop(0, NCOL // 2, late, 0)

    for h in range(2):
        sq[r, h, pl.ds(0, W)] = (acc[pl.ds(h * W, W), :] / ORDER * mask[h].astype(F32)).astype(BF16)
        for d in (1, -1):
            go(sq, ("sx", d), xs[d], (0, 0), (-d, 0), h)
        go(sq, "sy", yy, (0, 0), (0, 1), h)
    acc[...] = jnp.zeros_like(acc)
    got(("sy", 0, ALL))
    go(sq, ("sxb", -1), xs[-1], (0, 1), (1, 1), 0, LO2)
    got((("sx", 1), 0, ALL))
    go(sq, ("sys", 1), yy, (-1, 0), (-1, 1), 0)
    got((("sx", -1), 0, ALL))
    got(("sy", 1, ALL))
    go(sq, ("sxb", 1), xs[1], (0, 1), (-1, 1), 1, LO2)
    got((("sx", 1), 1, ALL))
    go(sq, ("sg", 1), xs[1], (-1, 0), (2, 0), 0)
    go(sq, ("sye", 1), yy, (-1, 0), (-1, 1), 1, HI2)
    go(sq, ("sye", -1), yy, (1, 0), (1, 1), 0, HI2)
    got((("sx", -1), 1, ALL))
    go(sq, ("sg", -1), xs[-1], (1, 0), (2, 0), 1)
    go(sq, ("sys", -1), yy, (1, 0), (1, 1), 1)

    def second(yhp, pair):
        for h in range(2):
            multiply((2 * h + yhp) * 2 + pair, sq)

    near = lax.div(x, 2)
    second(yh, near)
    got((("sxb", -1), 0, LO2))
    go(sq, ("sgb", -1), xs[-1], (1, 1), (2, 1), 0, LO2)
    got((("sxb", 1), 1, LO2))
    go(sq, ("sgb", 1), xs[1], (-1, 1), (2, 1), 1, LO2)
    got((("sye", -1), 0, HI2))
    go(sq, ("sgb", -1), xs[-1], (1, 1), (2, 1), 0, HI2)
    got((("sye", 1), 1, HI2))
    go(sq, ("sgb", 1), xs[1], (-1, 1), (2, 1), 1, HI2)
    got((("sg", 1), 0, ALL), (("sg", -1), 1, ALL))
    second(yh, 1 - near)
    got((("sys", 1), 0, ALL), (("sys", -1), 1, ALL))
    second(1 - yh, near)
    got(*[(("sgb", d), h, rows) for d, h in ((-1, 0), (1, 1)) for rows in (LO2, HI2)])
    second(1 - yh, 1 - near)

    for h in range(2):
        mat = left[c, h].astype(F32)
        new = kept[h].astype(F32) * (1.5 * mat - 0.5 * acc[pl.ds(h * W, W), :])
        for k in range(WP // 128):
            update[h, k] = new[:, k * 128 : k * 128 + 128]

    fill(update, owner, place, hot, blocks, outgoing)

    def partner(i, sign):
        dcore, dz = lax.rem(i, 2), lax.rem(lax.div(i, 2), 4)
        dyl, dyh, dx = lax.rem(lax.div(i, 8), 2), lax.rem(lax.div(i, 16), 2), lax.div(i, 32)
        to_row = lax.rem(yh + dyh, 2) * 4 + lax.rem(x + sign * dx + 4, 4)
        to_col = lax.rem(z + sign * dz + 4, 4) * 4 + lax.rem(yl + dyl, 2) * 2 + lax.rem(core + dcore, 2)
        return to_row, to_col

    def rows_of(buf, device):
        return buf.at[pl.ds(pl.multiple_of(device * ROWS, ROWS), ROWS)]

    def message(i):
        to_row, to_col = partner(i, 1)
        return pltpu.make_async_remote_copy(
            src_ref=rows_of(outgoing, to_row * NCOL + to_col), dst_ref=rows_of(arrived, me),
            send_sem=exchange_send.at[i], recv_sem=exchange_recv.at[i],
            device_id=(to_row, to_col), device_id_type=MESH)

    def arrival(i):
        from_row, from_col = partner(i, -1)
        here = rows_of(arrived, from_row * NCOL + from_col)
        return pltpu.make_async_remote_copy(
            src_ref=here, dst_ref=here, send_sem=exchange_send.at[i], recv_sem=exchange_recv.at[i],
            device_id=(from_row, from_col), device_id_type=MESH)

    def start_message(i, carry):
        message(lax.rem(i * 37, DEVICES)).start()
        return carry

    def finish_message(i, carry):
        arrival(lax.rem(i * 37, DEVICES)).wait_recv()
        return carry

    def message_sent(i, carry):
        message(i).wait_send()
        return carry

    lax.fori_loop(1, DEVICES, start_message, 0)
    own = pltpu.make_async_copy(rows_of(outgoing, me), rows_of(arrived, me), local.at[4])
    own.start()
    for op in started:
        op.wait_send()
    own.wait()
    lax.fori_loop(1, DEVICES, finish_message, 0)
    lax.fori_loop(1, DEVICES, message_sent, 0)


N_BLOCKS = 2 * PB * PB
WINDOWS = [
    (w, i) for w in range(3) for i in range(BS) if i * BS + BS > w * 256 and i * BS < w * 256 + 256
]


def ranks(owner_row):
    owner = jnp.broadcast_to(owner_row.astype(F32), (8, N_BLOCKS))
    same = owner.T[:, :1] == owner[:1]
    one = lax.broadcasted_iota(jnp.int32, (N_BLOCKS, N_BLOCKS), 0)
    two = lax.broadcasted_iota(jnp.int32, (N_BLOCKS, N_BLOCKS), 1)
    rank = jnp.sum(jnp.where(same & (one < two), 1.0, 0.0), axis=0, keepdims=True).astype(jnp.int32)
    rank_col = jnp.sum(jnp.where(same & (two < one), 1.0, 0.0), axis=1, keepdims=True).astype(jnp.int32)
    return rank, rank_col


def routing_tables(owner, place, hot):
    lane = lax.broadcasted_iota(jnp.int32, (WP, 256), 0)
    shift = lax.broadcasted_iota(jnp.int32, (WP, 256), 1) - (lane - lax.div(lane, BS) * BS)
    for k, (w, i) in enumerate(WINDOWS):
        place[k] = jnp.where(shift == i * BS - w * 256, 1.0, 0.0).astype(BF16)
    rank, _ = ranks(owner[...])
    third = rank - lax.div(rank, 3) * 3
    key = owner[...] * ROWS + rank
    tail_key = owner[...] * ROWS + CAP + third
    step = 512
    for k in range(0, DEVICES * ROWS, step):
        at = lax.broadcasted_iota(jnp.int32, (step, N_BLOCKS), 0) + k
        hot[pl.ds(k, step), pl.ds(0, N_BLOCKS)] = jnp.where(at == key, 1.0, 0.0).astype(BF16)
        hot[pl.ds(k, step), pl.ds(N_BLOCKS, N_BLOCKS)] = jnp.where(at == tail_key, 1.0, 0.0).astype(BF16)


def fill(update, owner, place, hot, blocks, outgoing):
    n = N_BLOCKS
    bc = lax.broadcasted_iota(jnp.int32, (PB, WP), 0)
    entry = lax.broadcasted_iota(jnp.int32, (PB, WP), 1)
    pick = jnp.where((entry >= bc * BS) & (entry < bc * BS + BS), 1.0, 0.0)[None]
    _, rank_col = ranks(owner[...])
    for w in range(3):
        total = jnp.zeros((n, 256), F32)
        for k, (wk, i) in enumerate(WINDOWS):
            if wk != w:
                continue
            rows = []
            for h in range(2):
                u = jnp.concatenate(
                    [update[h, j, pl.ds(i, PB, stride=BS), :] for j in range(WP // 128)], axis=1)
                rows.append((u[:, None, :] * pick).astype(BF16).reshape(PB * PB, WP))
            total = total + jnp.dot(jnp.concatenate(rows, axis=0), place[k], preferred_element_type=F32)
        if w < 2:
            blocks[pl.ds(0, n), pl.ds(256 * w, 256)] = total.astype(BF16)
        else:
            for j in range(4):
                mine = (rank_col >= 3 * j) & (rank_col < 3 * j + 3)
                blocks[pl.ds(n, n), pl.ds(128 * j, 128)] = jnp.where(mine, total[:, :128], 0.0).astype(BF16)
    step = 512
    for k in range(0, DEVICES * ROWS, step):
        outgoing[pl.ds(k, step), :] = jnp.dot(
            hot[pl.ds(k, step), :], blocks[...], preferred_element_type=F32).astype(BF16)


N_COPIES = 72


def stepped(density, pattern, keep, owner):
    anywhere = pl.BlockSpec(memory_space=pl.ANY)
    owner = owner.reshape(1, N_BLOCKS)
    return pl.pallas_call(
        whole_step,
        out_shape=jax.ShapeDtypeStruct((DEVICES * ROWS, LANES), BF16),
        in_specs=[anywhere] * 4,
        out_specs=pl.BlockSpec(memory_space=pltpu.VMEM),
        scratch_shapes=[
            pltpu.VMEM(density.shape, BF16),
            pltpu.VMEM(pattern.shape, jnp.int32),
            pltpu.VMEM(keep.shape, jnp.int32),
            pltpu.VMEM(owner.shape, jnp.int32),
            pltpu.VMEM((NCOL, 2, W, WP), BF16),
            pltpu.VMEM((NROW, 2, WP, WP), BF16),
            pltpu.VMEM((NROW, 2, WP, WP), BF16),
            pltpu.VMEM((2, W, WP), BF16),
            pltpu.VMEM((2, W, WP), BF16),
            pltpu.VMEM((2 * W, WP), F32),
            pltpu.VMEM((2, WP // 128, W, 128), F32),
            pltpu.VMEM((len(WINDOWS), WP, 256), BF16),
            pltpu.VMEM((DEVICES * ROWS, 2 * N_BLOCKS), BF16),
            pltpu.VMEM((2 * N_BLOCKS, LANES), BF16),
            pltpu.VMEM((DEVICES * ROWS, LANES), BF16),
            pltpu.SemaphoreType.DMA((N_COPIES,)),
            pltpu.SemaphoreType.DMA((N_COPIES,)),
            pltpu.SemaphoreType.DMA((DEVICES,)),
            pltpu.SemaphoreType.DMA((DEVICES,)),
            pltpu.SemaphoreType.DMA((5,)),
        ],
        compiler_params=pltpu.CompilerParams(
            collective_id=0, has_side_effects=True, vmem_limit_bytes=54 * 1024 * 1024),
        name="whole_step",
    )(density, pattern, keep, owner)


def unpack(arrived, out, wide):
    for k in range(LANES // 128):
        wide[k] = arrived[:, pl.ds(128 * k, 128)].astype(F32)
    for s in range(CAP):
        for k in range(LANES // 128):
            part = wide[k, pl.ds(s, DEVICES, stride=ROWS), :]
            out[s, pl.ds(128 * k, 128), :] = part.T.astype(BF16)
        tail = wide[s // 3, pl.ds(CAP + s % 3, DEVICES, stride=ROWS), :]
        out[s, pl.ds(LANES, ENT - LANES), :] = tail.T[: ENT - LANES].astype(BF16)


def unpacked(arrived):
    vmem = pl.BlockSpec(memory_space=pltpu.VMEM)
    out = pl.pallas_call(
        unpack,
        out_shape=jax.ShapeDtypeStruct((CAP, ENT, DEVICES), BF16),
        in_specs=[vmem],
        out_specs=vmem,
        scratch_shapes=[pltpu.VMEM((LANES // 128, DEVICES * ROWS, 128), F32)],
        compiler_params=pltpu.CompilerParams(vmem_limit_bytes=32 * 1024 * 1024),
        name="unpack",
    )(arrived)
    return out.transpose(2, 0, 1)[None]


def per_device(density, pattern, keep, owner):
    return unpacked(stepped(density, pattern, keep, owner))


def solution(mesh):
    placed = (
        P(None, "row", "col"),
        P(None, "row", "col"),
        P(None, "row", "col"),
        P(("row", "col"), None, None),
    )
    return jax.shard_map(
        per_device,
        mesh=mesh,
        in_specs=placed,
        out_specs=P(("row", "col"), None, None, None),
        check_vma=False,
    )
```

```python
import jax
import jax.numpy as jnp
from jax import lax
from jax.experimental import pallas as pl
from jax.experimental.pallas import tpu as pltpu
from jax.sharding import PartitionSpec as P

BS = 23
PB = 16
W = BS * PB
WP = 384
ORDER = 5888
NROW = 8
NCOL = 16
DEVICES = NROW * NCOL
CAP = 12
ENT = BS * BS
ROWS = 16
LANES = 384
TAIL = 21
MESH = pl.DeviceIdType.MESH
F32 = jnp.float32
BF16 = jnp.bfloat16


QUARTERS = ((0, 0, 192), (0, 192, W), (1, 0, 192), (1, 192, W))

OWN, SEND, WAIT, DO = range(4)
LEFT, SIBLING, RIGHT, SQUARE = range(4)
CORE, YA, YB, YY, ZP, ZM, XP, XM = range(8)
PREPARE, EARLY, NEAR_OWN, FAR_OWN, NEAR_OTHER, FAR_OTHER = range(6)
FIRST_GATHER = (
    (OWN, 0), (SEND, LEFT, 1, 0, 0, LEFT, 0, 0, ZM), (SEND, LEFT, -1, 0, 0, LEFT, 0, 0, ZP),
    (SEND, RIGHT, -1, 0, 0, RIGHT, 0, 0, XP), (SEND, LEFT, -1, 0, 1, LEFT, 0, 0, ZP),
    (SEND, RIGHT, 1, 0, 1, RIGHT, 0, 0, XM), (SEND, LEFT, 0, 1, 0, LEFT, 0, 0, YA),
    (SEND, LEFT, 1, 0, 1, LEFT, 0, 0, ZM), (SEND, RIGHT, 1, 0, 0, RIGHT, 0, 0, XM),
    (SEND, RIGHT, -1, 0, 1, RIGHT, 0, 0, XP), (SEND, LEFT, 0, 1, 1, LEFT, 0, 0, YA),
    (SEND, SIBLING, 0, 0, 0, LEFT, 0, 0, CORE), (SEND, SIBLING, 0, 0, 1, LEFT, 0, 0, CORE), (OWN, 1),
    (SEND, SIBLING, 0, 0, 2, LEFT, 0, 0, CORE), (SEND, SIBLING, 0, 0, 3, LEFT, 0, 0, CORE), (DO, PREPARE),
    (SEND, RIGHT, -1, 0, 2, RIGHT, 0, 0, XP), (SEND, LEFT, 1, 0, 2, LEFT, 0, 0, ZM),
    (SEND, RIGHT, 1, 0, 2, RIGHT, 0, 0, XM), (SEND, LEFT, 0, 1, 3, LEFT, 0, 0, YA),
    (SEND, LEFT, -1, 0, 2, LEFT, 0, 0, ZP), (WAIT, SIBLING, 0, 0, 0), (WAIT, SIBLING, 0, 0, 1),
    (WAIT, SIBLING, 0, 0, 2), (WAIT, SIBLING, 0, 0, 3), (WAIT, LEFT, 1, 0, 0),
    (SEND, SIBLING, 1, 0, 0, LEFT, 1, 0, CORE), (WAIT, LEFT, -1, 0, 0), (SEND, SIBLING, -1, 0, 0, LEFT, -1, 0, CORE),
    (SEND, LEFT, 2, 0, 0, LEFT, 1, 0, ZM), (WAIT, RIGHT, 1, 0, 1), (SEND, LEFT, 0, 1, 2, LEFT, 0, 0, YA),
    (SEND, RIGHT, -1, 0, 3, RIGHT, 0, 0, XP), (SEND, RIGHT, 1, 0, 3, RIGHT, 0, 0, XM),
    (SEND, LEFT, -1, 0, 3, LEFT, 0, 0, ZP), (WAIT, RIGHT, -1, 0, 0), (WAIT, LEFT, 0, 1, 0),
    (SEND, RIGHT, 0, 1, 0, LEFT, 0, 1, YB), (SEND, SIBLING, 0, 1, 0, LEFT, 0, 1, CORE), (WAIT, SIBLING, 1, 0, 0),
    (WAIT, SIBLING, -1, 0, 0), (WAIT, LEFT, 1, 0, 1), (SEND, SIBLING, 1, 0, 1, LEFT, 1, 0, CORE),
    (WAIT, SIBLING, 0, 1, 0), (WAIT, LEFT, -1, 0, 1), (SEND, SIBLING, -1, 0, 1, LEFT, -1, 0, CORE),
    (WAIT, RIGHT, -1, 0, 1), (SEND, LEFT, 2, 0, 1, LEFT, -1, 0, ZP), (SEND, LEFT, 1, 0, 3, LEFT, 0, 0, ZM),
    (SEND, RIGHT, 2, 0, 1, RIGHT, 1, 0, XM), (WAIT, RIGHT, 1, 0, 0), (SEND, LEFT, 1, 1, 0, LEFT, 1, 0, YA),
    (WAIT, LEFT, 0, 1, 1), (SEND, RIGHT, 0, 1, 1, LEFT, 0, 1, YB), (SEND, SIBLING, 0, 1, 1, LEFT, 0, 1, CORE),
    (WAIT, SIBLING, 1, 0, 1), (WAIT, SIBLING, -1, 0, 1), (WAIT, SIBLING, 0, 1, 1), (WAIT, LEFT, 1, 0, 2),
    (SEND, SIBLING, 1, 0, 2, LEFT, 1, 0, CORE), (SEND, LEFT, -1, 1, 1, LEFT, 0, 1, ZP),
    (SEND, LEFT, 2, 0, 2, LEFT, 1, 0, ZM), (WAIT, LEFT, -1, 0, 2), (SEND, RIGHT, 2, 0, 0, RIGHT, 1, 0, XM),
    (SEND, SIBLING, -1, 0, 2, LEFT, -1, 0, CORE), (WAIT, RIGHT, -1, 0, 2), (SEND, RIGHT, 2, 0, 2, RIGHT, -1, 0, XP),
    (WAIT, LEFT, 0, 1, 3), (SEND, SIBLING, 0, 1, 3, LEFT, 0, 1, CORE), (SEND, LEFT, 1, 1, 1, LEFT, 1, 0, YA),
    (SEND, RIGHT, 0, 1, 3, LEFT, 0, 1, YB), (WAIT, RIGHT, 1, 0, 2), (WAIT, RIGHT, 0, 1, 0),
    (SEND, RIGHT, -1, 1, 0, RIGHT, 0, 1, XP), (WAIT, SIBLING, 1, 0, 2), (WAIT, SIBLING, -1, 0, 2),
    (WAIT, SIBLING, 0, 1, 3), (WAIT, LEFT, -1, 0, 3), (SEND, LEFT, -1, 1, 3, LEFT, 0, 1, ZP),
    (SEND, SIBLING, -1, 0, 3, LEFT, -1, 0, CORE), (WAIT, RIGHT, -1, 0, 3), (WAIT, LEFT, 2, 0, 0),
    (SEND, LEFT, 1, 1, 3, LEFT, 0, 1, ZM), (SEND, SIBLING, 2, 0, 0, LEFT, 2, 0, CORE), (WAIT, RIGHT, 1, 0, 3),
    (SEND, RIGHT, 1, 1, 0, RIGHT, 0, 1, XM), (SEND, LEFT, -1, 1, 0, LEFT, -1, 0, YA), (WAIT, RIGHT, 0, 1, 1),
    (SEND, RIGHT, -1, 1, 1, RIGHT, 0, 1, XP), (WAIT, LEFT, 0, 1, 2), (SEND, RIGHT, 0, 1, 2, LEFT, 0, 1, YB),
    (SEND, SIBLING, 0, 1, 2, LEFT, 0, 1, CORE), (WAIT, SIBLING, -1, 0, 3), (WAIT, SIBLING, 2, 0, 0),
    (WAIT, LEFT, 2, 0, 1), (SEND, SIBLING, 2, 0, 1, LEFT, 2, 0, CORE), (SEND, LEFT, -1, 1, 2, LEFT, 0, 1, ZP),
    (WAIT, SIBLING, 0, 1, 2), (WAIT, LEFT, 1, 0, 3), (SEND, LEFT, 2, 0, 3, LEFT, 1, 0, ZM),
    (SEND, SIBLING, 1, 0, 3, LEFT, 1, 0, CORE), (WAIT, RIGHT, 2, 0, 1), (WAIT, RIGHT, 0, 1, 3),
    (SEND, RIGHT, -1, 1, 3, RIGHT, 0, 1, XP), (SEND, RIGHT, 1, 1, 3, RIGHT, 0, 1, XM),
    (SEND, RIGHT, 1, 1, 2, RIGHT, 1, 0, YY), (WAIT, RIGHT, 2, 0, 2), (WAIT, LEFT, 1, 1, 0),
    (SEND, SIBLING, 1, 1, 0, LEFT, 1, 1, CORE), (WAIT, SIBLING, 2, 0, 1), (WAIT, SIBLING, 1, 0, 3),
    (WAIT, SIBLING, 1, 1, 0), (WAIT, LEFT, -1, 1, 1), (SEND, SIBLING, -1, 1, 1, LEFT, -1, 1, CORE),
    (WAIT, LEFT, 2, 0, 2), (SEND, SIBLING, 2, 0, 2, LEFT, 2, 0, CORE), (SEND, LEFT, 1, 1, 2, LEFT, 0, 1, ZM),
    (WAIT, RIGHT, 2, 0, 0), (WAIT, RIGHT, -1, 1, 0), (SEND, RIGHT, 1, 1, 1, RIGHT, 0, 1, XM), (WAIT, LEFT, 1, 1, 1),
    (SEND, SIBLING, 1, 1, 1, LEFT, 1, 1, CORE), (WAIT, RIGHT, 0, 1, 2), (SEND, RIGHT, -1, 1, 2, RIGHT, 0, 1, XP),
    (SEND, LEFT, 2, 1, 2, LEFT, 2, 0, YA), (WAIT, SIBLING, -1, 1, 1), (WAIT, SIBLING, 2, 0, 2),
    (WAIT, SIBLING, 1, 1, 1), (WAIT, LEFT, -1, 1, 3), (SEND, LEFT, 2, 1, 3, LEFT, -1, 1, ZP),
    (SEND, SIBLING, -1, 1, 3, LEFT, -1, 1, CORE), (WAIT, LEFT, 1, 1, 3), (SEND, SIBLING, 1, 1, 3, LEFT, 1, 1, CORE),
    (WAIT, RIGHT, -1, 1, 1), (SEND, LEFT, 2, 1, 1, LEFT, 1, 1, ZM), (WAIT, RIGHT, 1, 1, 0),
    (SEND, RIGHT, 2, 0, 3, RIGHT, 1, 0, XM), (SEND, RIGHT, 2, 1, 1, RIGHT, -1, 1, XP), (WAIT, LEFT, -1, 1, 0),
    (SEND, LEFT, 2, 1, 0, LEFT, -1, 1, ZP), (SEND, SIBLING, -1, 1, 0, LEFT, -1, 1, CORE), (WAIT, SIBLING, -1, 1, 3),
    (SEND, RIGHT, 2, 1, 0, RIGHT, 2, 0, YY), (WAIT, SIBLING, 1, 1, 3), (WAIT, SIBLING, -1, 1, 0),
    (WAIT, LEFT, -1, 1, 2), (SEND, SIBLING, -1, 1, 2, LEFT, -1, 1, CORE), (WAIT, LEFT, 2, 0, 3),
    (SEND, SIBLING, 2, 0, 3, LEFT, 2, 0, CORE), (WAIT, RIGHT, -1, 1, 3), (WAIT, RIGHT, 1, 1, 3),
    (SEND, RIGHT, 2, 1, 3, RIGHT, -1, 1, XP), (WAIT, SIBLING, -1, 1, 2), (WAIT, RIGHT, 1, 1, 2),
    (SEND, RIGHT, 2, 1, 2, RIGHT, 1, 1, XM), (WAIT, SIBLING, 2, 0, 3), (WAIT, LEFT, 2, 1, 3),
    (SEND, SIBLING, 2, 1, 3, LEFT, 2, 1, CORE), (WAIT, LEFT, 1, 1, 2), (SEND, SIBLING, 1, 1, 2, LEFT, 1, 1, CORE),
    (WAIT, RIGHT, 1, 1, 1), (WAIT, RIGHT, -1, 1, 2), (WAIT, LEFT, 2, 1, 2),
    (SEND, SIBLING, 2, 1, 2, LEFT, 2, 1, CORE), (WAIT, SIBLING, 2, 1, 3), (WAIT, SIBLING, 1, 1, 2),
    (WAIT, SIBLING, 2, 1, 2), (WAIT, LEFT, 2, 1, 0), (SEND, SIBLING, 2, 1, 0, LEFT, 2, 1, CORE),
    (WAIT, LEFT, 2, 1, 1), (SEND, SIBLING, 2, 1, 1, LEFT, 2, 1, CORE), (WAIT, RIGHT, 2, 0, 3), (DO, EARLY),
    (WAIT, RIGHT, 2, 1, 1), (WAIT, SIBLING, 2, 1, 0), (WAIT, RIGHT, 2, 1, 0), (WAIT, SIBLING, 2, 1, 1),
    (WAIT, RIGHT, 2, 1, 3), (WAIT, RIGHT, 2, 1, 2),
)

SECOND_GATHER = (
    (OWN, 0), (SEND, SQUARE, 1, 0, 0, SQUARE, 0, 0, XM), (SEND, SQUARE, -1, 0, 1, SQUARE, 0, 0, XP),
    (SEND, SQUARE, -1, 0, 0, SQUARE, 0, 0, XP), (SEND, SQUARE, 0, 1, 1, SQUARE, 0, 0, YY),
    (SEND, SQUARE, 0, 1, 0, SQUARE, 0, 0, YY), (SEND, SQUARE, 1, 0, 1, SQUARE, 0, 0, XM), (OWN, 1),
    (WAIT, SQUARE, -1, 0, 1), (SEND, SQUARE, -1, 0, 3, SQUARE, 0, 0, XP), (SEND, SQUARE, 0, 1, 2, SQUARE, 0, 0, YY),
    (SEND, SQUARE, -1, 0, 2, SQUARE, 0, 0, XP), (SEND, SQUARE, 1, 0, 2, SQUARE, 0, 0, XM),
    (SEND, SQUARE, 1, 0, 3, SQUARE, 0, 0, XM), (WAIT, SQUARE, 1, 0, 0), (WAIT, SQUARE, 0, 1, 1),
    (SEND, SQUARE, 1, 1, 0, SQUARE, 1, 0, YY), (WAIT, SQUARE, 1, 0, 1), (WAIT, SQUARE, -1, 0, 0),
    (WAIT, SQUARE, 0, 1, 0), (SEND, SQUARE, 2, 0, 0, SQUARE, -1, 0, XP), (SEND, SQUARE, 2, 0, 1, SQUARE, 1, 0, XM),
    (SEND, SQUARE, 0, 1, 3, SQUARE, 0, 0, YY), (WAIT, SQUARE, -1, 0, 3), (WAIT, SQUARE, 1, 0, 2),
    (SEND, SQUARE, 1, 1, 1, SQUARE, 0, 1, XM), (WAIT, SQUARE, 0, 1, 2), (SEND, SQUARE, -1, 1, 0, SQUARE, 0, 1, XP),
    (SEND, SQUARE, 1, 1, 2, SQUARE, 1, 0, YY), (WAIT, SQUARE, 1, 0, 3), (SEND, SQUARE, 2, 0, 3, SQUARE, 1, 0, XM),
    (WAIT, SQUARE, -1, 0, 2), (DO, NEAR_OWN), (SEND, SQUARE, 2, 0, 2, SQUARE, -1, 0, XP),
    (SEND, SQUARE, -1, 1, 2, SQUARE, -1, 0, YY), (WAIT, SQUARE, 1, 1, 0), (WAIT, SQUARE, 2, 0, 1),
    (WAIT, SQUARE, 2, 0, 0), (WAIT, SQUARE, 0, 1, 3), (SEND, SQUARE, 2, 1, 0, SQUARE, 2, 0, YY),
    (SEND, SQUARE, 1, 1, 3, SQUARE, 0, 1, XM), (SEND, SQUARE, -1, 1, 3, SQUARE, 0, 1, XP), (WAIT, SQUARE, 1, 1, 1),
    (SEND, SQUARE, 2, 1, 1, SQUARE, 1, 1, XM), (WAIT, SQUARE, -1, 1, 0), (WAIT, SQUARE, 1, 1, 2),
    (SEND, SQUARE, -1, 1, 1, SQUARE, 0, 1, XP), (WAIT, SQUARE, 2, 0, 3), (WAIT, SQUARE, 2, 0, 2),
    (SEND, SQUARE, 2, 1, 2, SQUARE, 2, 0, YY), (DO, FAR_OWN), (WAIT, SQUARE, -1, 1, 2), (WAIT, SQUARE, 1, 1, 3),
    (SEND, SQUARE, 2, 1, 3, SQUARE, 1, 1, XM), (WAIT, SQUARE, -1, 1, 3), (WAIT, SQUARE, 2, 1, 0),
    (WAIT, SQUARE, 2, 1, 1), (WAIT, SQUARE, -1, 1, 1), (DO, NEAR_OTHER), (WAIT, SQUARE, 2, 1, 2),
    (WAIT, SQUARE, 2, 1, 3), (DO, FAR_OTHER),
)


def grow_columns(mask):
    block = lax.broadcasted_iota(jnp.int32, (PB, WP), 0)
    col = lax.broadcasted_iota(jnp.int32, (PB, WP), 1)
    spread = jnp.where((col >= block * BS) & (col < block * BS + BS), 1.0, 0.0).astype(BF16)
    return jnp.dot(mask, spread, preferred_element_type=F32).astype(BF16)


def grow(mask):
    wide = grow_columns(mask.astype(F32).astype(BF16))
    row = lax.broadcasted_iota(jnp.int32, (W, PB), 0)
    block = lax.broadcasted_iota(jnp.int32, (W, PB), 1)
    spread = jnp.where((row >= block * BS) & (row < block * BS + BS), 1.0, 0.0).astype(BF16)
    return jnp.dot(spread, wide, preferred_element_type=F32)


def whole_step(
    dens_in, pat_in, keep_in, owner_in, arrived, tails_arrived,
    dens, pat, keep, owner, left, right, sq, mask, kept, acc, update, place, hot, hot_tail, rank_at, tail_at, blocks, outgoing,
    tails, relay_in, relay_wide, relay_out, send, recv, exchange_send, exchange_recv, tail_send, tail_recv, local,
):
    r = lax.axis_index("row")
    c = lax.axis_index("col")
    x, yh = lax.rem(r, 4), lax.div(r, 4)
    z, yl, core = lax.div(c, 4), lax.rem(lax.div(c, 2), 2), lax.rem(c, 2)
    me = r * NCOL + c

    def col(dz, dyl, dcore=0):
        ycol = (1 - yl) if dyl else yl
        ccol = (1 - core) if dcore else core
        return lax.rem(z + dz + 4, 4) * 4 + ycol * 2 + ccol

    def row(dx, dyh):
        yrow = (1 - yh) if dyh else yh
        return yrow * 4 + lax.rem(x + dx + 4, 4)

    ways = {
        CORE: (r, col(0, 0, 1)),
        YA: (r, col(0, 1)),
        YB: (row(0, 1), col(0, 1)),
        YY: (row(0, 1), c),
        ZP: (r, col(1, 0)),
        ZM: (r, col(-1, 0)),
        XP: (row(1, 0), c),
        XM: (row(-1, 0), c),
    }

    fetches = [
        pltpu.make_async_copy(src, dst, local.at[k])
        for k, (src, dst) in enumerate(((pat_in, pat), (dens_in, dens), (keep_in, keep), (owner_in, owner)))
    ]
    for fetch in fetches:
        fetch.start()
    barrier = pltpu.get_barrier_semaphore()
    for dev in ways.values():
        pl.semaphore_signal(barrier, inc=1, device_id=dev, device_id_type=MESH)

    started = []
    arriving = {}

    def piece(buf, slot, q):
        h, first, end = QUARTERS[q]
        return buf.at[slot, h, pl.ds(first, end - first)]

    def find(kind, d, f, q):
        if kind == LEFT:
            return piece(left, col(d, f), q)
        if kind == SIBLING:
            return piece(left, col(d, f, 1), q)
        return piece(right if kind == RIGHT else sq, row(d, f), q)

    def start(kind, d, f, q, from_kind, from_d, from_f, way):
        k = len(started)
        if kind == RIGHT:
            src = piece(left, c, q) if (from_d, from_f) == (0, 0) else find(from_kind, from_d, from_f, q)
            dst = piece(right, r if from_kind == LEFT else row(from_d, from_f), q)
        else:
            src = dst = find(from_kind, from_d, from_f, q)
        op = pltpu.make_async_remote_copy(
            src_ref=src, dst_ref=dst, send_sem=send.at[k], recv_sem=recv.at[k],
            device_id=ways[way], device_id_type=MESH)
        op.start()
        started.append(op)
        here = find(kind, d, f, q)
        arriving[kind, d, f, q] = pltpu.make_async_remote_copy(
            src_ref=here, dst_ref=here, send_sem=send.at[k], recv_sem=recv.at[k],
            device_id=ways[way], device_id_type=MESH)

    def follow(table, own, work):
        for op, *what in table:
            if op == OWN:
                own(what[0])
            elif op == SEND:
                start(*what)
            elif op == WAIT:
                arriving[tuple(what)].wait_recv()
            else:
                work[what[0]]()

    def multiply(p, buf, h, fresh=False):
        if h is None:
            two = [left[2 * p + k].reshape(2 * W, WP) for k in range(2)]
            at = pl.ds(0, 2 * W)
        else:
            two = [left[2 * p + k, h] for k in range(2)]
            at = pl.ds(h * W, W)
        rows = buf[pl.ds(lax.rem(2 * p, NROW), 2), lax.div(p, 4)].reshape(2 * WP, WP)
        term = jnp.dot(jnp.concatenate(two, axis=1), rows, preferred_element_type=F32)
        acc[at, :] = term if fresh else acc[at, :] + term

    def is_late(p):
        zp, yp = lax.div(p, 2), lax.rem(p, 2)
        in_left = (zp == lax.rem(z + 2, 4)) & (yp == 1 - yl)
        in_right = (lax.rem(zp, 2) == 1 - yh) & (yp == lax.div(lax.rem(x + 2, 4), 2))
        return in_left | in_right

    def own_density(h):
        m = grow(pat[h]).astype(BF16)
        left[c, h, :, pl.ds(256, 128)] = jnp.zeros((W, 128), BF16)
        left[c, h, :, pl.ds(0, W)] = dens[h] * m[:, :W]
        mask[h] = m
        if h == 0:
            pl.semaphore_wait(barrier, len(ways))

    def prepare():
        for h in range(2):
            right[r, h, pl.ds(0, W)] = left[c, h]
        zero = jnp.zeros((2, WP - W, WP), BF16)

        def clear(k, carry):
            right[k, :, pl.ds(W, WP - W)] = zero
            sq[k, :, pl.ds(W, WP - W)] = zero
            return carry

        lax.fori_loop(0, NROW, clear, 0)
        acc[...] = jnp.zeros_like(acc)
        fetches[2].wait()
        fetches[3].wait()
        for h in range(2):
            kept[h] = grow(keep[h]).astype(BF16)
        routing_tables(owner, place, hot, hot_tail, rank_at, tail_at)

    def early():
        def add(p, carry):
            @pl.when(jnp.logical_not(is_late(p)))
            def _():
                multiply(p, right, None)
            return carry

        lax.fori_loop(0, NCOL // 2, add, 0)

    fetches[0].wait()
    fetches[1].wait()
    follow(FIRST_GATHER, own_density, {PREPARE: prepare, EARLY: early})

    def own_square(h):
        def add(p, carry):
            @pl.when(is_late(p))
            def _():
                multiply(p, right, h)
            return carry

        lax.fori_loop(0, NCOL // 2, add, 0)
        sq[r, h, pl.ds(0, W)] = (acc[pl.ds(h * W, W), :] / ORDER * mask[h].astype(F32)).astype(BF16)

    near = lax.div(x, 2)

    def second(yhp, pair, fresh=False):
        for h in range(2):
            multiply((2 * h + yhp) * 2 + pair, sq, None, fresh and h == 0)

    follow(SECOND_GATHER, own_square, {
        NEAR_OWN: lambda: second(yh, near, True),
        FAR_OWN: lambda: second(yh, 1 - near),
        NEAR_OTHER: lambda: second(1 - yh, near),
        FAR_OTHER: lambda: second(1 - yh, 1 - near),
    })

    for h in range(2):
        mat = left[c, h].astype(F32)
        new = kept[h].astype(F32) * (1.5 * mat - 0.5 * acc[pl.ds(h * W, W), :])
        for k in range(WP // 128):
            update[h, k] = new[:, k * 128 : k * 128 + 128]

    fill(update, rank_at, tail_at, place, hot, hot_tail, blocks, outgoing, tails)

    def partner(i, sign):
        dcore, dz = lax.rem(i, 2), lax.rem(lax.div(i, 2), 4)
        dyl, dyh, dx = lax.rem(lax.div(i, 8), 2), lax.rem(lax.div(i, 16), 2), lax.div(i, 32)
        to_row = lax.rem(yh + dyh, 2) * 4 + lax.rem(x + sign * dx + 4, 4)
        to_col = lax.rem(z + sign * dz + 4, 4) * 4 + lax.rem(yl + dyl, 2) * 2 + lax.rem(core + dcore, 2)
        return to_row, to_col

    def rows_of(buf, device):
        return buf.at[pl.ds(pl.multiple_of(device * ROWS, ROWS), ROWS)]

    def message(i):
        to_row, to_col = partner(i, 1)
        return pltpu.make_async_remote_copy(
            src_ref=rows_of(outgoing, to_row * NCOL + to_col), dst_ref=rows_of(arrived, me),
            send_sem=exchange_send.at[i], recv_sem=exchange_recv.at[i],
            device_id=(to_row, to_col), device_id_type=MESH)

    def arrival(i):
        from_row, from_col = partner(i, -1)
        here = rows_of(arrived, from_row * NCOL + from_col)
        return pltpu.make_async_remote_copy(
            src_ref=here, dst_ref=here, send_sem=exchange_send.at[i], recv_sem=exchange_recv.at[i],
            device_id=(from_row, from_col), device_id_type=MESH)

    def start_message(i, carry):
        message(lax.rem(i * 37, DEVICES)).start()
        return carry

    def finish_message(i, carry):
        arrival(lax.rem(i * 37, DEVICES)).wait_recv()
        return carry

    def message_sent(i, carry):
        message(i).wait_send()
        return carry

    line, in_line = r * 2 + yl, z * 2 + core

    def other_line(i):
        dyl, dyh, dx = i % 2, i // 2 % 2, i // 4
        return row(dx, dyh), yl if dyl == 0 else 1 - yl

    def line_copy(i, to_line, here_line, device):
        return pltpu.make_async_remote_copy(
            src_ref=rows_of(tails, to_line), dst_ref=rows_of(relay_in, here_line),
            send_sem=tail_send.at[i], recv_sem=tail_recv.at[i], device_id=device, device_id_type=MESH)

    def pass_on(i, to, here, device):
        return pltpu.make_async_remote_copy(
            src_ref=rows_of(relay_out, to), dst_ref=rows_of(tails_arrived, here),
            send_sem=tail_send.at[i], recv_sem=tail_recv.at[i], device_id=device, device_id_type=MESH)

    tail_ops = []
    tail_waits = []
    for i in range(1, 2 * NROW):
        to_row, to_yl = other_line(i)
        device = (to_row, z * 4 + to_yl * 2 + core)
        op = line_copy(i, to_row * 2 + to_yl, line, device)
        op.start()
        tail_ops.append(op)
        from_row = row(-(i // 4), i // 2 % 2)
        tail_waits.append(line_copy(i, line, from_row * 2 + to_yl, device))
    keep_line = pltpu.make_async_copy(rows_of(tails, line), rows_of(relay_in, line), local.at[5])
    keep_line.start()
    own = pltpu.make_async_copy(rows_of(outgoing, me), rows_of(arrived, me), local.at[4])
    own.start()
    lax.fori_loop(1, DEVICES // 2, start_message, 0)
    keep_line.wait()
    for op in tail_waits:
        op.wait_recv()
    relay_wide[...] = relay_in[...].astype(F32)
    for j in range(2 * 4):
        for k in range(2):
            part = relay_wide[pl.ds(2 * j + k, 2 * NROW, stride=ROWS), :]
            relay_out[pl.ds(j * ROWS, ROWS), pl.ds(128 * k, 128)] = part.astype(BF16)
    pass_waits = []
    for i in range(1, 2 * 4):
        to_core = core if i % 2 == 0 else 1 - core
        to_z, from_z = lax.rem(z + i // 2, 4), lax.rem(z + 4 - i // 2, 4)
        device = (r, to_z * 4 + yl * 2 + to_core)
        op = pass_on(2 * NROW + i, to_z * 2 + to_core, in_line, device)
        op.start()
        tail_ops.append(op)
        pass_waits.append(pass_on(2 * NROW + i, in_line, from_z * 2 + to_core, device))
    keep_tails = pltpu.make_async_copy(rows_of(relay_out, in_line), rows_of(tails_arrived, in_line), local.at[6])
    keep_tails.start()
    lax.fori_loop(DEVICES // 2, DEVICES, start_message, 0)
    for op in started:
        op.wait_send()
    own.wait()
    keep_tails.wait()
    lax.fori_loop(1, DEVICES, finish_message, 0)
    for op in pass_waits:
        op.wait_recv()
    lax.fori_loop(1, DEVICES, message_sent, 0)
    for op in tail_ops:
        op.wait_send()


N_BLOCKS = 2 * PB * PB
WINDOWS = [
    (w, i) for w in range(3) for i in range(BS) if i * BS + BS > w * 256 and i * BS < w * 256 + 256
]


def ranks(owner_row):
    owner = jnp.broadcast_to(owner_row.astype(F32), (8, N_BLOCKS))
    same = owner.T[:, :1] == owner[:1]
    one = lax.broadcasted_iota(jnp.int32, (N_BLOCKS, N_BLOCKS), 0)
    two = lax.broadcasted_iota(jnp.int32, (N_BLOCKS, N_BLOCKS), 1)
    rank = jnp.sum(jnp.where(same & (one < two), 1.0, 0.0), axis=0, keepdims=True).astype(jnp.int32)
    rank_col = jnp.sum(jnp.where(same & (two < one), 1.0, 0.0), axis=1, keepdims=True).astype(jnp.int32)
    return rank, rank_col


def routing_tables(owner, place, hot, hot_tail, rank_at, tail_at):
    lane = lax.broadcasted_iota(jnp.int32, (WP, 256), 0)
    at = lax.broadcasted_iota(jnp.int32, (WP, 256), 1)
    entry = lane - lax.div(lane, BS) * BS
    slot = lax.div(at, TAIL)
    for k, (w, i) in enumerate(WINDOWS):
        if w < 2:
            place[k] = jnp.where(at - entry == i * BS - w * 256, 1.0, 0.0).astype(BF16)
        else:
            offset = at - slot * TAIL
            fits = (slot < 6) & (offset - entry == i * BS - w * 256) & (offset < ENT - 512)
            place[k] = jnp.where(fits, 1.0, 0.0).astype(BF16)
    rank, rank_col = ranks(owner[...])
    rank_at[...] = jnp.broadcast_to(rank_col, rank_at.shape)
    group = lax.div(lax.broadcasted_iota(jnp.int32, tail_at.shape, 1), TAIL)
    tail_at[...] = jnp.where(rank_col - lax.div(rank_col, 6) * 6 == group, 1.0, 0.0)
    own = owner[...]
    key = own * ROWS + rank
    last_key = own * ROWS + CAP + rank - lax.div(rank, 4) * 4
    to_row, to_col = lax.div(own, NCOL), lax.rem(own, NCOL)
    line = to_row * 2 + lax.rem(lax.div(to_col, 2), 2)
    in_line = lax.div(to_col, 4) * 2 + lax.rem(to_col, 2)
    tail_key = line * ROWS + in_line * 2 + lax.div(rank, 6)
    step = 512
    for k in range(0, DEVICES * ROWS, step):
        at = lax.broadcasted_iota(jnp.int32, (step, N_BLOCKS), 0) + k
        hot[pl.ds(k, step), pl.ds(0, N_BLOCKS)] = jnp.where(at == key, 1.0, 0.0).astype(BF16)
        hot[pl.ds(k, step), pl.ds(N_BLOCKS, N_BLOCKS)] = jnp.where(at == last_key, 1.0, 0.0).astype(BF16)
    at = lax.broadcasted_iota(jnp.int32, hot_tail.shape, 0)
    hot_tail[...] = jnp.where(at == tail_key, 1.0, 0.0).astype(BF16)


def fill(update, rank_at, tail_at, place, hot, hot_tail, blocks, outgoing, tails):
    n = N_BLOCKS
    half = PB // 2
    picks = []
    for g in range(2):
        bc = lax.broadcasted_iota(jnp.int32, (half, 256), 0) + g * half
        entry = lax.broadcasted_iota(jnp.int32, (half, 256), 1) + g * 128
        picks.append(jnp.where((entry >= bc * BS) & (entry < bc * BS + BS), 1.0, 0.0)[None])
    for w in (2, 0, 1):
        total = [None, None]
        for k, (wk, i) in enumerate(WINDOWS):
            if wk != w:
                continue
            u = [[update[h, j, pl.ds(i, PB, stride=BS), :] for j in range(WP // 128)] for h in range(2)]
            for g in range(2):
                rows = [
                    (jnp.concatenate(u[h][g : g + 2], axis=1)[:, None, :] * picks[g]).astype(BF16)
                    .reshape(PB * half, 256)
                    for h in range(2)
                ]
                term = jnp.dot(jnp.concatenate(rows, axis=0), place[k, pl.ds(128 * g, 256), :],
                               preferred_element_type=F32)
                total[g] = term if total[g] is None else total[g] + term
        both = [t.reshape(2 * PB, 1, half, 256) for t in total]
        both = jnp.concatenate(both, axis=1).reshape(n, 256)
        if w == 2:
            tail = (both[:, :128] * tail_at[...]).astype(BF16)
            tails[...] = jnp.dot(hot_tail[...], tail, preferred_element_type=F32).astype(BF16)
        elif w == 0:
            blocks[pl.ds(0, n), pl.ds(0, 256)] = both.astype(BF16)
        else:
            blocks[pl.ds(0, n), pl.ds(256, 128)] = both[:, :128].astype(BF16)
            rank = rank_at[...]
            for j in range(3):
                mine = (rank >= 4 * j) & (rank < 4 * j + 4)
                blocks[pl.ds(n, n), pl.ds(128 * j, 128)] = jnp.where(mine, both[:, 128:], 0.0).astype(BF16)
    step = 512
    for k in range(0, DEVICES * ROWS, step):
        outgoing[pl.ds(k, step), :] = jnp.dot(
            hot[pl.ds(k, step), :], blocks[...], preferred_element_type=F32).astype(BF16)


N_COPIES = sum(op[0] == SEND for op in FIRST_GATHER + SECOND_GATHER)


def stepped(density, pattern, keep, owner):
    anywhere = pl.BlockSpec(memory_space=pl.ANY)
    owner = owner.reshape(1, N_BLOCKS)
    return pl.pallas_call(
        whole_step,
        out_shape=(
            jax.ShapeDtypeStruct((DEVICES * ROWS, LANES), BF16),
            jax.ShapeDtypeStruct((DEVICES, 256), BF16),
        ),
        in_specs=[anywhere] * 4,
        out_specs=(anywhere, anywhere),
        scratch_shapes=[
            pltpu.VMEM(density.shape, BF16),
            pltpu.VMEM(pattern.shape, jnp.int32),
            pltpu.VMEM(keep.shape, jnp.int32),
            pltpu.VMEM(owner.shape, jnp.int32),
            pltpu.VMEM((NCOL, 2, W, WP), BF16),
            pltpu.VMEM((NROW, 2, WP, WP), BF16),
            pltpu.VMEM((NROW, 2, WP, WP), BF16),
            pltpu.VMEM((2, W, WP), BF16),
            pltpu.VMEM((2, W, WP), BF16),
            pltpu.VMEM((2 * W, WP), F32),
            pltpu.VMEM((2, WP // 128, W, 128), F32),
            pltpu.VMEM((len(WINDOWS), WP, 256), BF16),
            pltpu.VMEM((DEVICES * ROWS, 2 * N_BLOCKS), BF16),
            pltpu.VMEM((2 * NROW * ROWS, N_BLOCKS), BF16),
            pltpu.VMEM((N_BLOCKS, 128), jnp.int32),
            pltpu.VMEM((N_BLOCKS, 128), F32),
            pltpu.VMEM((2 * N_BLOCKS, LANES), BF16),
            pltpu.VMEM((DEVICES * ROWS, LANES), BF16),
            pltpu.VMEM((2 * NROW * ROWS, 128), BF16),
            pltpu.VMEM((2 * NROW * ROWS, 128), BF16),
            pltpu.VMEM((2 * NROW * ROWS, 128), F32),
            pltpu.VMEM((DEVICES, 256), BF16),
            pltpu.SemaphoreType.DMA((N_COPIES,)),
            pltpu.SemaphoreType.DMA((N_COPIES,)),
            pltpu.SemaphoreType.DMA((DEVICES,)),
            pltpu.SemaphoreType.DMA((DEVICES,)),
            pltpu.SemaphoreType.DMA((2 * NROW + 8,)),
            pltpu.SemaphoreType.DMA((2 * NROW + 8,)),
            pltpu.SemaphoreType.DMA((7,)),
        ],
        compiler_params=pltpu.CompilerParams(
            collective_id=0, has_side_effects=True, vmem_limit_bytes=56 * 1024 * 1024),
        name="whole_step",
    )(density, pattern, keep, owner)


def unpack(messages, tails, out, arrived, tails_in, wide, tails_wide, by_source, ready, sem):
    chunks = [pl.ds(128 * k, 128) for k in range(LANES // 128)]
    fetches = [
        pltpu.make_async_copy(messages.at[:, at], arrived.at[:, at], sem.at[CAP + k])
        for k, at in enumerate(chunks)
    ]
    fetch_tails = pltpu.make_async_copy(tails, tails_in, sem.at[CAP + len(chunks)])
    fetch_tails.start()
    for fetch in fetches:
        fetch.start()

    fetch_tails.wait()
    for k in range(2):
        tails_wide[k] = tails_in[:, pl.ds(128 * k, 128)].astype(F32)
        for j in range(8):
            for yl in range(2):
                source = j // 2 * 4 + yl * 2 + j % 2
                by_source[k, pl.ds(source, NROW, stride=NCOL), :] = tails_wide[k, pl.ds(j * ROWS + yl, NROW, stride=2), :]
        rows = by_source[k].T.astype(BF16)
        for s in range(6):
            ready[6 * k + s, pl.ds(512, ENT - 512), :] = rows[s * TAIL : s * TAIL + ENT - 512]
    copies = []
    for k, at in enumerate(chunks):
        fetches[k].wait()
        wide[k] = arrived[:, at].astype(F32)
        for s in range(4):
            fourth = wide[k, pl.ds(CAP + s, DEVICES, stride=ROWS), :]
            ready[4 * k + s, pl.ds(384, 128), :] = fourth.T.astype(BF16)
        for s in range(CAP):
            ready[s, at, :] = wide[k, pl.ds(s, DEVICES, stride=ROWS), :].T.astype(BF16)
            if k == len(chunks) - 1:
                copies.append(pltpu.make_async_copy(ready.at[s], out.at[s], sem.at[s]))
                copies[-1].start()
    for copy in copies:
        copy.wait()


def unpacked(messages, tails):
    anywhere = pl.BlockSpec(memory_space=pl.ANY)
    out = pl.pallas_call(
        unpack,
        out_shape=jax.ShapeDtypeStruct((CAP, ENT, DEVICES), BF16),
        in_specs=[anywhere] * 2,
        out_specs=anywhere,
        scratch_shapes=[
            pltpu.VMEM((DEVICES * ROWS, LANES), BF16),
            pltpu.VMEM((DEVICES, 256), BF16),
            pltpu.VMEM((LANES // 128, DEVICES * ROWS, 128), F32),
            pltpu.VMEM((2, DEVICES, 128), F32),
            pltpu.VMEM((2, DEVICES, 128), F32),
            pltpu.VMEM((CAP, ENT, DEVICES), BF16),
            pltpu.SemaphoreType.DMA((CAP + 4,)),
        ],
        compiler_params=pltpu.CompilerParams(vmem_limit_bytes=58 * 1024 * 1024),
        name="unpack",
    )(messages, tails)
    return out.transpose(2, 0, 1)[None]


def per_device(density, pattern, keep, owner):
    return unpacked(*stepped(density, pattern, keep, owner))


def solution(mesh):
    placed = (
        P(None, "row", "col"),
        P(None, "row", "col"),
        P(None, "row", "col"),
        P(("row", "col"), None, None),
    )
    return jax.shard_map(
        per_device,
        mesh=mesh,
        in_specs=placed,
        out_specs=P(("row", "col"), None, None, None),
        check_vma=False,
    )
```

```python
import jax
import jax.numpy as jnp
from jax import lax
from jax.experimental import pallas as pl
from jax.experimental.pallas import tpu as pltpu
from jax.sharding import PartitionSpec as P

BS = 23
PB = 16
W = BS * PB
WP = 384
ORDER = 5888
NROW = 8
NCOL = 16
DEVICES = NROW * NCOL
CAP = 12
ENT = BS * BS
ROWS = 16
LANES = 384
TAIL = 21
MESH = pl.DeviceIdType.MESH
F32 = jnp.float32
BF16 = jnp.bfloat16


QUARTERS = ((0, 0, 192), (0, 192, W), (1, 0, 192), (1, 192, W))

OWN, SEND, WAIT, DO = range(4)
LEFT, SIBLING, RIGHT, SQUARE = range(4)
CORE, YA, YB, YY, ZP, ZM, XP, XM = range(8)
PREPARE, EARLY, NEAR_OWN, FAR_OWN, NEAR_OTHER, FAR_OTHER = range(6)
FIRST_GATHER = (
    (OWN, 0), (SEND, LEFT, 1, 0, 0, LEFT, 0, 0, ZM), (SEND, LEFT, -1, 0, 0, LEFT, 0, 0, ZP),
    (SEND, RIGHT, -1, 0, 0, RIGHT, 0, 0, XP), (SEND, LEFT, -1, 0, 1, LEFT, 0, 0, ZP),
    (SEND, RIGHT, 1, 0, 1, RIGHT, 0, 0, XM), (SEND, LEFT, 0, 1, 0, LEFT, 0, 0, YA),
    (SEND, LEFT, 1, 0, 1, LEFT, 0, 0, ZM), (SEND, RIGHT, 1, 0, 0, RIGHT, 0, 0, XM),
    (SEND, RIGHT, -1, 0, 1, RIGHT, 0, 0, XP), (SEND, LEFT, 0, 1, 1, LEFT, 0, 0, YA),
    (SEND, SIBLING, 0, 0, 0, LEFT, 0, 0, CORE), (SEND, SIBLING, 0, 0, 1, LEFT, 0, 0, CORE), (OWN, 1),
    (SEND, SIBLING, 0, 0, 2, LEFT, 0, 0, CORE), (SEND, SIBLING, 0, 0, 3, LEFT, 0, 0, CORE), (DO, PREPARE),
    (SEND, RIGHT, -1, 0, 2, RIGHT, 0, 0, XP), (SEND, LEFT, 1, 0, 2, LEFT, 0, 0, ZM),
    (SEND, RIGHT, 1, 0, 2, RIGHT, 0, 0, XM), (SEND, LEFT, 0, 1, 3, LEFT, 0, 0, YA),
    (SEND, LEFT, -1, 0, 2, LEFT, 0, 0, ZP), (WAIT, SIBLING, 0, 0, 0), (WAIT, SIBLING, 0, 0, 1),
    (WAIT, SIBLING, 0, 0, 2), (WAIT, SIBLING, 0, 0, 3), (WAIT, LEFT, 1, 0, 0),
    (SEND, SIBLING, 1, 0, 0, LEFT, 1, 0, CORE), (WAIT, LEFT, -1, 0, 0), (SEND, SIBLING, -1, 0, 0, LEFT, -1, 0, CORE),
    (SEND, LEFT, 2, 0, 0, LEFT, 1, 0, ZM), (WAIT, RIGHT, 1, 0, 1), (SEND, LEFT, 0, 1, 2, LEFT, 0, 0, YA),
    (SEND, RIGHT, -1, 0, 3, RIGHT, 0, 0, XP), (SEND, RIGHT, 1, 0, 3, RIGHT, 0, 0, XM),
    (SEND, LEFT, -1, 0, 3, LEFT, 0, 0, ZP), (WAIT, RIGHT, -1, 0, 0), (WAIT, LEFT, 0, 1, 0),
    (SEND, RIGHT, 0, 1, 0, LEFT, 0, 1, YB), (SEND, SIBLING, 0, 1, 0, LEFT, 0, 1, CORE), (WAIT, SIBLING, 1, 0, 0),
    (WAIT, SIBLING, -1, 0, 0), (WAIT, LEFT, 1, 0, 1), (SEND, SIBLING, 1, 0, 1, LEFT, 1, 0, CORE),
    (WAIT, SIBLING, 0, 1, 0), (WAIT, LEFT, -1, 0, 1), (SEND, SIBLING, -1, 0, 1, LEFT, -1, 0, CORE),
    (WAIT, RIGHT, -1, 0, 1), (SEND, LEFT, 2, 0, 1, LEFT, -1, 0, ZP), (SEND, LEFT, 1, 0, 3, LEFT, 0, 0, ZM),
    (SEND, RIGHT, 2, 0, 1, RIGHT, 1, 0, XM), (WAIT, RIGHT, 1, 0, 0), (SEND, LEFT, 1, 1, 0, LEFT, 1, 0, YA),
    (WAIT, LEFT, 0, 1, 1), (SEND, RIGHT, 0, 1, 1, LEFT, 0, 1, YB), (SEND, SIBLING, 0, 1, 1, LEFT, 0, 1, CORE),
    (WAIT, SIBLING, 1, 0, 1), (WAIT, SIBLING, -1, 0, 1), (WAIT, SIBLING, 0, 1, 1), (WAIT, LEFT, 1, 0, 2),
    (SEND, SIBLING, 1, 0, 2, LEFT, 1, 0, CORE), (SEND, LEFT, -1, 1, 1, LEFT, 0, 1, ZP),
    (SEND, LEFT, 2, 0, 2, LEFT, 1, 0, ZM), (WAIT, LEFT, -1, 0, 2), (SEND, RIGHT, 2, 0, 0, RIGHT, 1, 0, XM),
    (SEND, SIBLING, -1, 0, 2, LEFT, -1, 0, CORE), (WAIT, RIGHT, -1, 0, 2), (SEND, RIGHT, 2, 0, 2, RIGHT, -1, 0, XP),
    (WAIT, LEFT, 0, 1, 3), (SEND, SIBLING, 0, 1, 3, LEFT, 0, 1, CORE), (SEND, LEFT, 1, 1, 1, LEFT, 1, 0, YA),
    (SEND, RIGHT, 0, 1, 3, LEFT, 0, 1, YB), (WAIT, RIGHT, 1, 0, 2), (WAIT, RIGHT, 0, 1, 0),
    (SEND, RIGHT, -1, 1, 0, RIGHT, 0, 1, XP), (WAIT, SIBLING, 1, 0, 2), (WAIT, SIBLING, -1, 0, 2),
    (WAIT, SIBLING, 0, 1, 3), (WAIT, LEFT, -1, 0, 3), (SEND, LEFT, -1, 1, 3, LEFT, 0, 1, ZP),
    (SEND, SIBLING, -1, 0, 3, LEFT, -1, 0, CORE), (WAIT, RIGHT, -1, 0, 3), (WAIT, LEFT, 2, 0, 0),
    (SEND, LEFT, 1, 1, 3, LEFT, 0, 1, ZM), (SEND, SIBLING, 2, 0, 0, LEFT, 2, 0, CORE), (WAIT, RIGHT, 1, 0, 3),
    (SEND, RIGHT, 1, 1, 0, RIGHT, 0, 1, XM), (SEND, LEFT, -1, 1, 0, LEFT, -1, 0, YA), (WAIT, RIGHT, 0, 1, 1),
    (SEND, RIGHT, -1, 1, 1, RIGHT, 0, 1, XP), (WAIT, LEFT, 0, 1, 2), (SEND, RIGHT, 0, 1, 2, LEFT, 0, 1, YB),
    (SEND, SIBLING, 0, 1, 2, LEFT, 0, 1, CORE), (WAIT, SIBLING, -1, 0, 3), (WAIT, SIBLING, 2, 0, 0),
    (WAIT, LEFT, 2, 0, 1), (SEND, SIBLING, 2, 0, 1, LEFT, 2, 0, CORE), (SEND, LEFT, -1, 1, 2, LEFT, 0, 1, ZP),
    (WAIT, SIBLING, 0, 1, 2), (WAIT, LEFT, 1, 0, 3), (SEND, LEFT, 2, 0, 3, LEFT, 1, 0, ZM),
    (SEND, SIBLING, 1, 0, 3, LEFT, 1, 0, CORE), (WAIT, RIGHT, 2, 0, 1), (WAIT, RIGHT, 0, 1, 3),
    (SEND, RIGHT, -1, 1, 3, RIGHT, 0, 1, XP), (SEND, RIGHT, 1, 1, 3, RIGHT, 0, 1, XM),
    (SEND, RIGHT, 1, 1, 2, RIGHT, 1, 0, YY), (WAIT, RIGHT, 2, 0, 2), (WAIT, LEFT, 1, 1, 0),
    (SEND, SIBLING, 1, 1, 0, LEFT, 1, 1, CORE), (WAIT, SIBLING, 2, 0, 1), (WAIT, SIBLING, 1, 0, 3),
    (WAIT, SIBLING, 1, 1, 0), (WAIT, LEFT, -1, 1, 1), (SEND, SIBLING, -1, 1, 1, LEFT, -1, 1, CORE),
    (WAIT, LEFT, 2, 0, 2), (SEND, SIBLING, 2, 0, 2, LEFT, 2, 0, CORE), (SEND, LEFT, 1, 1, 2, LEFT, 0, 1, ZM),
    (WAIT, RIGHT, 2, 0, 0), (WAIT, RIGHT, -1, 1, 0), (SEND, RIGHT, 1, 1, 1, RIGHT, 0, 1, XM), (WAIT, LEFT, 1, 1, 1),
    (SEND, SIBLING, 1, 1, 1, LEFT, 1, 1, CORE), (WAIT, RIGHT, 0, 1, 2), (SEND, RIGHT, -1, 1, 2, RIGHT, 0, 1, XP),
    (SEND, LEFT, 2, 1, 2, LEFT, 2, 0, YA), (WAIT, SIBLING, -1, 1, 1), (WAIT, SIBLING, 2, 0, 2),
    (WAIT, SIBLING, 1, 1, 1), (WAIT, LEFT, -1, 1, 3), (SEND, LEFT, 2, 1, 3, LEFT, -1, 1, ZP),
    (SEND, SIBLING, -1, 1, 3, LEFT, -1, 1, CORE), (WAIT, LEFT, 1, 1, 3), (SEND, SIBLING, 1, 1, 3, LEFT, 1, 1, CORE),
    (WAIT, RIGHT, -1, 1, 1), (SEND, LEFT, 2, 1, 1, LEFT, 1, 1, ZM), (WAIT, RIGHT, 1, 1, 0),
    (SEND, RIGHT, 2, 0, 3, RIGHT, 1, 0, XM), (SEND, RIGHT, 2, 1, 1, RIGHT, -1, 1, XP), (WAIT, LEFT, -1, 1, 0),
    (SEND, LEFT, 2, 1, 0, LEFT, -1, 1, ZP), (SEND, SIBLING, -1, 1, 0, LEFT, -1, 1, CORE), (WAIT, SIBLING, -1, 1, 3),
    (SEND, RIGHT, 2, 1, 0, RIGHT, 2, 0, YY), (WAIT, SIBLING, 1, 1, 3), (WAIT, SIBLING, -1, 1, 0),
    (WAIT, LEFT, -1, 1, 2), (SEND, SIBLING, -1, 1, 2, LEFT, -1, 1, CORE), (WAIT, LEFT, 2, 0, 3),
    (SEND, SIBLING, 2, 0, 3, LEFT, 2, 0, CORE), (WAIT, RIGHT, -1, 1, 3), (WAIT, RIGHT, 1, 1, 3),
    (SEND, RIGHT, 2, 1, 3, RIGHT, -1, 1, XP), (WAIT, SIBLING, -1, 1, 2), (WAIT, RIGHT, 1, 1, 2),
    (SEND, RIGHT, 2, 1, 2, RIGHT, 1, 1, XM), (WAIT, SIBLING, 2, 0, 3), (WAIT, LEFT, 2, 1, 3),
    (SEND, SIBLING, 2, 1, 3, LEFT, 2, 1, CORE), (WAIT, LEFT, 1, 1, 2), (SEND, SIBLING, 1, 1, 2, LEFT, 1, 1, CORE),
    (WAIT, RIGHT, 1, 1, 1), (WAIT, RIGHT, -1, 1, 2), (WAIT, LEFT, 2, 1, 2),
    (SEND, SIBLING, 2, 1, 2, LEFT, 2, 1, CORE), (WAIT, SIBLING, 2, 1, 3), (WAIT, SIBLING, 1, 1, 2),
    (WAIT, SIBLING, 2, 1, 2), (WAIT, LEFT, 2, 1, 0), (SEND, SIBLING, 2, 1, 0, LEFT, 2, 1, CORE),
    (WAIT, LEFT, 2, 1, 1), (SEND, SIBLING, 2, 1, 1, LEFT, 2, 1, CORE), (WAIT, RIGHT, 2, 0, 3), (DO, EARLY),
    (WAIT, RIGHT, 2, 1, 1), (WAIT, SIBLING, 2, 1, 0), (WAIT, RIGHT, 2, 1, 0), (WAIT, SIBLING, 2, 1, 1),
    (WAIT, RIGHT, 2, 1, 3), (WAIT, RIGHT, 2, 1, 2),
)

SECOND_GATHER = (
    (OWN, 0), (SEND, SQUARE, 1, 0, 0, SQUARE, 0, 0, XM), (SEND, SQUARE, -1, 0, 1, SQUARE, 0, 0, XP),
    (SEND, SQUARE, -1, 0, 0, SQUARE, 0, 0, XP), (SEND, SQUARE, 0, 1, 1, SQUARE, 0, 0, YY),
    (SEND, SQUARE, 0, 1, 0, SQUARE, 0, 0, YY), (SEND, SQUARE, 1, 0, 1, SQUARE, 0, 0, XM), (OWN, 1),
    (WAIT, SQUARE, -1, 0, 1), (SEND, SQUARE, -1, 0, 3, SQUARE, 0, 0, XP), (SEND, SQUARE, 0, 1, 2, SQUARE, 0, 0, YY),
    (SEND, SQUARE, -1, 0, 2, SQUARE, 0, 0, XP), (SEND, SQUARE, 1, 0, 2, SQUARE, 0, 0, XM),
    (SEND, SQUARE, 1, 0, 3, SQUARE, 0, 0, XM), (WAIT, SQUARE, 1, 0, 0), (WAIT, SQUARE, 0, 1, 1),
    (SEND, SQUARE, 1, 1, 0, SQUARE, 1, 0, YY), (WAIT, SQUARE, 1, 0, 1), (WAIT, SQUARE, -1, 0, 0),
    (WAIT, SQUARE, 0, 1, 0), (SEND, SQUARE, 2, 0, 0, SQUARE, -1, 0, XP), (SEND, SQUARE, 2, 0, 1, SQUARE, 1, 0, XM),
    (SEND, SQUARE, 0, 1, 3, SQUARE, 0, 0, YY), (WAIT, SQUARE, -1, 0, 3), (WAIT, SQUARE, 1, 0, 2),
    (SEND, SQUARE, 1, 1, 1, SQUARE, 0, 1, XM), (WAIT, SQUARE, 0, 1, 2), (SEND, SQUARE, -1, 1, 0, SQUARE, 0, 1, XP),
    (SEND, SQUARE, 1, 1, 2, SQUARE, 1, 0, YY), (WAIT, SQUARE, 1, 0, 3), (SEND, SQUARE, 2, 0, 3, SQUARE, 1, 0, XM),
    (WAIT, SQUARE, -1, 0, 2), (DO, NEAR_OWN), (SEND, SQUARE, 2, 0, 2, SQUARE, -1, 0, XP),
    (SEND, SQUARE, -1, 1, 2, SQUARE, -1, 0, YY), (WAIT, SQUARE, 1, 1, 0), (WAIT, SQUARE, 2, 0, 1),
    (WAIT, SQUARE, 2, 0, 0), (WAIT, SQUARE, 0, 1, 3), (SEND, SQUARE, 2, 1, 0, SQUARE, 2, 0, YY),
    (SEND, SQUARE, 1, 1, 3, SQUARE, 0, 1, XM), (SEND, SQUARE, -1, 1, 3, SQUARE, 0, 1, XP), (WAIT, SQUARE, 1, 1, 1),
    (SEND, SQUARE, 2, 1, 1, SQUARE, 1, 1, XM), (WAIT, SQUARE, -1, 1, 0), (WAIT, SQUARE, 1, 1, 2),
    (SEND, SQUARE, -1, 1, 1, SQUARE, 0, 1, XP), (WAIT, SQUARE, 2, 0, 3), (WAIT, SQUARE, 2, 0, 2),
    (SEND, SQUARE, 2, 1, 2, SQUARE, 2, 0, YY), (DO, FAR_OWN), (WAIT, SQUARE, -1, 1, 2), (WAIT, SQUARE, 1, 1, 3),
    (SEND, SQUARE, 2, 1, 3, SQUARE, 1, 1, XM), (WAIT, SQUARE, -1, 1, 3), (WAIT, SQUARE, 2, 1, 0),
    (WAIT, SQUARE, 2, 1, 1), (WAIT, SQUARE, -1, 1, 1), (DO, NEAR_OTHER), (WAIT, SQUARE, 2, 1, 2),
    (WAIT, SQUARE, 2, 1, 3), (DO, FAR_OTHER),
)


def grow_columns(mask):
    block = lax.broadcasted_iota(jnp.int32, (PB, WP), 0)
    col = lax.broadcasted_iota(jnp.int32, (PB, WP), 1)
    spread = jnp.where((col >= block * BS) & (col < block * BS + BS), 1.0, 0.0).astype(BF16)
    return jnp.dot(mask, spread, preferred_element_type=F32).astype(BF16)


def grow(mask):
    wide = grow_columns(mask.astype(F32).astype(BF16))
    row = lax.broadcasted_iota(jnp.int32, (W, PB), 0)
    block = lax.broadcasted_iota(jnp.int32, (W, PB), 1)
    spread = jnp.where((row >= block * BS) & (row < block * BS + BS), 1.0, 0.0).astype(BF16)
    return jnp.dot(spread, wide, preferred_element_type=F32)


def whole_step(
    dens_in, pat_in, keep_in, owner_in, arrived, tails_arrived,
    dens, pat, keep, owner, left, right, sq, mask, kept, acc, update, place, hot, hot_tail, rank_at, tail_at, blocks, outgoing,
    tails, relay_in, relay_wide, relay_out, send, recv, exchange_send, exchange_recv, tail_send, tail_recv, local,
):
    r = lax.axis_index("row")
    c = lax.axis_index("col")
    x, yh = lax.rem(r, 4), lax.div(r, 4)
    z, yl, core = lax.div(c, 4), lax.rem(lax.div(c, 2), 2), lax.rem(c, 2)
    me = r * NCOL + c

    def col(dz, dyl, dcore=0):
        ycol = (1 - yl) if dyl else yl
        ccol = (1 - core) if dcore else core
        return lax.rem(z + dz + 4, 4) * 4 + ycol * 2 + ccol

    def row(dx, dyh):
        yrow = (1 - yh) if dyh else yh
        return yrow * 4 + lax.rem(x + dx + 4, 4)

    ways = {
        CORE: (r, col(0, 0, 1)),
        YA: (r, col(0, 1)),
        YB: (row(0, 1), col(0, 1)),
        YY: (row(0, 1), c),
        ZP: (r, col(1, 0)),
        ZM: (r, col(-1, 0)),
        XP: (row(1, 0), c),
        XM: (row(-1, 0), c),
    }

    fetches = [
        pltpu.make_async_copy(src, dst, local.at[k])
        for k, (src, dst) in enumerate(((pat_in, pat), (dens_in, dens), (keep_in, keep), (owner_in, owner)))
    ]
    for fetch in fetches:
        fetch.start()
    barrier = pltpu.get_barrier_semaphore()
    for dev in ways.values():
        pl.semaphore_signal(barrier, inc=1, device_id=dev, device_id_type=MESH)

    started = []
    arriving = {}

    def piece(buf, slot, q):
        h, first, end = QUARTERS[q]
        return buf.at[slot, h, pl.ds(first, end - first)]

    def find(kind, d, f, q):
        if kind == LEFT:
            return piece(left, col(d, f), q)
        if kind == SIBLING:
            return piece(left, col(d, f, 1), q)
        return piece(right if kind == RIGHT else sq, row(d, f), q)

    def start(kind, d, f, q, from_kind, from_d, from_f, way):
        k = len(started)
        group = 0 if kind in (LEFT, SIBLING) else 1
        if kind == RIGHT:
            src = piece(left, c, q) if (from_d, from_f) == (0, 0) else find(from_kind, from_d, from_f, q)
            dst = piece(right, r if from_kind == LEFT else row(from_d, from_f), q)
        else:
            src = dst = find(from_kind, from_d, from_f, q)
        op = pltpu.make_async_remote_copy(
            src_ref=src, dst_ref=dst, send_sem=send.at[group], recv_sem=recv.at[k],
            device_id=ways[way], device_id_type=MESH)
        op.start()
        started.append(kind)
        here = find(kind, d, f, q)
        arriving[kind, d, f, q] = pltpu.make_async_remote_copy(
            src_ref=here, dst_ref=here, send_sem=send.at[group], recv_sem=recv.at[k],
            device_id=ways[way], device_id_type=MESH)

    def follow(table, own, work):
        for op, *what in table:
            if op == OWN:
                own(what[0])
            elif op == SEND:
                start(*what)
            elif op == WAIT:
                arriving[tuple(what)].wait_recv()
            else:
                work[what[0]]()

    def multiply(p, buf, h):
        if h is None:
            two = [left[2 * p + k].reshape(2 * W, WP) for k in range(2)]
            at = pl.ds(0, 2 * W)
        else:
            two = [left[2 * p + k, h] for k in range(2)]
            at = pl.ds(h * W, W)
        rows = buf[pl.ds(lax.rem(2 * p, NROW), 2), lax.div(p, 4)].reshape(2 * WP, WP)
        acc[at, :] += jnp.dot(jnp.concatenate(two, axis=1), rows, preferred_element_type=F32)

    def is_late(p):
        zp, yp = lax.div(p, 2), lax.rem(p, 2)
        in_left = (zp == lax.rem(z + 2, 4)) & (yp == 1 - yl)
        in_right = (lax.rem(zp, 2) == 1 - yh) & (yp == lax.div(lax.rem(x + 2, 4), 2))
        return in_left | in_right

    def own_density(h):
        m = grow(pat[h]).astype(BF16)
        left[c, h, :, pl.ds(256, 128)] = jnp.zeros((W, 128), BF16)
        left[c, h, :, pl.ds(0, W)] = dens[h] * m[:, :W]
        mask[h] = m
        if h == 0:
            pl.semaphore_wait(barrier, len(ways))

    def prepare():
        for h in range(2):
            right[r, h, pl.ds(0, W)] = left[c, h]
        zero = jnp.zeros((2, WP - W, WP), BF16)

        def clear(k, carry):
            right[k, :, pl.ds(W, WP - W)] = zero
            sq[k, :, pl.ds(W, WP - W)] = zero
            return carry

        lax.fori_loop(0, NROW, clear, 0)
        acc[...] = jnp.zeros_like(acc)
        fetches[2].wait()
        fetches[3].wait()
        for h in range(2):
            kept[h] = grow(keep[h]).astype(BF16)
        routing_tables(owner, place, hot, hot_tail, rank_at, tail_at)

    def early():
        def add(p, carry):
            @pl.when(jnp.logical_not(is_late(p)))
            def _():
                multiply(p, right, None)
            return carry

        lax.fori_loop(0, NCOL // 2, add, 0)

    fetches[0].wait()
    fetches[1].wait()
    follow(FIRST_GATHER, own_density, {PREPARE: prepare, EARLY: early})

    def own_square(h):
        def add(p, carry):
            @pl.when(is_late(p))
            def _():
                multiply(p, right, h)
            return carry

        lax.fori_loop(0, NCOL // 2, add, 0)
        half = pl.ds(h * W, W)
        sq[r, h, pl.ds(0, W)] = (acc[half, :] / ORDER * mask[h].astype(F32)).astype(BF16)
        acc[half, :] = jnp.zeros((W, WP), F32)

    near = lax.div(x, 2)

    def second(yhp, pair):
        def add(h, carry):
            multiply((2 * h + yhp) * 2 + pair, sq, None)
            return carry

        lax.fori_loop(0, 2, add, 0)

    follow(SECOND_GATHER, own_square, {
        NEAR_OWN: lambda: second(yh, near),
        FAR_OWN: lambda: second(yh, 1 - near),
        NEAR_OTHER: lambda: second(1 - yh, near),
        FAR_OTHER: lambda: second(1 - yh, 1 - near),
    })

    for h in range(2):
        mat = left[c, h].astype(F32)
        new = kept[h].astype(F32) * (1.5 * mat - 0.5 * acc[pl.ds(h * W, W), :])
        for k in range(WP // 128):
            update[h, k] = new[:, k * 128 : k * 128 + 128]

    fill(update, rank_at, tail_at, place, hot, hot_tail, blocks, outgoing, tails)

    def partner(i):
        dcore, dz = lax.rem(i, 2), lax.rem(lax.div(i, 2), 4)
        dyl, dyh, dx = lax.rem(lax.div(i, 8), 2), lax.rem(lax.div(i, 16), 2), lax.div(i, 32)
        to_row = lax.rem(yh + dyh, 2) * 4 + lax.rem(x + dx, 4)
        to_col = lax.rem(z + dz, 4) * 4 + lax.rem(yl + dyl, 2) * 2 + lax.rem(core + dcore, 2)
        return to_row, to_col

    def rows_of(buf, device):
        return buf.at[pl.ds(pl.multiple_of(device * ROWS, ROWS), ROWS)]

    def message(i):
        to_row, to_col = partner(i)
        return pltpu.make_async_remote_copy(
            src_ref=rows_of(outgoing, to_row * NCOL + to_col), dst_ref=rows_of(arrived, me),
            send_sem=exchange_send, recv_sem=exchange_recv, device_id=(to_row, to_col), device_id_type=MESH)

    def start_message(i, carry):
        message(lax.rem(i * 37, DEVICES)).start()
        return carry

    line, in_line = r * 2 + yl, z * 2 + core

    def other_line(i):
        dyl, dyh, dx = i % 2, i // 2 % 2, i // 4
        return row(dx, dyh), yl if dyl == 0 else 1 - yl

    def line_copy(to, here, device):
        return pltpu.make_async_remote_copy(
            src_ref=to, dst_ref=here, send_sem=tail_send.at[0], recv_sem=tail_recv.at[0],
            device_id=device, device_id_type=MESH)

    def pass_on(to, here, device):
        return pltpu.make_async_remote_copy(
            src_ref=to, dst_ref=here, send_sem=tail_send.at[1], recv_sem=tail_recv.at[1],
            device_id=device, device_id_type=MESH)

    for i in range(1, 2 * NROW):
        to_row, to_yl = other_line(i)
        line_copy(rows_of(tails, to_row * 2 + to_yl), rows_of(relay_in, line),
                  (to_row, z * 4 + to_yl * 2 + core)).start()
    all_lines = line_copy(tails.at[pl.ds(0, (2 * NROW - 1) * ROWS)], relay_in.at[pl.ds(0, (2 * NROW - 1) * ROWS)],
                          ways[CORE])
    keep_line = pltpu.make_async_copy(rows_of(tails, line), rows_of(relay_in, line), local.at[5])
    keep_line.start()
    own = pltpu.make_async_copy(rows_of(outgoing, me), rows_of(arrived, me), local.at[4])
    own.start()
    lax.fori_loop(1, DEVICES // 2, start_message, 0)
    keep_line.wait()
    all_lines.wait_recv()
    relay_wide[...] = relay_in[...].astype(F32)
    for j in range(2 * 4):
        for k in range(2):
            part = relay_wide[pl.ds(2 * j + k, 2 * NROW, stride=ROWS), :]
            relay_out[pl.ds(j * ROWS, ROWS), pl.ds(128 * k, 128)] = part.astype(BF16)
    for i in range(1, 2 * 4):
        to_core = core if i % 2 == 0 else 1 - core
        to_z = lax.rem(z + i // 2, 4)
        pass_on(rows_of(relay_out, to_z * 2 + to_core), rows_of(tails_arrived, in_line),
                (r, to_z * 4 + yl * 2 + to_core)).start()
    all_passed = pass_on(relay_out.at[pl.ds(0, 7 * ROWS)], tails_arrived.at[pl.ds(0, 7 * ROWS)], ways[CORE])
    keep_tails = pltpu.make_async_copy(rows_of(relay_out, in_line), rows_of(tails_arrived, in_line), local.at[6])
    keep_tails.start()
    lax.fori_loop(DEVICES // 2, DEVICES, start_message, 0)
    for group, kinds in enumerate(((LEFT, SIBLING), (RIGHT, SQUARE))):
        sent = left.at[pl.ds(0, sum(kind in kinds for kind in started) // len(QUARTERS))]
        pltpu.make_async_remote_copy(
            src_ref=sent, dst_ref=sent, send_sem=send.at[group], recv_sem=recv.at[0],
            device_id=ways[CORE], device_id_type=MESH).wait_send()
    own.wait()
    keep_tails.wait()
    all_lines.wait_send()
    all_passed.wait_send()
    most = pl.ds(0, (DEVICES - 1) * ROWS)
    others = pltpu.make_async_remote_copy(
        src_ref=outgoing.at[most], dst_ref=arrived.at[most],
        send_sem=exchange_send, recv_sem=exchange_recv, device_id=ways[CORE], device_id_type=MESH)
    others.wait_send()
    others.wait_recv()
    all_passed.wait_recv()


N_BLOCKS = 2 * PB * PB


WINDOWS = [
    (w, i) for w in range(3) for i in range(BS) if i * BS + BS > w * 256 and i * BS < w * 256 + 256
]


def ranks(owner_row):
    owner = jnp.broadcast_to(owner_row.astype(F32), (8, N_BLOCKS))
    same = owner.T[:, :1] == owner[:1]
    one = lax.broadcasted_iota(jnp.int32, (N_BLOCKS, N_BLOCKS), 0)
    two = lax.broadcasted_iota(jnp.int32, (N_BLOCKS, N_BLOCKS), 1)
    rank = jnp.sum(jnp.where(same & (one < two), 1.0, 0.0), axis=0, keepdims=True).astype(jnp.int32)
    rank_col = jnp.sum(jnp.where(same & (two < one), 1.0, 0.0), axis=1, keepdims=True).astype(jnp.int32)
    return rank, rank_col


def routing_tables(owner, place, hot, hot_tail, rank_at, tail_at):
    lane = lax.broadcasted_iota(jnp.int32, (WP, 256), 0)
    at = lax.broadcasted_iota(jnp.int32, (WP, 256), 1)
    entry = lane - lax.div(lane, BS) * BS
    slot = lax.div(at, TAIL)
    def spread(k, carry):
        w = lax.div(k, 12)
        place[k] = jnp.where(at - entry == (k - w) * BS - w * 256, 1.0, 0.0).astype(BF16)
        return carry

    lax.fori_loop(0, 24, spread, 0)
    offset = at - slot * TAIL
    fits = (slot < 6) & (offset - entry == (BS - 1) * BS - 512) & (offset < ENT - 512)
    place[24] = jnp.where(fits, 1.0, 0.0).astype(BF16)
    rank, rank_col = ranks(owner[...])
    rank_at[...] = jnp.broadcast_to(rank_col, rank_at.shape)
    group = lax.div(lax.broadcasted_iota(jnp.int32, tail_at.shape, 1), TAIL)
    tail_at[...] = jnp.where(rank_col - lax.div(rank_col, 6) * 6 == group, 1.0, 0.0)
    own = owner[...]
    key = own * ROWS + rank
    last_key = own * ROWS + CAP + rank - lax.div(rank, 4) * 4
    to_row, to_col = lax.div(own, NCOL), lax.rem(own, NCOL)
    line = to_row * 2 + lax.rem(lax.div(to_col, 2), 2)
    in_line = lax.div(to_col, 4) * 2 + lax.rem(to_col, 2)
    tail_key = line * ROWS + in_line * 2 + lax.div(rank, 6)
    step = 256

    def compare(k, carry):
        rows = pl.ds(pl.multiple_of(k * step, step), step)
        at = lax.broadcasted_iota(jnp.int32, (step, N_BLOCKS), 0) + k * step
        hot[rows, pl.ds(0, N_BLOCKS)] = jnp.where(at == key, 1.0, 0.0).astype(BF16)
        hot[rows, pl.ds(N_BLOCKS, N_BLOCKS)] = jnp.where(at == last_key, 1.0, 0.0).astype(BF16)
        return carry

    lax.fori_loop(0, DEVICES * ROWS // step, compare, 0)
    at = lax.broadcasted_iota(jnp.int32, hot_tail.shape, 0)
    hot_tail[...] = jnp.where(at == tail_key, 1.0, 0.0).astype(BF16)


def fill(update, rank_at, tail_at, place, hot, hot_tail, blocks, outgoing, tails):
    n = N_BLOCKS
    half = PB // 2
    picks = []
    for g in range(2):
        bc = lax.broadcasted_iota(jnp.int32, (half, 256), 0) + g * half
        entry = lax.broadcasted_iota(jnp.int32, (half, 256), 1) + g * 128
        picks.append(jnp.where((entry >= bc * BS) & (entry < bc * BS + BS), 1.0, 0.0)[None])
    for w in (2, 0, 1):
        total = [None, None]
        for k, (wk, i) in enumerate(WINDOWS):
            if wk != w:
                continue
            u = [[update[h, j, pl.ds(i, PB, stride=BS), :] for j in range(WP // 128)] for h in range(2)]
            for g in range(2):
                rows = [
                    (jnp.concatenate(u[h][g : g + 2], axis=1)[:, None, :] * picks[g]).astype(BF16)
                    .reshape(PB * half, 256)
                    for h in range(2)
                ]
                term = jnp.dot(jnp.concatenate(rows, axis=0), place[k, pl.ds(128 * g, 256), :],
                               preferred_element_type=F32)
                total[g] = term if total[g] is None else total[g] + term
        both = [t.reshape(2 * PB, 1, half, 256) for t in total]
        both = jnp.concatenate(both, axis=1).reshape(n, 256)
        if w == 2:
            tail = (both[:, :128] * tail_at[...]).astype(BF16)
            tails[...] = jnp.dot(hot_tail[...], tail, preferred_element_type=F32).astype(BF16)
        elif w == 0:
            blocks[pl.ds(0, n), pl.ds(0, 256)] = both.astype(BF16)
        else:
            blocks[pl.ds(0, n), pl.ds(256, 128)] = both[:, :128].astype(BF16)
            rank = rank_at[...]
            for j in range(3):
                mine = (rank >= 4 * j) & (rank < 4 * j + 4)
                blocks[pl.ds(n, n), pl.ds(128 * j, 128)] = jnp.where(mine, both[:, 128:], 0.0).astype(BF16)
    step = 512
    for k in range(0, DEVICES * ROWS, step):
        outgoing[pl.ds(k, step), :] = jnp.dot(
            hot[pl.ds(k, step), :], blocks[...], preferred_element_type=F32).astype(BF16)


N_COPIES = sum(op[0] == SEND for op in FIRST_GATHER + SECOND_GATHER)


def stepped(density, pattern, keep, owner):
    anywhere = pl.BlockSpec(memory_space=pl.ANY)
    owner = owner.reshape(1, N_BLOCKS)
    return pl.pallas_call(
        whole_step,
        out_shape=(
            jax.ShapeDtypeStruct((DEVICES * ROWS, LANES), BF16),
            jax.ShapeDtypeStruct((DEVICES, 256), BF16),
        ),
        in_specs=[anywhere] * 4,
        out_specs=(anywhere, anywhere),
        scratch_shapes=[
            pltpu.VMEM(density.shape, BF16),
            pltpu.VMEM(pattern.shape, jnp.int32),
            pltpu.VMEM(keep.shape, jnp.int32),
            pltpu.VMEM(owner.shape, jnp.int32),
            pltpu.VMEM((NCOL, 2, W, WP), BF16),
            pltpu.VMEM((NROW, 2, WP, WP), BF16),
            pltpu.VMEM((NROW, 2, WP, WP), BF16),
            pltpu.VMEM((2, W, WP), BF16),
            pltpu.VMEM((2, W, WP), BF16),
            pltpu.VMEM((2 * W, WP), F32),
            pltpu.VMEM((2, WP // 128, W, 128), F32),
            pltpu.VMEM((25, WP, 256), BF16),
            pltpu.VMEM((DEVICES * ROWS, 2 * N_BLOCKS), BF16),
            pltpu.VMEM((2 * NROW * ROWS, N_BLOCKS), BF16),
            pltpu.VMEM((N_BLOCKS, 128), jnp.int32),
            pltpu.VMEM((N_BLOCKS, 128), F32),
            pltpu.VMEM((2 * N_BLOCKS, LANES), BF16),
            pltpu.VMEM((DEVICES * ROWS, LANES), BF16),
            pltpu.VMEM((2 * NROW * ROWS, 128), BF16),
            pltpu.VMEM((2 * NROW * ROWS, 128), BF16),
            pltpu.VMEM((2 * NROW * ROWS, 128), F32),
            pltpu.VMEM((DEVICES, 256), BF16),
            pltpu.SemaphoreType.DMA((2,)),
            pltpu.SemaphoreType.DMA((N_COPIES,)),
            pltpu.SemaphoreType.DMA,
            pltpu.SemaphoreType.DMA,
            pltpu.SemaphoreType.DMA((2,)),
            pltpu.SemaphoreType.DMA((2,)),
            pltpu.SemaphoreType.DMA((7,)),
        ],
        compiler_params=pltpu.CompilerParams(
            collective_id=0, has_side_effects=True, vmem_limit_bytes=56 * 1024 * 1024),
        name="whole_step",
    )(density, pattern, keep, owner)


def unpack(messages, tails, out, arrived, tails_in, wide, tails_wide, by_source, ready, sem):
    chunks = [pl.ds(128 * k, 128) for k in range(LANES // 128)]
    fetches = [
        pltpu.make_async_copy(messages.at[:, at], arrived.at[:, at], sem.at[CAP + k])
        for k, at in enumerate(chunks)
    ]
    fetch_tails = pltpu.make_async_copy(tails, tails_in, sem.at[CAP + len(chunks)])
    fetch_tails.start()
    for fetch in fetches:
        fetch.start()

    fetch_tails.wait()
    for k in range(2):
        tails_wide[k] = tails_in[:, pl.ds(128 * k, 128)].astype(F32)
        for j in range(8):
            for yl in range(2):
                source = j // 2 * 4 + yl * 2 + j % 2
                by_source[k, pl.ds(source, NROW, stride=NCOL), :] = tails_wide[k, pl.ds(j * ROWS + yl, NROW, stride=2), :]
        rows = by_source[k].T.astype(BF16)
        for s in range(6):
            ready[6 * k + s, pl.ds(512, ENT - 512), :] = rows[s * TAIL : s * TAIL + ENT - 512]
    copies = []
    for k, at in enumerate(chunks):
        fetches[k].wait()
        wide[k] = arrived[:, at].astype(F32)
        for s in range(4):
            fourth = wide[k, pl.ds(CAP + s, DEVICES, stride=ROWS), :]
            ready[4 * k + s, pl.ds(384, 128), :] = fourth.T.astype(BF16)
        for s in range(CAP):
            ready[s, at, :] = wide[k, pl.ds(s, DEVICES, stride=ROWS), :].T.astype(BF16)
            if k == len(chunks) - 1:
                copies.append(pltpu.make_async_copy(ready.at[s], out.at[s], sem.at[s]))
                copies[-1].start()
    for copy in copies:
        copy.wait()


def unpacked(messages, tails):
    anywhere = pl.BlockSpec(memory_space=pl.ANY)
    out = pl.pallas_call(
        unpack,
        out_shape=jax.ShapeDtypeStruct((CAP, ENT, DEVICES), BF16),
        in_specs=[anywhere] * 2,
        out_specs=anywhere,
        scratch_shapes=[
            pltpu.VMEM((DEVICES * ROWS, LANES), BF16),
            pltpu.VMEM((DEVICES, 256), BF16),
            pltpu.VMEM((LANES // 128, DEVICES * ROWS, 128), F32),
            pltpu.VMEM((2, DEVICES, 128), F32),
            pltpu.VMEM((2, DEVICES, 128), F32),
            pltpu.VMEM((CAP, ENT, DEVICES), BF16),
            pltpu.SemaphoreType.DMA((CAP + 4,)),
        ],
        compiler_params=pltpu.CompilerParams(vmem_limit_bytes=58 * 1024 * 1024),
        name="unpack",
    )(messages, tails)
    return out.transpose(2, 0, 1)[None]


def per_device(density, pattern, keep, owner):
    return unpacked(*stepped(density, pattern, keep, owner))


def solution(mesh):
    placed = (
        P(None, "row", "col"),
        P(None, "row", "col"),
        P(None, "row", "col"),
        P(("row", "col"), None, None),
    )
    return jax.shard_map(
        per_device,
        mesh=mesh,
        in_specs=placed,
        out_specs=P(("row", "col"), None, None, None),
        check_vma=False,
    )
```

```python
import jax
import jax.numpy as jnp
from jax import lax
from jax.experimental import pallas as pl
from jax.experimental.pallas import tpu as pltpu
from jax.sharding import PartitionSpec as P

BS = 23
PB = 16
W = BS * PB
WP = 384
ORDER = 5888
NROW = 8
NCOL = 16
DEVICES = NROW * NCOL
CAP = 12
ENT = BS * BS
ROWS = 16
LANES = 384
TAIL = 21
MESH = pl.DeviceIdType.MESH
F32 = jnp.float32
BF16 = jnp.bfloat16


QUARTERS = ((0, 0, 240), (0, 240, W), (1, 0, 240), (1, 240, W))

OWN, SEND, WAIT, DO = range(4)
LEFT, SIBLING, RIGHT, SQUARE = range(4)
CORE, YA, YB, YY, ZP, ZM, XP, XM = range(8)
PREPARE, FIRST_PAIRS, EARLY, LATE, NEAR_OWN, FAR_OWN, NEAR_OTHER, FAR_OTHER = range(8)
FIRST_GATHER = (
    (OWN, 0), (SEND, LEFT, 0, 1, 0, LEFT, 0, 0, YA), (SEND, LEFT, -1, 0, 0, LEFT, 0, 0, ZP), (WAIT, SIBLING, 0, 0, 0),
    (SEND, SIBLING, 0, 0, 0, LEFT, 0, 0, CORE), (SEND, LEFT, 1, 0, 1, LEFT, 0, 0, ZM),
    (SEND, RIGHT, -1, 0, 1, RIGHT, 0, 0, XP), (WAIT, RIGHT, 1, 0, 0), (SEND, RIGHT, 1, 0, 0, RIGHT, 0, 0, XM),
    (SEND, RIGHT, -1, 0, 0, RIGHT, 0, 0, XP), (SEND, LEFT, -1, 0, 1, LEFT, 0, 0, ZP),
    (SEND, LEFT, 1, 0, 0, LEFT, 0, 0, ZM), (WAIT, SIBLING, 0, 0, 1), (SEND, SIBLING, 0, 0, 1, LEFT, 0, 0, CORE),
    (OWN, 1), (SEND, LEFT, 0, 1, 1, LEFT, 0, 0, YA), (WAIT, SIBLING, 0, 0, 2),
    (SEND, SIBLING, 0, 0, 2, LEFT, 0, 0, CORE), (SEND, RIGHT, 1, 0, 3, RIGHT, 0, 0, XM), (WAIT, SIBLING, 0, 0, 3),
    (SEND, SIBLING, 0, 0, 3, LEFT, 0, 0, CORE), (DO, PREPARE), (SEND, LEFT, -1, 0, 3, LEFT, 0, 0, ZP),
    (SEND, LEFT, 0, 1, 2, LEFT, 0, 0, YA), (SEND, LEFT, 1, 0, 2, LEFT, 0, 0, ZM), (WAIT, RIGHT, 1, 0, 1),
    (SEND, RIGHT, 1, 0, 1, RIGHT, 0, 0, XM), (SEND, RIGHT, -1, 0, 2, RIGHT, 0, 0, XP), (WAIT, LEFT, 1, 0, 1),
    (WAIT, SIBLING, 1, 0, 1), (SEND, SIBLING, 1, 0, 1, LEFT, 1, 0, CORE), (SEND, LEFT, -1, 0, 2, LEFT, 0, 0, ZP),
    (WAIT, RIGHT, -1, 0, 1), (WAIT, LEFT, 0, 1, 0), (SEND, RIGHT, 0, 1, 0, LEFT, 0, 1, YB), (WAIT, SIBLING, 0, 1, 0),
    (SEND, SIBLING, 0, 1, 0, LEFT, 0, 1, CORE), (SEND, LEFT, 0, 1, 3, LEFT, 0, 0, YA), (WAIT, RIGHT, 1, 0, 2),
    (SEND, RIGHT, 1, 0, 2, RIGHT, 0, 0, XM), (WAIT, LEFT, -1, 0, 0), (WAIT, SIBLING, -1, 0, 0),
    (SEND, SIBLING, -1, 0, 0, LEFT, -1, 0, CORE), (SEND, LEFT, 1, 0, 3, LEFT, 0, 0, ZM), (WAIT, RIGHT, 2, 0, 1),
    (SEND, RIGHT, 2, 0, 1, RIGHT, -1, 0, XP), (WAIT, LEFT, 0, 1, 1), (WAIT, SIBLING, 0, 1, 1),
    (SEND, SIBLING, 0, 1, 1, LEFT, 0, 1, CORE), (SEND, RIGHT, 0, 1, 1, LEFT, 0, 1, YB), (WAIT, LEFT, -1, 0, 1),
    (SEND, LEFT, -1, 1, 0, LEFT, -1, 0, YA), (WAIT, SIBLING, -1, 0, 1), (SEND, SIBLING, -1, 0, 1, LEFT, -1, 0, CORE),
    (SEND, LEFT, 2, 0, 1, LEFT, -1, 0, ZP), (WAIT, LEFT, 1, 0, 0), (SEND, LEFT, 1, 1, 0, LEFT, 0, 1, ZM),
    (WAIT, SIBLING, 1, 0, 0), (SEND, SIBLING, 1, 0, 0, LEFT, 1, 0, CORE), (SEND, RIGHT, -1, 0, 3, RIGHT, 0, 0, XP),
    (WAIT, RIGHT, -1, 0, 0), (WAIT, RIGHT, 1, 0, 3), (WAIT, RIGHT, 2, 0, 3), (SEND, RIGHT, 2, 0, 3, RIGHT, 1, 0, XM),
    (WAIT, LEFT, -1, 0, 3), (WAIT, SIBLING, -1, 0, 3), (SEND, SIBLING, -1, 0, 3, LEFT, -1, 0, CORE),
    (WAIT, LEFT, 0, 1, 2), (SEND, LEFT, 2, 0, 0, LEFT, -1, 0, ZP), (WAIT, SIBLING, 0, 1, 2),
    (SEND, SIBLING, 0, 1, 2, LEFT, 0, 1, CORE), (SEND, RIGHT, 0, 1, 2, LEFT, 0, 1, YB),
    (SEND, LEFT, -1, 1, 3, LEFT, -1, 0, YA), (SEND, RIGHT, 2, 0, 0, RIGHT, -1, 0, XP), (WAIT, RIGHT, 0, 1, 0),
    (SEND, LEFT, 1, 1, 2, LEFT, 0, 1, ZM), (WAIT, RIGHT, 1, 1, 0), (SEND, RIGHT, 1, 1, 0, RIGHT, 0, 1, XM),
    (WAIT, LEFT, 1, 0, 2), (WAIT, SIBLING, 1, 0, 2), (SEND, SIBLING, 1, 0, 2, LEFT, 1, 0, CORE),
    (WAIT, RIGHT, -1, 0, 2), (WAIT, LEFT, 0, 1, 3), (WAIT, SIBLING, 0, 1, 3),
    (SEND, SIBLING, 0, 1, 3, LEFT, 0, 1, CORE), (SEND, RIGHT, 0, 1, 3, LEFT, 0, 1, YB), (WAIT, LEFT, -1, 0, 2),
    (SEND, LEFT, 1, 1, 1, LEFT, 1, 0, YA), (WAIT, SIBLING, -1, 0, 2), (SEND, SIBLING, -1, 0, 2, LEFT, -1, 0, CORE),
    (SEND, LEFT, 2, 0, 3, LEFT, -1, 0, ZP), (WAIT, RIGHT, 0, 1, 1), (WAIT, RIGHT, 2, 0, 2),
    (SEND, RIGHT, 2, 0, 2, RIGHT, -1, 0, XP), (WAIT, LEFT, 1, 0, 3), (SEND, RIGHT, 1, 1, 1, RIGHT, 0, 1, XM),
    (WAIT, SIBLING, 1, 0, 3), (SEND, SIBLING, 1, 0, 3, LEFT, 1, 0, CORE), (WAIT, LEFT, 2, 0, 1),
    (WAIT, SIBLING, 2, 0, 1), (SEND, SIBLING, 2, 0, 1, LEFT, 2, 0, CORE), (WAIT, RIGHT, -1, 1, 1),
    (SEND, RIGHT, -1, 1, 1, RIGHT, -1, 0, YY), (SEND, LEFT, 2, 0, 2, LEFT, 1, 0, ZM), (WAIT, RIGHT, -1, 0, 3),
    (SEND, LEFT, -1, 1, 1, LEFT, 0, 1, ZP), (WAIT, LEFT, -1, 1, 0), (WAIT, SIBLING, -1, 1, 0),
    (SEND, SIBLING, -1, 1, 0, LEFT, -1, 1, CORE), (WAIT, LEFT, 1, 1, 0), (WAIT, SIBLING, 1, 1, 0),
    (SEND, SIBLING, 1, 1, 0, LEFT, 1, 1, CORE), (WAIT, RIGHT, 0, 1, 2), (SEND, RIGHT, -1, 1, 3, RIGHT, -1, 0, YY),
    (SEND, LEFT, 2, 1, 0, LEFT, -1, 1, ZP), (SEND, RIGHT, 1, 1, 2, RIGHT, 0, 1, XM), (WAIT, LEFT, -1, 1, 3),
    (WAIT, SIBLING, -1, 1, 3), (SEND, SIBLING, -1, 1, 3, LEFT, -1, 1, CORE), (WAIT, RIGHT, -1, 1, 2),
    (SEND, RIGHT, -1, 1, 2, RIGHT, 0, 1, XP), (WAIT, LEFT, 2, 0, 0), (WAIT, SIBLING, 2, 0, 0),
    (SEND, SIBLING, 2, 0, 0, LEFT, 2, 0, CORE), (SEND, LEFT, 1, 1, 3, LEFT, 0, 1, ZM),
    (SEND, LEFT, -1, 1, 2, LEFT, -1, 0, YA), (WAIT, RIGHT, 2, 0, 0), (WAIT, RIGHT, 0, 1, 3), (WAIT, RIGHT, 1, 1, 3),
    (SEND, RIGHT, 1, 1, 3, RIGHT, 0, 1, XM), (WAIT, LEFT, 1, 1, 1), (WAIT, SIBLING, 1, 1, 1),
    (SEND, SIBLING, 1, 1, 1, LEFT, 1, 1, CORE), (WAIT, LEFT, 1, 1, 2), (WAIT, SIBLING, 1, 1, 2),
    (SEND, SIBLING, 1, 1, 2, LEFT, 1, 1, CORE), (WAIT, LEFT, 2, 0, 3), (SEND, LEFT, 2, 1, 2, LEFT, 1, 1, ZM),
    (SEND, LEFT, 2, 1, 3, LEFT, -1, 1, ZP), (WAIT, RIGHT, -1, 1, 0), (SEND, RIGHT, -1, 1, 0, RIGHT, 0, 1, XP),
    (WAIT, SIBLING, 2, 0, 3), (SEND, SIBLING, 2, 0, 3, LEFT, 2, 0, CORE), (WAIT, RIGHT, 1, 1, 1),
    (WAIT, RIGHT, 2, 1, 1), (SEND, RIGHT, 2, 1, 1, RIGHT, 1, 1, XM), (WAIT, LEFT, -1, 1, 1),
    (WAIT, SIBLING, -1, 1, 1), (SEND, SIBLING, -1, 1, 1, LEFT, -1, 1, CORE), (WAIT, RIGHT, 2, 1, 0),
    (SEND, RIGHT, 2, 1, 0, RIGHT, 2, 0, YY), (SEND, LEFT, 2, 1, 1, LEFT, -1, 1, ZP), (WAIT, LEFT, 2, 0, 2),
    (WAIT, SIBLING, 2, 0, 2), (SEND, SIBLING, 2, 0, 2, LEFT, 2, 0, CORE), (WAIT, RIGHT, 1, 1, 2),
    (WAIT, RIGHT, 2, 1, 2), (SEND, RIGHT, 2, 1, 2, RIGHT, 1, 1, XM), (WAIT, RIGHT, -1, 1, 3), (WAIT, RIGHT, 2, 1, 3),
    (SEND, RIGHT, 2, 1, 3, RIGHT, -1, 1, XP), (DO, FIRST_PAIRS), (WAIT, LEFT, 1, 1, 3), (WAIT, SIBLING, 1, 1, 3),
    (SEND, SIBLING, 1, 1, 3, LEFT, 1, 1, CORE), (WAIT, LEFT, 2, 1, 0), (WAIT, SIBLING, 2, 1, 0),
    (SEND, SIBLING, 2, 1, 0, LEFT, 2, 1, CORE), (WAIT, LEFT, -1, 1, 2), (WAIT, SIBLING, -1, 1, 2),
    (SEND, SIBLING, -1, 1, 2, LEFT, -1, 1, CORE), (WAIT, LEFT, 2, 1, 3), (WAIT, SIBLING, 2, 1, 3),
    (SEND, SIBLING, 2, 1, 3, LEFT, 2, 1, CORE), (WAIT, LEFT, 2, 1, 2), (WAIT, SIBLING, 2, 1, 2),
    (SEND, SIBLING, 2, 1, 2, LEFT, 2, 1, CORE), (WAIT, LEFT, 2, 1, 1), (WAIT, SIBLING, 2, 1, 1),
    (SEND, SIBLING, 2, 1, 1, LEFT, 2, 1, CORE), (DO, EARLY),
)

SECOND_GATHER = (
    (OWN, 0), (SEND, SQUARE, 0, 1, 1, SQUARE, 0, 0, YY), (WAIT, SQUARE, 1, 0, 0),
    (SEND, SQUARE, 1, 0, 0, SQUARE, 0, 0, XM), (SEND, SQUARE, 0, 1, 0, SQUARE, 0, 0, YY),
    (SEND, SQUARE, -1, 0, 1, SQUARE, 0, 0, XP), (SEND, SQUARE, -1, 0, 0, SQUARE, 0, 0, XP), (OWN, 1),
    (SEND, SQUARE, 1, 0, 3, SQUARE, 0, 0, XM), (WAIT, SQUARE, -1, 0, 1), (SEND, SQUARE, 0, 1, 3, SQUARE, 0, 0, YY),
    (WAIT, SQUARE, -1, 0, 3), (SEND, SQUARE, -1, 0, 3, SQUARE, 0, 0, XP), (WAIT, SQUARE, 2, 0, 1),
    (SEND, SQUARE, 2, 0, 1, SQUARE, -1, 0, XP), (WAIT, SQUARE, 1, 0, 1), (SEND, SQUARE, 1, 0, 1, SQUARE, 0, 0, XM),
    (SEND, SQUARE, 1, 0, 2, SQUARE, 0, 0, XM), (WAIT, SQUARE, 0, 1, 2), (SEND, SQUARE, 0, 1, 2, SQUARE, 0, 0, YY),
    (WAIT, SQUARE, 0, 1, 1), (WAIT, SQUARE, 1, 0, 3), (SEND, SQUARE, -1, 0, 2, SQUARE, 0, 0, XP),
    (WAIT, SQUARE, -1, 0, 0), (SEND, SQUARE, -1, 1, 0, SQUARE, -1, 0, YY), (WAIT, SQUARE, 1, 1, 1),
    (SEND, SQUARE, 1, 1, 1, SQUARE, 0, 1, XM), (WAIT, SQUARE, 0, 1, 0), (WAIT, SQUARE, 0, 1, 3),
    (WAIT, SQUARE, -1, 1, 3), (SEND, SQUARE, -1, 1, 3, SQUARE, 0, 1, XP), (WAIT, SQUARE, 2, 0, 3),
    (SEND, SQUARE, 2, 0, 3, SQUARE, 1, 0, XM), (WAIT, SQUARE, 1, 0, 2), (SEND, SQUARE, 2, 0, 2, SQUARE, 1, 0, XM),
    (WAIT, SQUARE, 1, 1, 2), (SEND, SQUARE, 1, 1, 2, SQUARE, 1, 0, YY), (SEND, SQUARE, -1, 1, 1, SQUARE, 0, 1, XP),
    (WAIT, SQUARE, -1, 0, 2), (SEND, SQUARE, 1, 1, 3, SQUARE, 0, 1, XM), (WAIT, SQUARE, -1, 1, 2),
    (SEND, SQUARE, -1, 1, 2, SQUARE, -1, 0, YY), (WAIT, SQUARE, 2, 0, 0), (SEND, SQUARE, 2, 0, 0, SQUARE, -1, 0, XP),
    (DO, NEAR_OWN), (WAIT, SQUARE, -1, 1, 0), (WAIT, SQUARE, 2, 1, 0), (SEND, SQUARE, 2, 1, 0, SQUARE, -1, 1, XP),
    (WAIT, SQUARE, 1, 1, 0), (SEND, SQUARE, 1, 1, 0, SQUARE, 0, 1, XM), (WAIT, SQUARE, -1, 1, 1),
    (WAIT, SQUARE, 2, 0, 2), (WAIT, SQUARE, 2, 1, 2), (SEND, SQUARE, 2, 1, 2, SQUARE, 2, 0, YY),
    (WAIT, SQUARE, 1, 1, 3), (WAIT, SQUARE, 2, 1, 3), (SEND, SQUARE, 2, 1, 3, SQUARE, 1, 1, XM),
    (WAIT, SQUARE, 2, 1, 1), (SEND, SQUARE, 2, 1, 1, SQUARE, -1, 1, XP), (DO, FAR_OWN), (DO, NEAR_OTHER),
    (DO, FAR_OTHER),
)


FORWARDED = {(*op[5:8], op[4]) for op in FIRST_GATHER + SECOND_GATHER if op[0] == SEND}
GROUPS = 11


def group_of(kind, d, f, q):
    if (kind, d, f, q) in FORWARDED:
        return None
    if kind == SQUARE:
        return (NEAR_OTHER if d < 2 else FAR_OTHER) if f else (NEAR_OWN if d < 2 else FAR_OWN)
    work = LATE if (d, f) == (2, 1) else EARLY if f and (d or kind == RIGHT) else FIRST_PAIRS
    return 7 + work if kind == SIBLING else work


def grow_columns(mask):
    block = lax.broadcasted_iota(jnp.int32, (PB, WP), 0)
    col = lax.broadcasted_iota(jnp.int32, (PB, WP), 1)
    spread = jnp.where((col >= block * BS) & (col < block * BS + BS), 1.0, 0.0).astype(BF16)
    return jnp.dot(mask, spread, preferred_element_type=F32).astype(BF16)


def grow(mask):
    wide = grow_columns(mask.astype(F32).astype(BF16))
    row = lax.broadcasted_iota(jnp.int32, (W, PB), 0)
    block = lax.broadcasted_iota(jnp.int32, (W, PB), 1)
    spread = jnp.where((row >= block * BS) & (row < block * BS + BS), 1.0, 0.0).astype(BF16)
    return jnp.dot(spread, wide, preferred_element_type=F32)


def whole_step(
    dens_in, pat_in, keep_in, owner_in, arrived, tails_arrived,
    dens, pat, keep, owner, left, right, sq, mask, kept, acc, update, place, hot, hot_tail, rank_at, tail_at, blocks, outgoing,
    tails, relay_in, relay_wide, relay_out, send, recv, exchange_send, exchange_recv, tail_send, tail_recv, local,
):
    r = lax.axis_index("row")
    c = lax.axis_index("col")
    x, yh = lax.rem(r, 4), lax.div(r, 4)
    z, yl, core = lax.div(c, 4), lax.rem(lax.div(c, 2), 2), lax.rem(c, 2)
    me = r * NCOL + c

    def col(dz, dyl, dcore=0):
        ycol = (1 - yl) if dyl else yl
        ccol = (1 - core) if dcore else core
        return lax.rem(z + dz + 4, 4) * 4 + ycol * 2 + ccol

    def row(dx, dyh):
        yrow = (1 - yh) if dyh else yh
        return yrow * 4 + lax.rem(x + dx + 4, 4)

    ways = {
        CORE: (r, col(0, 0, 1)),
        YA: (r, col(0, 1)),
        YB: (row(0, 1), col(0, 1)),
        YY: (row(0, 1), c),
        ZP: (r, col(1, 0)),
        ZM: (r, col(-1, 0)),
        XP: (row(1, 0), c),
        XM: (row(-1, 0), c),
    }

    fetches = [
        pltpu.make_async_copy(src, dst, local.at[k])
        for k, (src, dst) in enumerate(((pat_in, pat), (dens_in, dens), (keep_in, keep), (owner_in, owner)))
    ]
    for fetch in fetches:
        fetch.start()
    barrier = pltpu.get_barrier_semaphore()
    for dev in ways.values():
        pl.semaphore_signal(barrier, inc=1, device_id=dev, device_id_type=MESH)

    started = []
    arriving = {}
    expected = [0] * GROUPS

    def piece(buf, slot, q):
        h, first, end = QUARTERS[q]
        return buf.at[slot, h, pl.ds(first, end - first)]

    def find(kind, d, f, q):
        if kind == LEFT:
            return piece(left, col(d, f), q)
        if kind == SIBLING:
            return piece(left, col(d, f, 1), q)
        return piece(right if kind == RIGHT else sq, row(d, f), q)

    def start(kind, d, f, q, from_kind, from_d, from_f, way):
        k = group_of(kind, d, f, q)
        if k is None:
            k = GROUPS + len(arriving)
        else:
            _, first, end = QUARTERS[q]
            expected[k] += end - first
        group = 0 if kind in (LEFT, SIBLING) else 1
        if kind == RIGHT:
            src = piece(left, c, q) if (from_d, from_f) == (0, 0) else find(from_kind, from_d, from_f, q)
            dst = piece(right, r if from_kind == LEFT else row(from_d, from_f), q)
        else:
            src = dst = find(from_kind, from_d, from_f, q)
        op = pltpu.make_async_remote_copy(
            src_ref=src, dst_ref=dst, send_sem=send.at[group], recv_sem=recv.at[k],
            device_id=ways[way], device_id_type=MESH)
        op.start()
        started.append(kind)
        if k < GROUPS:
            return
        here = find(kind, d, f, q)
        arriving[kind, d, f, q] = pltpu.make_async_remote_copy(
            src_ref=here, dst_ref=here, send_sem=send.at[group], recv_sem=recv.at[k],
            device_id=ways[way], device_id_type=MESH)

    def join(group):
        rows = expected[group]
        if rows == 0:
            return
        all_rows = left.at[pl.ds(0, rows // (2 * W))] if rows % (2 * W) == 0 else outgoing.at[pl.ds(0, rows)]
        pltpu.make_async_remote_copy(
            src_ref=all_rows, dst_ref=all_rows, send_sem=send.at[0], recv_sem=recv.at[group],
            device_id=ways[CORE], device_id_type=MESH).wait_recv()

    def follow(table, own, work):
        for op, *what in table:
            if op == OWN:
                own(what[0])
            elif op == SEND:
                start(*what)
            elif op == WAIT:
                if group_of(*what) is None:
                    arriving[tuple(what)].wait_recv()
            else:
                join(what[0])
                work[what[0]]()

    def multiply(p, buf, h):
        if h is None:
            two = [left[2 * p + k].reshape(2 * W, WP) for k in range(2)]
            at = pl.ds(0, 2 * W)
        else:
            two = [left[2 * p + k, h] for k in range(2)]
            at = pl.ds(h * W, W)
        rows = buf[pl.ds(lax.rem(2 * p, NROW), 2), lax.div(p, 4)].reshape(2 * WP, WP)
        acc[at, :] += jnp.dot(jnp.concatenate(two, axis=1), rows, preferred_element_type=F32)

    def is_late(p):
        zp, yp = lax.div(p, 2), lax.rem(p, 2)
        in_left = (zp == lax.rem(z + 2, 4)) & (yp == 1 - yl)
        in_right = (lax.rem(zp, 2) == 1 - yh) & (yp == lax.div(lax.rem(x + 2, 4), 2))
        return in_left | in_right

    def own_density(h):
        m = grow(pat[h]).astype(BF16)
        left[c, h, :, pl.ds(256, 128)] = jnp.zeros((W, 128), BF16)
        left[c, h, :, pl.ds(0, W)] = dens[h] * m[:, :W]
        mask[h] = m
        if h == 0:
            pl.semaphore_wait(barrier, len(ways))

    def prepare():
        for h in range(2):
            right[r, h, pl.ds(0, W)] = left[c, h]
        zero = jnp.zeros((2, WP - W, WP), BF16)

        def clear(k, carry):
            right[k, :, pl.ds(W, WP - W)] = zero
            sq[k, :, pl.ds(W, WP - W)] = zero
            return carry

        lax.fori_loop(0, NROW, clear, 0)
        acc[...] = jnp.zeros_like(acc)
        fetches[2].wait()
        fetches[3].wait()
        for h in range(2):
            kept[h] = grow(keep[h]).astype(BF16)
        routing_tables(owner, place, hot, hot_tail, rank_at, tail_at)

    def is_first(p):
        zp, yp = lax.div(p, 2), lax.rem(p, 2)
        return (lax.rem(zp, 2) == yh) & ((yp == yl) | (zp == z)) & jnp.logical_not(is_late(p))

    def pairs(chosen, group):
        def add(p, carry):
            @pl.when(chosen(p))
            def _():
                multiply(p, right, None)
            return carry

        join(7 + group)
        lax.fori_loop(0, NCOL // 2, add, 0)

    fetches[0].wait()
    fetches[1].wait()
    follow(FIRST_GATHER, own_density, {
        PREPARE: prepare,
        FIRST_PAIRS: lambda: pairs(is_first, FIRST_PAIRS),
        EARLY: lambda: pairs(lambda p: jnp.logical_not(is_first(p) | is_late(p)), EARLY),
    })

    def own_square(h):
        if h == 0:
            join(LATE)
            join(7 + LATE)

        def add(p, carry):
            @pl.when(is_late(p))
            def _():
                multiply(p, right, h)
            return carry

        lax.fori_loop(0, NCOL // 2, add, 0)
        half = pl.ds(h * W, W)
        sq[r, h, pl.ds(0, W)] = (acc[half, :] / ORDER * mask[h].astype(F32)).astype(BF16)
        acc[half, :] = jnp.zeros((W, WP), F32)

    near = lax.div(x, 2)

    def second(yhp, pair):
        def add(h, carry):
            multiply((2 * h + yhp) * 2 + pair, sq, None)
            return carry

        lax.fori_loop(0, 2, add, 0)

    follow(SECOND_GATHER, own_square, {
        NEAR_OWN: lambda: second(yh, near),
        FAR_OWN: lambda: second(yh, 1 - near),
        NEAR_OTHER: lambda: second(1 - yh, near),
        FAR_OTHER: lambda: second(1 - yh, 1 - near),
    })

    for h in range(2):
        mat = left[c, h].astype(F32)
        new = kept[h].astype(F32) * (1.5 * mat - 0.5 * acc[pl.ds(h * W, W), :])
        for k in range(WP // 128):
            update[h, k] = new[:, k * 128 : k * 128 + 128]

    def rows_of(buf, device):
        return buf.at[pl.ds(pl.multiple_of(device * ROWS, ROWS), ROWS)]

    def messages(yhp, xp, first):
        at = pl.ds(pl.multiple_of((yhp * 2 + xp) * 512, 512), 512)
        outgoing[at, :] = jnp.dot(hot[at, :], blocks[...], preferred_element_type=F32).astype(BF16)

        def start_message(i, carry):
            i = lax.rem(i * 13, 32)
            dz, dyl, dcore, dx = lax.div(i, 8), lax.rem(lax.div(i, 4), 2), lax.rem(lax.div(i, 2), 2), lax.rem(i, 2)
            to_row = yhp * 4 + xp * 2 + lax.rem(x + dx, 2)
            to_col = lax.rem(z + dz, 4) * 4 + lax.rem(yl + dyl, 2) * 2 + lax.rem(core + dcore, 2)
            pltpu.make_async_remote_copy(
                src_ref=rows_of(outgoing, to_row * NCOL + to_col), dst_ref=rows_of(arrived, me),
                send_sem=exchange_send, recv_sem=exchange_recv, device_id=(to_row, to_col), device_id_type=MESH).start()
            return carry

        lax.fori_loop(first, 32, start_message, 0)

    line, in_line = r * 2 + yl, z * 2 + core

    def other_line(i):
        dyl, dyh, dx = i % 2, i // 2 % 2, i // 4
        return row(dx, dyh), yl if dyl == 0 else 1 - yl

    def line_copy(to, here, device):
        return pltpu.make_async_remote_copy(
            src_ref=to, dst_ref=here, send_sem=tail_send.at[0], recv_sem=tail_recv.at[0],
            device_id=device, device_id_type=MESH)

    def pass_on(to, here, device):
        return pltpu.make_async_remote_copy(
            src_ref=to, dst_ref=here, send_sem=tail_send.at[1], recv_sem=tail_recv.at[1],
            device_id=device, device_id_type=MESH)

    all_lines = line_copy(tails.at[pl.ds(0, (2 * NROW - 1) * ROWS)], relay_in.at[pl.ds(0, (2 * NROW - 1) * ROWS)],
                          ways[CORE])
    keep_line = pltpu.make_async_copy(rows_of(tails, line), rows_of(relay_in, line), local.at[5])

    def send_tails():
        for i in range(1, 2 * NROW):
            to_row, to_yl = other_line(i)
            line_copy(rows_of(tails, to_row * 2 + to_yl), rows_of(relay_in, line),
                      (to_row, z * 4 + to_yl * 2 + core)).start()
        keep_line.start()

    fill(update, rank_at, tail_at, place, hot_tail, blocks, tails, send_tails)

    messages(1 - yh, 1 - near, 0)
    messages(yh, 1 - near, 0)
    keep_line.wait()
    all_lines.wait_recv()
    relay_wide[...] = relay_in[...].astype(F32)
    for j in range(2 * 4):
        for k in range(2):
            part = relay_wide[pl.ds(2 * j + k, 2 * NROW, stride=ROWS), :]
            relay_out[pl.ds(j * ROWS, ROWS), pl.ds(128 * k, 128)] = part.astype(BF16)
    for i in range(1, 2 * 4):
        to_core = core if i % 2 == 0 else 1 - core
        to_z = lax.rem(z + i // 2, 4)
        pass_on(rows_of(relay_out, to_z * 2 + to_core), rows_of(tails_arrived, in_line),
                (r, to_z * 4 + yl * 2 + to_core)).start()
    all_passed = pass_on(relay_out.at[pl.ds(0, 7 * ROWS)], tails_arrived.at[pl.ds(0, 7 * ROWS)], ways[CORE])
    keep_tails = pltpu.make_async_copy(rows_of(relay_out, in_line), rows_of(tails_arrived, in_line), local.at[6])
    keep_tails.start()
    messages(1 - yh, near, 0)
    messages(yh, near, 1)
    own = pltpu.make_async_copy(rows_of(outgoing, me), rows_of(arrived, me), local.at[4])
    own.start()
    for group, kinds in enumerate(((LEFT, SIBLING), (RIGHT, SQUARE))):
        sent = left.at[pl.ds(0, sum(kind in kinds for kind in started) // len(QUARTERS))]
        pltpu.make_async_remote_copy(
            src_ref=sent, dst_ref=sent, send_sem=send.at[group], recv_sem=recv.at[group],
            device_id=ways[CORE], device_id_type=MESH).wait_send()
    own.wait()
    keep_tails.wait()
    all_lines.wait_send()
    all_passed.wait_send()
    most = pl.ds(0, (DEVICES - 1) * ROWS)
    others = pltpu.make_async_remote_copy(
        src_ref=outgoing.at[most], dst_ref=arrived.at[most],
        send_sem=exchange_send, recv_sem=exchange_recv, device_id=ways[CORE], device_id_type=MESH)
    others.wait_send()
    others.wait_recv()
    all_passed.wait_recv()


N_BLOCKS = 2 * PB * PB


WINDOWS = [
    (w, i) for w in range(3) for i in range(BS) if i * BS + BS > w * 256 and i * BS < w * 256 + 256
]


def ranks(owner_row):
    owner = jnp.broadcast_to(owner_row.astype(F32), (8, N_BLOCKS))
    same = owner.T[:, :1] == owner[:1]
    one = lax.broadcasted_iota(jnp.int32, (N_BLOCKS, N_BLOCKS), 0)
    two = lax.broadcasted_iota(jnp.int32, (N_BLOCKS, N_BLOCKS), 1)
    rank = jnp.sum(jnp.where(same & (one < two), 1.0, 0.0), axis=0, keepdims=True).astype(jnp.int32)
    rank_col = jnp.sum(jnp.where(same & (two < one), 1.0, 0.0), axis=1, keepdims=True).astype(jnp.int32)
    return rank, rank_col


def routing_tables(owner, place, hot, hot_tail, rank_at, tail_at):
    lane = lax.broadcasted_iota(jnp.int32, (WP, 256), 0)
    at = lax.broadcasted_iota(jnp.int32, (WP, 256), 1)
    entry = lane - lax.div(lane, BS) * BS
    slot = lax.div(at, TAIL)
    def spread(k, carry):
        w = lax.div(k, 12)
        place[k] = jnp.where(at - entry == (k - w) * BS - w * 256, 1.0, 0.0).astype(BF16)
        return carry

    lax.fori_loop(0, 24, spread, 0)
    offset = at - slot * TAIL
    fits = (slot < 6) & (offset - entry == (BS - 1) * BS - 512) & (offset < ENT - 512)
    place[24] = jnp.where(fits, 1.0, 0.0).astype(BF16)
    rank, rank_col = ranks(owner[...])
    rank_at[...] = jnp.broadcast_to(rank_col, rank_at.shape)
    group = lax.div(lax.broadcasted_iota(jnp.int32, tail_at.shape, 1), TAIL)
    tail_at[...] = jnp.where(rank_col - lax.div(rank_col, 6) * 6 == group, 1.0, 0.0)
    own = owner[...]
    key = own * ROWS + rank
    last_key = own * ROWS + CAP + rank - lax.div(rank, 4) * 4
    to_row, to_col = lax.div(own, NCOL), lax.rem(own, NCOL)
    line = to_row * 2 + lax.rem(lax.div(to_col, 2), 2)
    in_line = lax.div(to_col, 4) * 2 + lax.rem(to_col, 2)
    tail_key = line * ROWS + in_line * 2 + lax.div(rank, 6)
    step = 256

    def compare(k, carry):
        rows = pl.ds(pl.multiple_of(k * step, step), step)
        at = lax.broadcasted_iota(jnp.int32, (step, N_BLOCKS), 0) + k * step
        hot[rows, pl.ds(0, N_BLOCKS)] = jnp.where(at == key, 1.0, 0.0).astype(BF16)
        hot[rows, pl.ds(N_BLOCKS, N_BLOCKS)] = jnp.where(at == last_key, 1.0, 0.0).astype(BF16)
        return carry

    lax.fori_loop(0, DEVICES * ROWS // step, compare, 0)
    at = lax.broadcasted_iota(jnp.int32, hot_tail.shape, 0)
    hot_tail[...] = jnp.where(at == tail_key, 1.0, 0.0).astype(BF16)


def fill(update, rank_at, tail_at, place, hot_tail, blocks, tails, send_tails):
    n = N_BLOCKS
    half = PB // 2
    picks = []
    for g in range(2):
        bc = lax.broadcasted_iota(jnp.int32, (half, 256), 0) + g * half
        entry = lax.broadcasted_iota(jnp.int32, (half, 256), 1) + g * 128
        picks.append(jnp.where((entry >= bc * BS) & (entry < bc * BS + BS), 1.0, 0.0)[None])
    for w in (2, 0, 1):
        total = [None, None]
        for k, (wk, i) in enumerate(WINDOWS):
            if wk != w:
                continue
            u = [[update[h, j, pl.ds(i, PB, stride=BS), :] for j in range(WP // 128)] for h in range(2)]
            for g in range(2):
                rows = [
                    (jnp.concatenate(u[h][g : g + 2], axis=1)[:, None, :] * picks[g]).astype(BF16)
                    .reshape(PB * half, 256)
                    for h in range(2)
                ]
                term = jnp.dot(jnp.concatenate(rows, axis=0), place[k, pl.ds(128 * g, 256), :],
                               preferred_element_type=F32)
                total[g] = term if total[g] is None else total[g] + term
        both = [t.reshape(2 * PB, 1, half, 256) for t in total]
        both = jnp.concatenate(both, axis=1).reshape(n, 256)
        if w == 2:
            tail = (both[:, :128] * tail_at[...]).astype(BF16)
            tails[...] = jnp.dot(hot_tail[...], tail, preferred_element_type=F32).astype(BF16)
            send_tails()
        elif w == 0:
            blocks[pl.ds(0, n), pl.ds(0, 256)] = both.astype(BF16)
        else:
            blocks[pl.ds(0, n), pl.ds(256, 128)] = both[:, :128].astype(BF16)
            rank = rank_at[...]
            for j in range(3):
                mine = (rank >= 4 * j) & (rank < 4 * j + 4)
                blocks[pl.ds(n, n), pl.ds(128 * j, 128)] = jnp.where(mine, both[:, 128:], 0.0).astype(BF16)


N_ARRIVALS = GROUPS + sum(
    op[0] == SEND and group_of(*op[1:5]) is None for op in FIRST_GATHER + SECOND_GATHER)


def stepped(density, pattern, keep, owner):
    anywhere = pl.BlockSpec(memory_space=pl.ANY)
    owner = owner.reshape(1, N_BLOCKS)
    return pl.pallas_call(
        whole_step,
        out_shape=(
            jax.ShapeDtypeStruct((DEVICES * ROWS, LANES), BF16),
            jax.ShapeDtypeStruct((DEVICES, 256), BF16),
        ),
        in_specs=[anywhere] * 4,
        out_specs=(anywhere, anywhere),
        scratch_shapes=[
            pltpu.VMEM(density.shape, BF16),
            pltpu.VMEM(pattern.shape, jnp.int32),
            pltpu.VMEM(keep.shape, jnp.int32),
            pltpu.VMEM(owner.shape, jnp.int32),
            pltpu.VMEM((NCOL, 2, W, WP), BF16),
            pltpu.VMEM((NROW, 2, WP, WP), BF16),
            pltpu.VMEM((NROW, 2, WP, WP), BF16),
            pltpu.VMEM((2, W, WP), BF16),
            pltpu.VMEM((2, W, WP), BF16),
            pltpu.VMEM((2 * W, WP), F32),
            pltpu.VMEM((2, WP // 128, W, 128), F32),
            pltpu.VMEM((25, WP, 256), BF16),
            pltpu.VMEM((DEVICES * ROWS, 2 * N_BLOCKS), BF16),
            pltpu.VMEM((2 * NROW * ROWS, N_BLOCKS), BF16),
            pltpu.VMEM((N_BLOCKS, 128), jnp.int32),
            pltpu.VMEM((N_BLOCKS, 128), F32),
            pltpu.VMEM((2 * N_BLOCKS, LANES), BF16),
            pltpu.VMEM((DEVICES * ROWS, LANES), BF16),
            pltpu.VMEM((2 * NROW * ROWS, 128), BF16),
            pltpu.VMEM((2 * NROW * ROWS, 128), BF16),
            pltpu.VMEM((2 * NROW * ROWS, 128), F32),
            pltpu.VMEM((DEVICES, 256), BF16),
            pltpu.SemaphoreType.DMA((2,)),
            pltpu.SemaphoreType.DMA((N_ARRIVALS,)),
            pltpu.SemaphoreType.DMA,
            pltpu.SemaphoreType.DMA,
            pltpu.SemaphoreType.DMA((2,)),
            pltpu.SemaphoreType.DMA((2,)),
            pltpu.SemaphoreType.DMA((7,)),
        ],
        compiler_params=pltpu.CompilerParams(
            collective_id=0, has_side_effects=True, vmem_limit_bytes=56 * 1024 * 1024),
        name="whole_step",
    )(density, pattern, keep, owner)


def unpack(messages, tails, out, arrived, tails_in, wide, tails_wide, by_source, ready, sem):
    chunks = [pl.ds(128 * k, 128) for k in range(LANES // 128)]
    fetches = [
        pltpu.make_async_copy(messages.at[:, at], arrived.at[:, at], sem.at[CAP + k])
        for k, at in enumerate(chunks)
    ]
    fetch_tails = pltpu.make_async_copy(tails, tails_in, sem.at[CAP + len(chunks)])
    fetch_tails.start()
    for fetch in fetches:
        fetch.start()

    fetch_tails.wait()
    for k in range(2):
        tails_wide[k] = tails_in[:, pl.ds(128 * k, 128)].astype(F32)
        for j in range(8):
            for yl in range(2):
                source = j // 2 * 4 + yl * 2 + j % 2
                by_source[k, pl.ds(source, NROW, stride=NCOL), :] = tails_wide[k, pl.ds(j * ROWS + yl, NROW, stride=2), :]
        rows = by_source[k].T.astype(BF16)
        for s in range(6):
            ready[6 * k + s, pl.ds(512, ENT - 512), :] = rows[s * TAIL : s * TAIL + ENT - 512]
    copies = []
    for k, at in enumerate(chunks):
        fetches[k].wait()
        wide[k] = arrived[:, at].astype(F32)
        for s in range(4):
            fourth = wide[k, pl.ds(CAP + s, DEVICES, stride=ROWS), :]
            ready[4 * k + s, pl.ds(384, 128), :] = fourth.T.astype(BF16)
        for s in range(CAP):
            ready[s, at, :] = wide[k, pl.ds(s, DEVICES, stride=ROWS), :].T.astype(BF16)
            if k == len(chunks) - 1:
                copies.append(pltpu.make_async_copy(ready.at[s], out.at[s], sem.at[s]))
                copies[-1].start()
    for copy in copies:
        copy.wait()


def unpacked(messages, tails):
    anywhere = pl.BlockSpec(memory_space=pl.ANY)
    out = pl.pallas_call(
        unpack,
        out_shape=jax.ShapeDtypeStruct((CAP, ENT, DEVICES), BF16),
        in_specs=[anywhere] * 2,
        out_specs=anywhere,
        scratch_shapes=[
            pltpu.VMEM((DEVICES * ROWS, LANES), BF16),
            pltpu.VMEM((DEVICES, 256), BF16),
            pltpu.VMEM((LANES // 128, DEVICES * ROWS, 128), F32),
            pltpu.VMEM((2, DEVICES, 128), F32),
            pltpu.VMEM((2, DEVICES, 128), F32),
            pltpu.VMEM((CAP, ENT, DEVICES), BF16),
            pltpu.SemaphoreType.DMA((CAP + 4,)),
        ],
        compiler_params=pltpu.CompilerParams(vmem_limit_bytes=58 * 1024 * 1024),
        name="unpack",
    )(messages, tails)
    return out.transpose(2, 0, 1)[None]


def per_device(density, pattern, keep, owner):
    return unpacked(*stepped(density, pattern, keep, owner))


def solution(mesh):
    placed = (
        P(None, "row", "col"),
        P(None, "row", "col"),
        P(None, "row", "col"),
        P(("row", "col"), None, None),
    )
    return jax.shard_map(
        per_device,
        mesh=mesh,
        in_specs=placed,
        out_specs=P(("row", "col"), None, None, None),
        check_vma=False,
    )
```

```python
import jax
import jax.numpy as jnp
from jax import lax
from jax.experimental import pallas as pl
from jax.experimental.pallas import tpu as pltpu
from jax.sharding import PartitionSpec as P

BS = 23
PB = 16
W = BS * PB
WP = 384
ORDER = 5888
NROW = 8
NCOL = 16
DEVICES = NROW * NCOL
CAP = 12
ENT = BS * BS
ROWS = 16
LANES = 384
TAIL = 21
MESH = pl.DeviceIdType.MESH
F32 = jnp.float32
BF16 = jnp.bfloat16


QUARTERS = ((0, 0, 240), (0, 240, W), (1, 0, 240), (1, 240, W))

OWN, SEND, WAIT, DO = range(4)
LEFT, SIBLING, RIGHT, SQUARE = range(4)
CORE, YA, YB, YY, ZP, ZM, XP, XM = range(8)
PREPARE, FIRST_PAIRS, EARLY, LATE, NEAR_OWN, FAR_OWN, NEAR_OTHER, FAR_OTHER = range(8)
FIRST_GATHER = (
    (OWN, 0), (SEND, LEFT, 0, 1, 0, LEFT, 0, 0, YA), (SEND, LEFT, -1, 0, 0, LEFT, 0, 0, ZP), (WAIT, SIBLING, 0, 0, 0),
    (SEND, SIBLING, 0, 0, 0, LEFT, 0, 0, CORE), (SEND, LEFT, 1, 0, 1, LEFT, 0, 0, ZM),
    (SEND, RIGHT, -1, 0, 1, RIGHT, 0, 0, XP), (WAIT, RIGHT, 1, 0, 0), (SEND, RIGHT, 1, 0, 0, RIGHT, 0, 0, XM),
    (SEND, RIGHT, -1, 0, 0, RIGHT, 0, 0, XP), (SEND, LEFT, -1, 0, 1, LEFT, 0, 0, ZP),
    (SEND, LEFT, 1, 0, 0, LEFT, 0, 0, ZM), (WAIT, SIBLING, 0, 0, 1), (SEND, SIBLING, 0, 0, 1, LEFT, 0, 0, CORE),
    (OWN, 1), (SEND, LEFT, 0, 1, 1, LEFT, 0, 0, YA), (WAIT, SIBLING, 0, 0, 2),
    (SEND, SIBLING, 0, 0, 2, LEFT, 0, 0, CORE), (SEND, RIGHT, 1, 0, 3, RIGHT, 0, 0, XM), (WAIT, SIBLING, 0, 0, 3),
    (SEND, SIBLING, 0, 0, 3, LEFT, 0, 0, CORE), (DO, PREPARE), (SEND, LEFT, -1, 0, 3, LEFT, 0, 0, ZP),
    (SEND, LEFT, 0, 1, 2, LEFT, 0, 0, YA), (SEND, LEFT, 1, 0, 2, LEFT, 0, 0, ZM), (WAIT, RIGHT, 1, 0, 1),
    (SEND, RIGHT, 1, 0, 1, RIGHT, 0, 0, XM), (SEND, RIGHT, -1, 0, 2, RIGHT, 0, 0, XP), (WAIT, LEFT, 1, 0, 1),
    (WAIT, SIBLING, 1, 0, 1), (SEND, SIBLING, 1, 0, 1, LEFT, 1, 0, CORE), (SEND, LEFT, -1, 0, 2, LEFT, 0, 0, ZP),
    (WAIT, RIGHT, -1, 0, 1), (WAIT, LEFT, 0, 1, 0), (SEND, RIGHT, 0, 1, 0, LEFT, 0, 1, YB), (WAIT, SIBLING, 0, 1, 0),
    (SEND, SIBLING, 0, 1, 0, LEFT, 0, 1, CORE), (SEND, LEFT, 0, 1, 3, LEFT, 0, 0, YA), (WAIT, RIGHT, 1, 0, 2),
    (SEND, RIGHT, 1, 0, 2, RIGHT, 0, 0, XM), (WAIT, LEFT, -1, 0, 0), (WAIT, SIBLING, -1, 0, 0),
    (SEND, SIBLING, -1, 0, 0, LEFT, -1, 0, CORE), (SEND, LEFT, 1, 0, 3, LEFT, 0, 0, ZM), (WAIT, RIGHT, 2, 0, 1),
    (SEND, RIGHT, 2, 0, 1, RIGHT, -1, 0, XP), (WAIT, LEFT, 0, 1, 1), (WAIT, SIBLING, 0, 1, 1),
    (SEND, SIBLING, 0, 1, 1, LEFT, 0, 1, CORE), (SEND, RIGHT, 0, 1, 1, LEFT, 0, 1, YB), (WAIT, LEFT, -1, 0, 1),
    (SEND, LEFT, -1, 1, 0, LEFT, -1, 0, YA), (WAIT, SIBLING, -1, 0, 1), (SEND, SIBLING, -1, 0, 1, LEFT, -1, 0, CORE),
    (SEND, LEFT, 2, 0, 1, LEFT, -1, 0, ZP), (WAIT, LEFT, 1, 0, 0), (SEND, LEFT, 1, 1, 0, LEFT, 0, 1, ZM),
    (WAIT, SIBLING, 1, 0, 0), (SEND, SIBLING, 1, 0, 0, LEFT, 1, 0, CORE), (SEND, RIGHT, -1, 0, 3, RIGHT, 0, 0, XP),
    (WAIT, RIGHT, -1, 0, 0), (WAIT, RIGHT, 1, 0, 3), (WAIT, RIGHT, 2, 0, 3), (SEND, RIGHT, 2, 0, 3, RIGHT, 1, 0, XM),
    (WAIT, LEFT, -1, 0, 3), (WAIT, SIBLING, -1, 0, 3), (SEND, SIBLING, -1, 0, 3, LEFT, -1, 0, CORE),
    (WAIT, LEFT, 0, 1, 2), (SEND, LEFT, 2, 0, 0, LEFT, -1, 0, ZP), (WAIT, SIBLING, 0, 1, 2),
    (SEND, SIBLING, 0, 1, 2, LEFT, 0, 1, CORE), (SEND, RIGHT, 0, 1, 2, LEFT, 0, 1, YB),
    (SEND, LEFT, -1, 1, 3, LEFT, -1, 0, YA), (SEND, RIGHT, 2, 0, 0, RIGHT, -1, 0, XP), (WAIT, RIGHT, 0, 1, 0),
    (SEND, LEFT, 1, 1, 2, LEFT, 0, 1, ZM), (WAIT, RIGHT, 1, 1, 0), (SEND, RIGHT, 1, 1, 0, RIGHT, 0, 1, XM),
    (WAIT, LEFT, 1, 0, 2), (WAIT, SIBLING, 1, 0, 2), (SEND, SIBLING, 1, 0, 2, LEFT, 1, 0, CORE),
    (WAIT, RIGHT, -1, 0, 2), (WAIT, LEFT, 0, 1, 3), (WAIT, SIBLING, 0, 1, 3),
    (SEND, SIBLING, 0, 1, 3, LEFT, 0, 1, CORE), (SEND, RIGHT, 0, 1, 3, LEFT, 0, 1, YB), (WAIT, LEFT, -1, 0, 2),
    (SEND, LEFT, 1, 1, 1, LEFT, 1, 0, YA), (WAIT, SIBLING, -1, 0, 2), (SEND, SIBLING, -1, 0, 2, LEFT, -1, 0, CORE),
    (SEND, LEFT, 2, 0, 3, LEFT, -1, 0, ZP), (WAIT, RIGHT, 0, 1, 1), (WAIT, RIGHT, 2, 0, 2),
    (SEND, RIGHT, 2, 0, 2, RIGHT, -1, 0, XP), (WAIT, LEFT, 1, 0, 3), (SEND, RIGHT, 1, 1, 1, RIGHT, 0, 1, XM),
    (WAIT, SIBLING, 1, 0, 3), (SEND, SIBLING, 1, 0, 3, LEFT, 1, 0, CORE), (WAIT, LEFT, 2, 0, 1),
    (WAIT, SIBLING, 2, 0, 1), (SEND, SIBLING, 2, 0, 1, LEFT, 2, 0, CORE), (WAIT, RIGHT, -1, 1, 1),
    (SEND, RIGHT, -1, 1, 1, RIGHT, -1, 0, YY), (SEND, LEFT, 2, 0, 2, LEFT, 1, 0, ZM), (WAIT, RIGHT, -1, 0, 3),
    (SEND, LEFT, -1, 1, 1, LEFT, 0, 1, ZP), (WAIT, LEFT, -1, 1, 0), (WAIT, SIBLING, -1, 1, 0),
    (SEND, SIBLING, -1, 1, 0, LEFT, -1, 1, CORE), (WAIT, LEFT, 1, 1, 0), (WAIT, SIBLING, 1, 1, 0),
    (SEND, SIBLING, 1, 1, 0, LEFT, 1, 1, CORE), (WAIT, RIGHT, 0, 1, 2), (SEND, RIGHT, -1, 1, 3, RIGHT, -1, 0, YY),
    (SEND, LEFT, 2, 1, 0, LEFT, -1, 1, ZP), (SEND, RIGHT, 1, 1, 2, RIGHT, 0, 1, XM), (WAIT, LEFT, -1, 1, 3),
    (WAIT, SIBLING, -1, 1, 3), (SEND, SIBLING, -1, 1, 3, LEFT, -1, 1, CORE), (WAIT, RIGHT, -1, 1, 2),
    (SEND, RIGHT, -1, 1, 2, RIGHT, 0, 1, XP), (WAIT, LEFT, 2, 0, 0), (WAIT, SIBLING, 2, 0, 0),
    (SEND, SIBLING, 2, 0, 0, LEFT, 2, 0, CORE), (SEND, LEFT, 1, 1, 3, LEFT, 0, 1, ZM),
    (SEND, LEFT, -1, 1, 2, LEFT, -1, 0, YA), (WAIT, RIGHT, 2, 0, 0), (WAIT, RIGHT, 0, 1, 3), (WAIT, RIGHT, 1, 1, 3),
    (SEND, RIGHT, 1, 1, 3, RIGHT, 0, 1, XM), (WAIT, LEFT, 1, 1, 1), (WAIT, SIBLING, 1, 1, 1),
    (SEND, SIBLING, 1, 1, 1, LEFT, 1, 1, CORE), (WAIT, LEFT, 1, 1, 2), (WAIT, SIBLING, 1, 1, 2),
    (SEND, SIBLING, 1, 1, 2, LEFT, 1, 1, CORE), (WAIT, LEFT, 2, 0, 3), (SEND, LEFT, 2, 1, 2, LEFT, 1, 1, ZM),
    (SEND, LEFT, 2, 1, 3, LEFT, -1, 1, ZP), (WAIT, RIGHT, -1, 1, 0), (SEND, RIGHT, -1, 1, 0, RIGHT, 0, 1, XP),
    (WAIT, SIBLING, 2, 0, 3), (SEND, SIBLING, 2, 0, 3, LEFT, 2, 0, CORE), (WAIT, RIGHT, 1, 1, 1),
    (WAIT, RIGHT, 2, 1, 1), (SEND, RIGHT, 2, 1, 1, RIGHT, 1, 1, XM), (WAIT, LEFT, -1, 1, 1),
    (WAIT, SIBLING, -1, 1, 1), (SEND, SIBLING, -1, 1, 1, LEFT, -1, 1, CORE), (WAIT, RIGHT, 2, 1, 0),
    (SEND, RIGHT, 2, 1, 0, RIGHT, 2, 0, YY), (SEND, LEFT, 2, 1, 1, LEFT, -1, 1, ZP), (WAIT, LEFT, 2, 0, 2),
    (WAIT, SIBLING, 2, 0, 2), (SEND, SIBLING, 2, 0, 2, LEFT, 2, 0, CORE), (WAIT, RIGHT, 1, 1, 2),
    (WAIT, RIGHT, 2, 1, 2), (SEND, RIGHT, 2, 1, 2, RIGHT, 1, 1, XM), (WAIT, RIGHT, -1, 1, 3), (WAIT, RIGHT, 2, 1, 3),
    (SEND, RIGHT, 2, 1, 3, RIGHT, -1, 1, XP), (DO, FIRST_PAIRS), (WAIT, LEFT, 1, 1, 3), (WAIT, SIBLING, 1, 1, 3),
    (SEND, SIBLING, 1, 1, 3, LEFT, 1, 1, CORE), (WAIT, LEFT, 2, 1, 0), (WAIT, SIBLING, 2, 1, 0),
    (SEND, SIBLING, 2, 1, 0, LEFT, 2, 1, CORE), (WAIT, LEFT, -1, 1, 2), (WAIT, SIBLING, -1, 1, 2),
    (SEND, SIBLING, -1, 1, 2, LEFT, -1, 1, CORE), (WAIT, LEFT, 2, 1, 3), (WAIT, SIBLING, 2, 1, 3),
    (SEND, SIBLING, 2, 1, 3, LEFT, 2, 1, CORE), (WAIT, LEFT, 2, 1, 2), (WAIT, SIBLING, 2, 1, 2),
    (SEND, SIBLING, 2, 1, 2, LEFT, 2, 1, CORE), (WAIT, LEFT, 2, 1, 1), (WAIT, SIBLING, 2, 1, 1),
    (SEND, SIBLING, 2, 1, 1, LEFT, 2, 1, CORE), (DO, EARLY),
)

SECOND_GATHER = (
    (OWN, 0), (SEND, SQUARE, 0, 1, 1, SQUARE, 0, 0, YY), (WAIT, SQUARE, 1, 0, 0),
    (SEND, SQUARE, 1, 0, 0, SQUARE, 0, 0, XM), (SEND, SQUARE, 0, 1, 0, SQUARE, 0, 0, YY),
    (SEND, SQUARE, -1, 0, 1, SQUARE, 0, 0, XP), (SEND, SQUARE, -1, 0, 0, SQUARE, 0, 0, XP), (OWN, 1),
    (SEND, SQUARE, 1, 0, 3, SQUARE, 0, 0, XM), (WAIT, SQUARE, -1, 0, 1), (SEND, SQUARE, 0, 1, 3, SQUARE, 0, 0, YY),
    (WAIT, SQUARE, -1, 0, 3), (SEND, SQUARE, -1, 0, 3, SQUARE, 0, 0, XP), (WAIT, SQUARE, 2, 0, 1),
    (SEND, SQUARE, 2, 0, 1, SQUARE, -1, 0, XP), (WAIT, SQUARE, 1, 0, 1), (SEND, SQUARE, 1, 0, 1, SQUARE, 0, 0, XM),
    (SEND, SQUARE, 1, 0, 2, SQUARE, 0, 0, XM), (WAIT, SQUARE, 0, 1, 2), (SEND, SQUARE, 0, 1, 2, SQUARE, 0, 0, YY),
    (WAIT, SQUARE, 0, 1, 1), (WAIT, SQUARE, 1, 0, 3), (SEND, SQUARE, -1, 0, 2, SQUARE, 0, 0, XP),
    (WAIT, SQUARE, -1, 0, 0), (SEND, SQUARE, -1, 1, 0, SQUARE, -1, 0, YY), (WAIT, SQUARE, 1, 1, 1),
    (SEND, SQUARE, 1, 1, 1, SQUARE, 0, 1, XM), (WAIT, SQUARE, 0, 1, 0), (WAIT, SQUARE, 0, 1, 3),
    (WAIT, SQUARE, -1, 1, 3), (SEND, SQUARE, -1, 1, 3, SQUARE, 0, 1, XP), (WAIT, SQUARE, 2, 0, 3),
    (SEND, SQUARE, 2, 0, 3, SQUARE, 1, 0, XM), (WAIT, SQUARE, 1, 0, 2), (SEND, SQUARE, 2, 0, 2, SQUARE, 1, 0, XM),
    (WAIT, SQUARE, 1, 1, 2), (SEND, SQUARE, 1, 1, 2, SQUARE, 1, 0, YY), (SEND, SQUARE, -1, 1, 1, SQUARE, 0, 1, XP),
    (WAIT, SQUARE, -1, 0, 2), (SEND, SQUARE, 1, 1, 3, SQUARE, 0, 1, XM), (WAIT, SQUARE, -1, 1, 2),
    (SEND, SQUARE, -1, 1, 2, SQUARE, -1, 0, YY), (WAIT, SQUARE, 2, 0, 0), (SEND, SQUARE, 2, 0, 0, SQUARE, -1, 0, XP),
    (DO, NEAR_OWN), (WAIT, SQUARE, -1, 1, 0), (WAIT, SQUARE, 2, 1, 0), (SEND, SQUARE, 2, 1, 0, SQUARE, -1, 1, XP),
    (WAIT, SQUARE, 1, 1, 0), (SEND, SQUARE, 1, 1, 0, SQUARE, 0, 1, XM), (WAIT, SQUARE, -1, 1, 1),
    (WAIT, SQUARE, 2, 0, 2), (WAIT, SQUARE, 2, 1, 2), (SEND, SQUARE, 2, 1, 2, SQUARE, 2, 0, YY),
    (WAIT, SQUARE, 1, 1, 3), (WAIT, SQUARE, 2, 1, 3), (SEND, SQUARE, 2, 1, 3, SQUARE, 1, 1, XM),
    (WAIT, SQUARE, 2, 1, 1), (SEND, SQUARE, 2, 1, 1, SQUARE, -1, 1, XP), (DO, FAR_OWN), (DO, NEAR_OTHER),
    (DO, FAR_OTHER),
)


FORWARDED = {(*op[5:8], op[4]) for op in FIRST_GATHER + SECOND_GATHER if op[0] == SEND}
GROUPS = 11


def group_of(kind, d, f, q):
    if (kind, d, f, q) in FORWARDED:
        return None
    if kind == SQUARE:
        return (NEAR_OTHER if d < 2 else FAR_OTHER) if f else (NEAR_OWN if d < 2 else FAR_OWN)
    work = LATE if (d, f) == (2, 1) else EARLY if f and (d or kind == RIGHT) else FIRST_PAIRS
    return 7 + work if kind == SIBLING else work


def grow_columns(mask):
    block = lax.broadcasted_iota(jnp.int32, (PB, WP), 0)
    col = lax.broadcasted_iota(jnp.int32, (PB, WP), 1)
    spread = jnp.where((col >= block * BS) & (col < block * BS + BS), 1.0, 0.0).astype(BF16)
    return jnp.dot(mask, spread, preferred_element_type=F32).astype(BF16)


def grow(mask):
    wide = grow_columns(mask.astype(F32).astype(BF16))
    row = lax.broadcasted_iota(jnp.int32, (W, PB), 0)
    block = lax.broadcasted_iota(jnp.int32, (W, PB), 1)
    spread = jnp.where((row >= block * BS) & (row < block * BS + BS), 1.0, 0.0).astype(BF16)
    return jnp.dot(spread, wide, preferred_element_type=F32)


def whole_step(
    dens_in, pat_in, keep_in, owner_in, arrived, tails_arrived,
    dens, pat, keep, owner, left, right, sq, mask, kept, acc, update, place, hot, hot_tail, rank_at, tail_at, blocks, outgoing,
    tails, relay_in, relay_wide, relay_out, send, recv, exchange_send, exchange_recv, tail_send, tail_recv, local,
):
    r = lax.axis_index("row")
    c = lax.axis_index("col")
    x, yh = lax.rem(r, 4), lax.div(r, 4)
    z, yl, core = lax.div(c, 4), lax.rem(lax.div(c, 2), 2), lax.rem(c, 2)
    me = r * NCOL + c

    def col(dz, dyl, dcore=0):
        ycol = (1 - yl) if dyl else yl
        ccol = (1 - core) if dcore else core
        return lax.rem(z + dz + 4, 4) * 4 + ycol * 2 + ccol

    def row(dx, dyh):
        yrow = (1 - yh) if dyh else yh
        return yrow * 4 + lax.rem(x + dx + 4, 4)

    ways = {
        CORE: (r, col(0, 0, 1)),
        YA: (r, col(0, 1)),
        YB: (row(0, 1), col(0, 1)),
        YY: (row(0, 1), c),
        ZP: (r, col(1, 0)),
        ZM: (r, col(-1, 0)),
        XP: (row(1, 0), c),
        XM: (row(-1, 0), c),
    }

    fetches = [
        pltpu.make_async_copy(src, dst, local.at[k])
        for k, (src, dst) in enumerate(((pat_in, pat), (dens_in, dens), (keep_in, keep), (owner_in, owner)))
    ]
    for fetch in fetches:
        fetch.start()
    barrier = pltpu.get_barrier_semaphore()
    for dev in ways.values():
        pl.semaphore_signal(barrier, inc=1, device_id=dev, device_id_type=MESH)

    started = [0, 0]
    arriving = {}
    expected = [0] * GROUPS

    def piece(buf, slot, q):
        h, first, end = QUARTERS[q]
        return buf.at[slot, h, pl.ds(first, end - first)]

    def find(kind, d, f, q):
        if kind == LEFT:
            return piece(left, col(d, f), q)
        if kind == SIBLING:
            return piece(left, col(d, f, 1), q)
        return piece(right if kind == RIGHT else sq, row(d, f), q)

    def start(kind, d, f, q, from_kind, from_d, from_f, way):
        k = group_of(kind, d, f, q)
        if k is None:
            k = GROUPS + len(arriving)
        else:
            _, first, end = QUARTERS[q]
            expected[k] += end - first
        group = 0 if kind in (LEFT, SIBLING) else 1
        if kind == RIGHT:
            src = piece(left, c, q) if (from_d, from_f) == (0, 0) else find(from_kind, from_d, from_f, q)
            dst = piece(right, r if from_kind == LEFT else row(from_d, from_f), q)
        else:
            src = dst = find(from_kind, from_d, from_f, q)
        op = pltpu.make_async_remote_copy(
            src_ref=src, dst_ref=dst, send_sem=send.at[group], recv_sem=recv.at[k],
            device_id=ways[way], device_id_type=MESH)
        op.start()
        started[group] += QUARTERS[q][2] - QUARTERS[q][1]
        if k < GROUPS:
            return
        here = find(kind, d, f, q)
        arriving[kind, d, f, q] = pltpu.make_async_remote_copy(
            src_ref=here, dst_ref=here, send_sem=send.at[group], recv_sem=recv.at[k],
            device_id=ways[way], device_id_type=MESH)

    def join(group):
        rows = expected[group]
        if rows == 0:
            return
        all_rows = left.at[pl.ds(0, rows // (2 * W))] if rows % (2 * W) == 0 else outgoing.at[pl.ds(0, rows)]
        pltpu.make_async_remote_copy(
            src_ref=all_rows, dst_ref=all_rows, send_sem=send.at[0], recv_sem=recv.at[group],
            device_id=ways[CORE], device_id_type=MESH).wait_recv()

    def follow(table, own, work):
        for op, *what in table:
            if op == OWN:
                own(what[0])
            elif op == SEND:
                start(*what)
            elif op == WAIT:
                if group_of(*what) is None:
                    arriving[tuple(what)].wait_recv()
            else:
                join(what[0])
                work[what[0]]()

    def multiply(p, buf, h):
        if h is None:
            two = [left[2 * p + k].reshape(2 * W, WP) for k in range(2)]
            at = pl.ds(0, 2 * W)
        else:
            two = [left[2 * p + k, h] for k in range(2)]
            at = pl.ds(h * W, W)
        rows = buf[pl.ds(lax.rem(2 * p, NROW), 2), lax.div(p, 4)].reshape(2 * WP, WP)
        acc[at, :] += jnp.dot(jnp.concatenate(two, axis=1), rows, preferred_element_type=F32)

    def is_late(p):
        zp, yp = lax.div(p, 2), lax.rem(p, 2)
        in_left = (zp == lax.rem(z + 2, 4)) & (yp == 1 - yl)
        in_right = (lax.rem(zp, 2) == 1 - yh) & (yp == lax.div(lax.rem(x + 2, 4), 2))
        return in_left | in_right

    def own_density(h):
        m = grow(pat[h]).astype(BF16)
        left[c, h, :, pl.ds(256, 128)] = jnp.zeros((W, 128), BF16)
        left[c, h, :, pl.ds(0, W)] = dens[h] * m[:, :W]
        mask[h] = m
        if h == 0:
            pl.semaphore_wait(barrier, len(ways))

    def prepare():
        for h in range(2):
            right[r, h, pl.ds(0, W)] = left[c, h]
        zero = jnp.zeros((2, WP - W, WP), BF16)

        def clear(k, carry):
            right[k, :, pl.ds(W, WP - W)] = zero
            sq[k, :, pl.ds(W, WP - W)] = zero
            return carry

        lax.fori_loop(0, NROW, clear, 0)
        acc[...] = jnp.zeros_like(acc)
        fetches[2].wait()
        fetches[3].wait()
        for h in range(2):
            kept[h] = grow(keep[h]).astype(BF16)
        routing_tables(owner, place, hot, hot_tail, rank_at, tail_at)

    def is_first(p):
        zp, yp = lax.div(p, 2), lax.rem(p, 2)
        return (lax.rem(zp, 2) == yh) & ((yp == yl) | (zp == z)) & jnp.logical_not(is_late(p))

    def pairs(chosen, group):
        def add(p, carry):
            @pl.when(chosen(p))
            def _():
                multiply(p, right, None)
            return carry

        join(7 + group)
        lax.fori_loop(0, NCOL // 2, add, 0)

    fetches[0].wait()
    fetches[1].wait()
    follow(FIRST_GATHER, own_density, {
        PREPARE: prepare,
        FIRST_PAIRS: lambda: pairs(is_first, FIRST_PAIRS),
        EARLY: lambda: pairs(lambda p: jnp.logical_not(is_first(p) | is_late(p)), EARLY),
    })

    def own_square(h):
        if h == 0:
            join(LATE)
            join(7 + LATE)

        def add(p, carry):
            @pl.when(is_late(p))
            def _():
                multiply(p, right, h)
            return carry

        lax.fori_loop(0, NCOL // 2, add, 0)
        half = pl.ds(h * W, W)
        sq[r, h, pl.ds(0, W)] = (acc[half, :] / ORDER * mask[h].astype(F32)).astype(BF16)
        acc[half, :] = jnp.zeros((W, WP), F32)

    near = lax.div(x, 2)

    def second(yhp, pair):
        def add(h, carry):
            multiply((2 * h + yhp) * 2 + pair, sq, None)
            return carry

        lax.fori_loop(0, 2, add, 0)

    follow(SECOND_GATHER, own_square, {
        NEAR_OWN: lambda: second(yh, near),
        FAR_OWN: lambda: second(yh, 1 - near),
        NEAR_OTHER: lambda: second(1 - yh, near),
        FAR_OTHER: lambda: second(1 - yh, 1 - near),
    })

    for h in range(2):
        mat = left[c, h].astype(F32)
        new = kept[h].astype(F32) * (1.5 * mat - 0.5 * acc[pl.ds(h * W, W), :])
        for k in range(WP // 128):
            update[h, k] = new[:, k * 128 : k * 128 + 128]

    def rows_of(buf, device):
        return buf.at[pl.ds(pl.multiple_of(device * ROWS, ROWS), ROWS)]

    def messages(yhp, xp, first):
        at = pl.ds(pl.multiple_of((yhp * 2 + xp) * 512, 512), 512)
        outgoing[at, :] = jnp.dot(hot[at, :], blocks[...], preferred_element_type=F32).astype(BF16)

        def start_message(i, carry):
            i = lax.rem(i * 13, 32)
            dz, dyl, dcore, dx = lax.div(i, 8), lax.rem(lax.div(i, 4), 2), lax.rem(lax.div(i, 2), 2), lax.rem(i, 2)
            to_row = yhp * 4 + xp * 2 + lax.rem(x + dx, 2)
            to_col = lax.rem(z + dz, 4) * 4 + lax.rem(yl + dyl, 2) * 2 + lax.rem(core + dcore, 2)
            pltpu.make_async_remote_copy(
                src_ref=rows_of(outgoing, to_row * NCOL + to_col), dst_ref=rows_of(arrived, me),
                send_sem=exchange_send, recv_sem=exchange_recv, device_id=(to_row, to_col), device_id_type=MESH).start()
            return carry

        lax.fori_loop(first, 32, start_message, 0)

    line, in_line = r * 2 + yl, z * 2 + core

    def other_line(i):
        dyl, dyh, dx = i % 2, i // 2 % 2, i // 4
        return row(dx, dyh), yl if dyl == 0 else 1 - yl

    def line_copy(to, here, device):
        return pltpu.make_async_remote_copy(
            src_ref=to, dst_ref=here, send_sem=tail_send.at[0], recv_sem=tail_recv.at[0],
            device_id=device, device_id_type=MESH)

    def pass_on(to, here, device):
        return pltpu.make_async_remote_copy(
            src_ref=to, dst_ref=here, send_sem=tail_send.at[1], recv_sem=tail_recv.at[1],
            device_id=device, device_id_type=MESH)

    all_lines = line_copy(tails.at[pl.ds(0, (2 * NROW - 1) * ROWS)], relay_in.at[pl.ds(0, (2 * NROW - 1) * ROWS)],
                          ways[CORE])
    keep_line = pltpu.make_async_copy(rows_of(tails, line), rows_of(relay_in, line), local.at[5])

    def send_tails():
        for i in range(1, 2 * NROW):
            to_row, to_yl = other_line(i)
            line_copy(rows_of(tails, to_row * 2 + to_yl), rows_of(relay_in, line),
                      (to_row, z * 4 + to_yl * 2 + core)).start()
        keep_line.start()

    fill(update, rank_at, tail_at, place, hot_tail, blocks, tails, send_tails)

    messages(1 - yh, 1 - near, 0)
    messages(yh, 1 - near, 0)
    keep_line.wait()
    all_lines.wait_recv()
    relay_wide[...] = relay_in[...].astype(F32)
    for j in range(2 * 4):
        for k in range(2):
            part = relay_wide[pl.ds(2 * j + k, 2 * NROW, stride=ROWS), :]
            relay_out[pl.ds(j * ROWS, ROWS), pl.ds(128 * k, 128)] = part.astype(BF16)
    for i in range(1, 2 * 4):
        to_core = core if i % 2 == 0 else 1 - core
        to_z = lax.rem(z + i // 2, 4)
        pass_on(rows_of(relay_out, to_z * 2 + to_core), rows_of(tails_arrived, in_line),
                (r, to_z * 4 + yl * 2 + to_core)).start()
    all_passed = pass_on(relay_out.at[pl.ds(0, 7 * ROWS)], tails_arrived.at[pl.ds(0, 7 * ROWS)], ways[CORE])
    keep_tails = pltpu.make_async_copy(rows_of(relay_out, in_line), rows_of(tails_arrived, in_line), local.at[6])
    keep_tails.start()
    messages(1 - yh, near, 0)
    messages(yh, near, 1)
    own = pltpu.make_async_copy(rows_of(outgoing, me), rows_of(arrived, me), local.at[4])
    own.start()
    for group, rows in enumerate(started):
        sent = left.at[pl.ds(0, rows // (2 * W))]
        pltpu.make_async_remote_copy(
            src_ref=sent, dst_ref=sent, send_sem=send.at[group], recv_sem=recv.at[group],
            device_id=ways[CORE], device_id_type=MESH).wait_send()
    own.wait()
    keep_tails.wait()
    all_lines.wait_send()
    all_passed.wait_send()
    most = pl.ds(0, (DEVICES - 1) * ROWS)
    others = pltpu.make_async_remote_copy(
        src_ref=outgoing.at[most], dst_ref=arrived.at[most],
        send_sem=exchange_send, recv_sem=exchange_recv, device_id=ways[CORE], device_id_type=MESH)
    others.wait_send()
    others.wait_recv()
    all_passed.wait_recv()


N_BLOCKS = 2 * PB * PB


WINDOWS = [
    (w, i) for w in range(3) for i in range(BS) if i * BS + BS > w * 256 and i * BS < w * 256 + 256
]


def ranks(owner_row):
    owner = jnp.broadcast_to(owner_row.astype(F32), (8, N_BLOCKS))
    same = owner.T[:, :1] == owner[:1]
    one = lax.broadcasted_iota(jnp.int32, (N_BLOCKS, N_BLOCKS), 0)
    two = lax.broadcasted_iota(jnp.int32, (N_BLOCKS, N_BLOCKS), 1)
    rank = jnp.sum(jnp.where(same & (one < two), 1.0, 0.0), axis=0, keepdims=True).astype(jnp.int32)
    rank_col = jnp.sum(jnp.where(same & (two < one), 1.0, 0.0), axis=1, keepdims=True).astype(jnp.int32)
    return rank, rank_col


def routing_tables(owner, place, hot, hot_tail, rank_at, tail_at):
    lane = lax.broadcasted_iota(jnp.int32, (WP, 256), 0)
    at = lax.broadcasted_iota(jnp.int32, (WP, 256), 1)
    entry = lane - lax.div(lane, BS) * BS
    slot = lax.div(at, TAIL)
    def spread(k, carry):
        w = lax.div(k, 12)
        place[k] = jnp.where(at - entry == (k - w) * BS - w * 256, 1.0, 0.0).astype(BF16)
        return carry

    lax.fori_loop(0, 24, spread, 0)
    offset = at - slot * TAIL
    fits = (slot < 6) & (offset - entry == (BS - 1) * BS - 512) & (offset < ENT - 512)
    place[24] = jnp.where(fits, 1.0, 0.0).astype(BF16)
    rank, rank_col = ranks(owner[...])
    rank_at[...] = jnp.broadcast_to(rank_col, rank_at.shape)
    group = lax.div(lax.broadcasted_iota(jnp.int32, tail_at.shape, 1), TAIL)
    tail_at[...] = jnp.where(rank_col - lax.div(rank_col, 6) * 6 == group, 1.0, 0.0)
    own = owner[...]
    key = own * ROWS + rank
    last_key = own * ROWS + CAP + rank - lax.div(rank, 4) * 4
    to_row, to_col = lax.div(own, NCOL), lax.rem(own, NCOL)
    line = to_row * 2 + lax.rem(lax.div(to_col, 2), 2)
    in_line = lax.div(to_col, 4) * 2 + lax.rem(to_col, 2)
    tail_key = line * ROWS + in_line * 2 + lax.div(rank, 6)
    step = 256

    def compare(k, carry):
        rows = pl.ds(pl.multiple_of(k * step, step), step)
        at = lax.broadcasted_iota(jnp.int32, (step, N_BLOCKS), 0) + k * step
        hot[rows, pl.ds(0, N_BLOCKS)] = jnp.where(at == key, 1.0, 0.0).astype(BF16)
        hot[rows, pl.ds(N_BLOCKS, N_BLOCKS)] = jnp.where(at == last_key, 1.0, 0.0).astype(BF16)
        return carry

    lax.fori_loop(0, DEVICES * ROWS // step, compare, 0)
    at = lax.broadcasted_iota(jnp.int32, hot_tail.shape, 0)
    hot_tail[...] = jnp.where(at == tail_key, 1.0, 0.0).astype(BF16)


def fill(update, rank_at, tail_at, place, hot_tail, blocks, tails, send_tails):
    n = N_BLOCKS
    half = PB // 2
    picks = []
    for g in range(2):
        bc = lax.broadcasted_iota(jnp.int32, (half, 256), 0) + g * half
        entry = lax.broadcasted_iota(jnp.int32, (half, 256), 1) + g * 128
        picks.append(jnp.where((entry >= bc * BS) & (entry < bc * BS + BS), 1.0, 0.0)[None])
    for w in (2, 0, 1):
        total = [None, None]
        for k, (wk, i) in enumerate(WINDOWS):
            if wk != w:
                continue
            u = [[update[h, j, pl.ds(i, PB, stride=BS), :] for j in range(WP // 128)] for h in range(2)]
            for g in range(2):
                rows = [
                    (jnp.concatenate(u[h][g : g + 2], axis=1)[:, None, :] * picks[g]).astype(BF16)
                    .reshape(PB * half, 256)
                    for h in range(2)
                ]
                term = jnp.dot(jnp.concatenate(rows, axis=0), place[k, pl.ds(128 * g, 256), :],
                               preferred_element_type=F32)
                total[g] = term if total[g] is None else total[g] + term
        both = [t.reshape(2 * PB, 1, half, 256) for t in total]
        both = jnp.concatenate(both, axis=1).reshape(n, 256)
        if w == 2:
            tail = (both[:, :128] * tail_at[...]).astype(BF16)
            tails[...] = jnp.dot(hot_tail[...], tail, preferred_element_type=F32).astype(BF16)
            send_tails()
        elif w == 0:
            blocks[pl.ds(0, n), pl.ds(0, 256)] = both.astype(BF16)
        else:
            blocks[pl.ds(0, n), pl.ds(256, 128)] = both[:, :128].astype(BF16)
            rank = rank_at[...]
            for j in range(3):
                mine = (rank >= 4 * j) & (rank < 4 * j + 4)
                blocks[pl.ds(n, n), pl.ds(128 * j, 128)] = jnp.where(mine, both[:, 128:], 0.0).astype(BF16)


N_ARRIVALS = GROUPS + sum(
    op[0] == SEND and group_of(*op[1:5]) is None for op in FIRST_GATHER + SECOND_GATHER)


def stepped(density, pattern, keep, owner):
    anywhere = pl.BlockSpec(memory_space=pl.ANY)
    owner = owner.reshape(1, N_BLOCKS)
    return pl.pallas_call(
        whole_step,
        out_shape=(
            jax.ShapeDtypeStruct((DEVICES * ROWS, LANES), BF16),
            jax.ShapeDtypeStruct((DEVICES, 256), BF16),
        ),
        in_specs=[anywhere] * 4,
        out_specs=(anywhere, anywhere),
        scratch_shapes=[
            pltpu.VMEM(density.shape, BF16),
            pltpu.VMEM(pattern.shape, jnp.int32),
            pltpu.VMEM(keep.shape, jnp.int32),
            pltpu.VMEM(owner.shape, jnp.int32),
            pltpu.VMEM((NCOL, 2, W, WP), BF16),
            pltpu.VMEM((NROW, 2, WP, WP), BF16),
            pltpu.VMEM((NROW, 2, WP, WP), BF16),
            pltpu.VMEM((2, W, WP), BF16),
            pltpu.VMEM((2, W, WP), BF16),
            pltpu.VMEM((2 * W, WP), F32),
            pltpu.VMEM((2, WP // 128, W, 128), F32),
            pltpu.VMEM((25, WP, 256), BF16),
            pltpu.VMEM((DEVICES * ROWS, 2 * N_BLOCKS), BF16),
            pltpu.VMEM((2 * NROW * ROWS, N_BLOCKS), BF16),
            pltpu.VMEM((N_BLOCKS, 128), jnp.int32),
            pltpu.VMEM((N_BLOCKS, 128), F32),
            pltpu.VMEM((2 * N_BLOCKS, LANES), BF16),
            pltpu.VMEM((DEVICES * ROWS, LANES), BF16),
            pltpu.VMEM((2 * NROW * ROWS, 128), BF16),
            pltpu.VMEM((2 * NROW * ROWS, 128), BF16),
            pltpu.VMEM((2 * NROW * ROWS, 128), F32),
            pltpu.VMEM((DEVICES, 256), BF16),
            pltpu.SemaphoreType.DMA((2,)),
            pltpu.SemaphoreType.DMA((N_ARRIVALS,)),
            pltpu.SemaphoreType.DMA,
            pltpu.SemaphoreType.DMA,
            pltpu.SemaphoreType.DMA((2,)),
            pltpu.SemaphoreType.DMA((2,)),
            pltpu.SemaphoreType.DMA((7,)),
        ],
        compiler_params=pltpu.CompilerParams(
            collective_id=0, has_side_effects=True, vmem_limit_bytes=56 * 1024 * 1024),
        name="whole_step",
    )(density, pattern, keep, owner)


def unpack(messages, tails, out, arrived, tails_in, tails_wide, by_source, ready, sem):
    chunks = [pl.ds(128 * k, 128) for k in range(LANES // 128)]
    fetches = [
        pltpu.make_async_copy(messages.at[:, at], arrived.at[:, at], sem.at[CAP + k])
        for k, at in enumerate(chunks)
    ]
    fetch_tails = pltpu.make_async_copy(tails, tails_in, sem.at[CAP + len(chunks)])
    fetch_tails.start()
    for fetch in fetches:
        fetch.start()

    fetch_tails.wait()
    for k in range(2):
        tails_wide[k] = tails_in[:, pl.ds(128 * k, 128)].astype(F32)
        for j in range(8):
            for yl in range(2):
                source = j // 2 * 4 + yl * 2 + j % 2
                by_source[k, pl.ds(source, NROW, stride=NCOL), :] = tails_wide[k, pl.ds(j * ROWS + yl, NROW, stride=2), :]
        rows = by_source[k].T.astype(BF16)
        for s in range(6):
            ready[6 * k + s, pl.ds(512, ENT - 512), :] = rows[s * TAIL : s * TAIL + ENT - 512]
    copies = []
    for k, at in enumerate(chunks):
        fetches[k].wait()
        wide = jnp.transpose(arrived[:, at].astype(F32).reshape(DEVICES, ROWS, 128), (1, 0, 2))
        for s in range(4):
            ready[4 * k + s, pl.ds(384, 128), :] = wide[CAP + s].T.astype(BF16)
        for s in range(CAP):
            ready[s, at, :] = wide[s].T.astype(BF16)
            if k == len(chunks) - 1:
                copies.append(pltpu.make_async_copy(ready.at[s], out.at[s], sem.at[s]))
                copies[-1].start()
    for copy in copies:
        copy.wait()


def unpacked(messages, tails):
    anywhere = pl.BlockSpec(memory_space=pl.ANY)
    out = pl.pallas_call(
        unpack,
        out_shape=jax.ShapeDtypeStruct((CAP, ENT, DEVICES), BF16),
        in_specs=[anywhere] * 2,
        out_specs=anywhere,
        scratch_shapes=[
            pltpu.VMEM((DEVICES * ROWS, LANES), BF16),
            pltpu.VMEM((DEVICES, 256), BF16),
            pltpu.VMEM((2, DEVICES, 128), F32),
            pltpu.VMEM((2, DEVICES, 128), F32),
            pltpu.VMEM((CAP, ENT, DEVICES), BF16),
            pltpu.SemaphoreType.DMA((CAP + 4,)),
        ],
        compiler_params=pltpu.CompilerParams(vmem_limit_bytes=58 * 1024 * 1024),
        name="unpack",
    )(messages, tails)
    return out.transpose(2, 0, 1)[None]


def per_device(density, pattern, keep, owner):
    return unpacked(*stepped(density, pattern, keep, owner))


def solution(mesh):
    placed = (
        P(None, "row", "col"),
        P(None, "row", "col"),
        P(None, "row", "col"),
        P(("row", "col"), None, None),
    )
    return jax.shard_map(
        per_device,
        mesh=mesh,
        in_specs=placed,
        out_specs=P(("row", "col"), None, None, None),
        check_vma=False,
    )
```

```python
import jax
import jax.numpy as jnp
from jax import lax
from jax.experimental import pallas as pl
from jax.experimental.pallas import tpu as pltpu
from jax.sharding import PartitionSpec as P

BS = 23
PB = 16
W = BS * PB
WP = 384
ORDER = 5888
NROW = 8
NCOL = 16
DEVICES = NROW * NCOL
CAP = 12
ENT = BS * BS
ROWS = 16
LANES = 384
TAIL = 21
MESH = pl.DeviceIdType.MESH
F32 = jnp.float32
BF16 = jnp.bfloat16


QUARTERS = ((0, 0, 240), (0, 240, W), (1, 0, 240), (1, 240, W))

OWN, SEND, WAIT, DO = range(4)
LEFT, SIBLING, RIGHT, SQUARE = range(4)
CORE, YA, YB, YY, ZP, ZM, XP, XM = range(8)
PREPARE, FIRST_PAIRS, EARLY, LATE, NEAR_OWN, FAR_OWN, NEAR_OTHER, FAR_OTHER = range(8)
FIRST_GATHER = (
    (OWN, 0), (SEND, LEFT, 0, 1, 0, LEFT, 0, 0, YA), (SEND, LEFT, -1, 0, 0, LEFT, 0, 0, ZP), (WAIT, SIBLING, 0, 0, 0),
    (SEND, SIBLING, 0, 0, 0, LEFT, 0, 0, CORE), (SEND, LEFT, 1, 0, 1, LEFT, 0, 0, ZM),
    (SEND, RIGHT, -1, 0, 1, RIGHT, 0, 0, XP), (WAIT, RIGHT, 1, 0, 0), (SEND, RIGHT, 1, 0, 0, RIGHT, 0, 0, XM),
    (SEND, RIGHT, -1, 0, 0, RIGHT, 0, 0, XP), (SEND, LEFT, -1, 0, 1, LEFT, 0, 0, ZP),
    (SEND, LEFT, 1, 0, 0, LEFT, 0, 0, ZM), (WAIT, SIBLING, 0, 0, 1), (SEND, SIBLING, 0, 0, 1, LEFT, 0, 0, CORE),
    (OWN, 1), (SEND, LEFT, 0, 1, 1, LEFT, 0, 0, YA), (WAIT, SIBLING, 0, 0, 2),
    (SEND, SIBLING, 0, 0, 2, LEFT, 0, 0, CORE), (SEND, RIGHT, 1, 0, 3, RIGHT, 0, 0, XM), (WAIT, SIBLING, 0, 0, 3),
    (SEND, SIBLING, 0, 0, 3, LEFT, 0, 0, CORE), (DO, PREPARE), (SEND, LEFT, -1, 0, 3, LEFT, 0, 0, ZP),
    (SEND, LEFT, 0, 1, 2, LEFT, 0, 0, YA), (SEND, LEFT, 1, 0, 2, LEFT, 0, 0, ZM), (WAIT, RIGHT, 1, 0, 1),
    (SEND, RIGHT, 1, 0, 1, RIGHT, 0, 0, XM), (SEND, RIGHT, -1, 0, 2, RIGHT, 0, 0, XP), (WAIT, LEFT, 1, 0, 1),
    (WAIT, SIBLING, 1, 0, 1), (SEND, SIBLING, 1, 0, 1, LEFT, 1, 0, CORE), (SEND, LEFT, -1, 0, 2, LEFT, 0, 0, ZP),
    (WAIT, RIGHT, -1, 0, 1), (WAIT, LEFT, 0, 1, 0), (SEND, RIGHT, 0, 1, 0, LEFT, 0, 1, YB), (WAIT, SIBLING, 0, 1, 0),
    (SEND, SIBLING, 0, 1, 0, LEFT, 0, 1, CORE), (SEND, LEFT, 0, 1, 3, LEFT, 0, 0, YA), (WAIT, RIGHT, 1, 0, 2),
    (SEND, RIGHT, 1, 0, 2, RIGHT, 0, 0, XM), (WAIT, LEFT, -1, 0, 0), (WAIT, SIBLING, -1, 0, 0),
    (SEND, SIBLING, -1, 0, 0, LEFT, -1, 0, CORE), (SEND, LEFT, 1, 0, 3, LEFT, 0, 0, ZM), (WAIT, RIGHT, 2, 0, 1),
    (SEND, RIGHT, 2, 0, 1, RIGHT, -1, 0, XP), (WAIT, LEFT, 0, 1, 1), (WAIT, SIBLING, 0, 1, 1),
    (SEND, SIBLING, 0, 1, 1, LEFT, 0, 1, CORE), (SEND, RIGHT, 0, 1, 1, LEFT, 0, 1, YB), (WAIT, LEFT, -1, 0, 1),
    (SEND, LEFT, -1, 1, 0, LEFT, -1, 0, YA), (WAIT, SIBLING, -1, 0, 1), (SEND, SIBLING, -1, 0, 1, LEFT, -1, 0, CORE),
    (SEND, LEFT, 2, 0, 1, LEFT, -1, 0, ZP), (WAIT, LEFT, 1, 0, 0), (SEND, LEFT, 1, 1, 0, LEFT, 0, 1, ZM),
    (WAIT, SIBLING, 1, 0, 0), (SEND, SIBLING, 1, 0, 0, LEFT, 1, 0, CORE), (SEND, RIGHT, -1, 0, 3, RIGHT, 0, 0, XP),
    (WAIT, RIGHT, -1, 0, 0), (WAIT, RIGHT, 1, 0, 3), (WAIT, RIGHT, 2, 0, 3), (SEND, RIGHT, 2, 0, 3, RIGHT, 1, 0, XM),
    (WAIT, LEFT, -1, 0, 3), (WAIT, SIBLING, -1, 0, 3), (SEND, SIBLING, -1, 0, 3, LEFT, -1, 0, CORE),
    (WAIT, LEFT, 0, 1, 2), (SEND, LEFT, 2, 0, 0, LEFT, -1, 0, ZP), (WAIT, SIBLING, 0, 1, 2),
    (SEND, SIBLING, 0, 1, 2, LEFT, 0, 1, CORE), (SEND, RIGHT, 0, 1, 2, LEFT, 0, 1, YB),
    (SEND, LEFT, -1, 1, 3, LEFT, -1, 0, YA), (SEND, RIGHT, 2, 0, 0, RIGHT, -1, 0, XP), (WAIT, RIGHT, 0, 1, 0),
    (SEND, LEFT, 1, 1, 2, LEFT, 0, 1, ZM), (WAIT, RIGHT, 1, 1, 0), (SEND, RIGHT, 1, 1, 0, RIGHT, 0, 1, XM),
    (WAIT, LEFT, 1, 0, 2), (WAIT, SIBLING, 1, 0, 2), (SEND, SIBLING, 1, 0, 2, LEFT, 1, 0, CORE),
    (WAIT, RIGHT, -1, 0, 2), (WAIT, LEFT, 0, 1, 3), (WAIT, SIBLING, 0, 1, 3),
    (SEND, SIBLING, 0, 1, 3, LEFT, 0, 1, CORE), (SEND, RIGHT, 0, 1, 3, LEFT, 0, 1, YB), (WAIT, LEFT, -1, 0, 2),
    (SEND, LEFT, 1, 1, 1, LEFT, 1, 0, YA), (WAIT, SIBLING, -1, 0, 2), (SEND, SIBLING, -1, 0, 2, LEFT, -1, 0, CORE),
    (SEND, LEFT, 2, 0, 3, LEFT, -1, 0, ZP), (WAIT, RIGHT, 0, 1, 1), (WAIT, RIGHT, 2, 0, 2),
    (SEND, RIGHT, 2, 0, 2, RIGHT, -1, 0, XP), (WAIT, LEFT, 1, 0, 3), (SEND, RIGHT, 1, 1, 1, RIGHT, 0, 1, XM),
    (WAIT, SIBLING, 1, 0, 3), (SEND, SIBLING, 1, 0, 3, LEFT, 1, 0, CORE), (WAIT, LEFT, 2, 0, 1),
    (WAIT, SIBLING, 2, 0, 1), (SEND, SIBLING, 2, 0, 1, LEFT, 2, 0, CORE), (WAIT, RIGHT, -1, 1, 1),
    (SEND, RIGHT, -1, 1, 1, RIGHT, -1, 0, YY), (SEND, LEFT, 2, 0, 2, LEFT, 1, 0, ZM), (WAIT, RIGHT, -1, 0, 3),
    (SEND, LEFT, -1, 1, 1, LEFT, 0, 1, ZP), (WAIT, LEFT, -1, 1, 0), (WAIT, SIBLING, -1, 1, 0),
    (SEND, SIBLING, -1, 1, 0, LEFT, -1, 1, CORE), (WAIT, LEFT, 1, 1, 0), (WAIT, SIBLING, 1, 1, 0),
    (SEND, SIBLING, 1, 1, 0, LEFT, 1, 1, CORE), (WAIT, RIGHT, 0, 1, 2), (SEND, RIGHT, -1, 1, 3, RIGHT, -1, 0, YY),
    (SEND, LEFT, 2, 1, 0, LEFT, -1, 1, ZP), (SEND, RIGHT, 1, 1, 2, RIGHT, 0, 1, XM), (WAIT, LEFT, -1, 1, 3),
    (WAIT, SIBLING, -1, 1, 3), (SEND, SIBLING, -1, 1, 3, LEFT, -1, 1, CORE), (WAIT, RIGHT, -1, 1, 2),
    (SEND, RIGHT, -1, 1, 2, RIGHT, 0, 1, XP), (WAIT, LEFT, 2, 0, 0), (WAIT, SIBLING, 2, 0, 0),
    (SEND, SIBLING, 2, 0, 0, LEFT, 2, 0, CORE), (SEND, LEFT, 1, 1, 3, LEFT, 0, 1, ZM),
    (SEND, LEFT, -1, 1, 2, LEFT, -1, 0, YA), (WAIT, RIGHT, 2, 0, 0), (WAIT, RIGHT, 0, 1, 3), (WAIT, RIGHT, 1, 1, 3),
    (SEND, RIGHT, 1, 1, 3, RIGHT, 0, 1, XM), (WAIT, LEFT, 1, 1, 1), (WAIT, SIBLING, 1, 1, 1),
    (SEND, SIBLING, 1, 1, 1, LEFT, 1, 1, CORE), (WAIT, LEFT, 1, 1, 2), (WAIT, SIBLING, 1, 1, 2),
    (SEND, SIBLING, 1, 1, 2, LEFT, 1, 1, CORE), (WAIT, LEFT, 2, 0, 3), (SEND, LEFT, 2, 1, 2, LEFT, 1, 1, ZM),
    (SEND, LEFT, 2, 1, 3, LEFT, -1, 1, ZP), (WAIT, RIGHT, -1, 1, 0), (SEND, RIGHT, -1, 1, 0, RIGHT, 0, 1, XP),
    (WAIT, SIBLING, 2, 0, 3), (SEND, SIBLING, 2, 0, 3, LEFT, 2, 0, CORE), (WAIT, RIGHT, 1, 1, 1),
    (WAIT, RIGHT, 2, 1, 1), (SEND, RIGHT, 2, 1, 1, RIGHT, 1, 1, XM), (WAIT, LEFT, -1, 1, 1),
    (WAIT, SIBLING, -1, 1, 1), (SEND, SIBLING, -1, 1, 1, LEFT, -1, 1, CORE), (WAIT, RIGHT, 2, 1, 0),
    (SEND, RIGHT, 2, 1, 0, RIGHT, 2, 0, YY), (SEND, LEFT, 2, 1, 1, LEFT, -1, 1, ZP), (WAIT, LEFT, 2, 0, 2),
    (WAIT, SIBLING, 2, 0, 2), (SEND, SIBLING, 2, 0, 2, LEFT, 2, 0, CORE), (WAIT, RIGHT, 1, 1, 2),
    (WAIT, RIGHT, 2, 1, 2), (SEND, RIGHT, 2, 1, 2, RIGHT, 1, 1, XM), (WAIT, RIGHT, -1, 1, 3), (WAIT, RIGHT, 2, 1, 3),
    (SEND, RIGHT, 2, 1, 3, RIGHT, -1, 1, XP), (DO, FIRST_PAIRS), (WAIT, LEFT, 1, 1, 3), (WAIT, SIBLING, 1, 1, 3),
    (SEND, SIBLING, 1, 1, 3, LEFT, 1, 1, CORE), (WAIT, LEFT, 2, 1, 0), (WAIT, SIBLING, 2, 1, 0),
    (SEND, SIBLING, 2, 1, 0, LEFT, 2, 1, CORE), (WAIT, LEFT, -1, 1, 2), (WAIT, SIBLING, -1, 1, 2),
    (SEND, SIBLING, -1, 1, 2, LEFT, -1, 1, CORE), (WAIT, LEFT, 2, 1, 3), (WAIT, SIBLING, 2, 1, 3),
    (SEND, SIBLING, 2, 1, 3, LEFT, 2, 1, CORE), (WAIT, LEFT, 2, 1, 2), (WAIT, SIBLING, 2, 1, 2),
    (SEND, SIBLING, 2, 1, 2, LEFT, 2, 1, CORE), (WAIT, LEFT, 2, 1, 1), (WAIT, SIBLING, 2, 1, 1),
    (SEND, SIBLING, 2, 1, 1, LEFT, 2, 1, CORE), (DO, EARLY),
)

SECOND_GATHER = (
    (OWN, 0), (SEND, SQUARE, 0, 1, 1, SQUARE, 0, 0, YY), (WAIT, SQUARE, 1, 0, 0),
    (SEND, SQUARE, 1, 0, 0, SQUARE, 0, 0, XM), (SEND, SQUARE, 0, 1, 0, SQUARE, 0, 0, YY),
    (SEND, SQUARE, -1, 0, 1, SQUARE, 0, 0, XP), (SEND, SQUARE, -1, 0, 0, SQUARE, 0, 0, XP), (OWN, 1),
    (SEND, SQUARE, 1, 0, 3, SQUARE, 0, 0, XM), (WAIT, SQUARE, -1, 0, 1), (SEND, SQUARE, 0, 1, 3, SQUARE, 0, 0, YY),
    (WAIT, SQUARE, -1, 0, 3), (SEND, SQUARE, -1, 0, 3, SQUARE, 0, 0, XP), (WAIT, SQUARE, 2, 0, 1),
    (SEND, SQUARE, 2, 0, 1, SQUARE, -1, 0, XP), (WAIT, SQUARE, 1, 0, 1), (SEND, SQUARE, 1, 0, 1, SQUARE, 0, 0, XM),
    (SEND, SQUARE, 1, 0, 2, SQUARE, 0, 0, XM), (WAIT, SQUARE, 0, 1, 2), (SEND, SQUARE, 0, 1, 2, SQUARE, 0, 0, YY),
    (WAIT, SQUARE, 0, 1, 1), (WAIT, SQUARE, 1, 0, 3), (SEND, SQUARE, -1, 0, 2, SQUARE, 0, 0, XP),
    (WAIT, SQUARE, -1, 0, 0), (SEND, SQUARE, -1, 1, 0, SQUARE, -1, 0, YY), (WAIT, SQUARE, 1, 1, 1),
    (SEND, SQUARE, 1, 1, 1, SQUARE, 0, 1, XM), (WAIT, SQUARE, 0, 1, 0), (WAIT, SQUARE, 0, 1, 3),
    (WAIT, SQUARE, -1, 1, 3), (SEND, SQUARE, -1, 1, 3, SQUARE, 0, 1, XP), (WAIT, SQUARE, 2, 0, 3),
    (SEND, SQUARE, 2, 0, 3, SQUARE, 1, 0, XM), (WAIT, SQUARE, 1, 0, 2), (SEND, SQUARE, 2, 0, 2, SQUARE, 1, 0, XM),
    (WAIT, SQUARE, 1, 1, 2), (SEND, SQUARE, 1, 1, 2, SQUARE, 1, 0, YY), (SEND, SQUARE, -1, 1, 1, SQUARE, 0, 1, XP),
    (WAIT, SQUARE, -1, 0, 2), (SEND, SQUARE, 1, 1, 3, SQUARE, 0, 1, XM), (WAIT, SQUARE, -1, 1, 2),
    (SEND, SQUARE, -1, 1, 2, SQUARE, -1, 0, YY), (WAIT, SQUARE, 2, 0, 0), (SEND, SQUARE, 2, 0, 0, SQUARE, -1, 0, XP),
    (DO, NEAR_OWN), (WAIT, SQUARE, -1, 1, 0), (WAIT, SQUARE, 2, 1, 0), (SEND, SQUARE, 2, 1, 0, SQUARE, -1, 1, XP),
    (WAIT, SQUARE, 1, 1, 0), (SEND, SQUARE, 1, 1, 0, SQUARE, 0, 1, XM), (WAIT, SQUARE, -1, 1, 1),
    (WAIT, SQUARE, 2, 0, 2), (WAIT, SQUARE, 2, 1, 2), (SEND, SQUARE, 2, 1, 2, SQUARE, 2, 0, YY),
    (WAIT, SQUARE, 1, 1, 3), (WAIT, SQUARE, 2, 1, 3), (SEND, SQUARE, 2, 1, 3, SQUARE, 1, 1, XM),
    (WAIT, SQUARE, 2, 1, 1), (SEND, SQUARE, 2, 1, 1, SQUARE, -1, 1, XP), (DO, FAR_OWN), (DO, NEAR_OTHER),
    (DO, FAR_OTHER),
)


FORWARDED = {(*op[5:8], op[4]) for op in FIRST_GATHER + SECOND_GATHER if op[0] == SEND}
GROUPS = 11


def group_of(kind, d, f, q):
    if (kind, d, f, q) in FORWARDED:
        return None
    if kind == SQUARE:
        return (NEAR_OTHER if d < 2 else FAR_OTHER) if f else (NEAR_OWN if d < 2 else FAR_OWN)
    work = LATE if (d, f) == (2, 1) else EARLY if f and (d or kind == RIGHT) else FIRST_PAIRS
    return 7 + work if kind == SIBLING else work


def grow_columns(mask):
    block = lax.broadcasted_iota(jnp.int32, (PB, WP), 0)
    col = lax.broadcasted_iota(jnp.int32, (PB, WP), 1)
    spread = jnp.where((col >= block * BS) & (col < block * BS + BS), 1.0, 0.0).astype(BF16)
    return jnp.dot(mask, spread, preferred_element_type=F32).astype(BF16)


def grow(mask):
    wide = grow_columns(mask.astype(F32).astype(BF16))
    row = lax.broadcasted_iota(jnp.int32, (W, PB), 0)
    block = lax.broadcasted_iota(jnp.int32, (W, PB), 1)
    spread = jnp.where((row >= block * BS) & (row < block * BS + BS), 1.0, 0.0).astype(BF16)
    return jnp.dot(spread, wide, preferred_element_type=F32)


def whole_step(
    dens_in, pat_in, keep_in, owner_in, arrived, tails_arrived,
    dens, pat, keep, owner, left, right, sq, mask, kept, acc, update, place, hot, hot_tail, rank_at, tail_at, blocks, outgoing,
    tails, relay_in, relay_wide, relay_out, send, recv, exchange_send, exchange_recv, tail_send, tail_recv, local,
):
    r = lax.axis_index("row")
    c = lax.axis_index("col")
    x, yh = lax.rem(r, 4), lax.div(r, 4)
    z, yl, core = lax.div(c, 4), lax.rem(lax.div(c, 2), 2), lax.rem(c, 2)
    me = r * NCOL + c

    def col(dz, dyl, dcore=0):
        ycol = (1 - yl) if dyl else yl
        ccol = (1 - core) if dcore else core
        return lax.rem(z + dz + 4, 4) * 4 + ycol * 2 + ccol

    def row(dx, dyh):
        yrow = (1 - yh) if dyh else yh
        return yrow * 4 + lax.rem(x + dx + 4, 4)

    ways = {
        CORE: (r, col(0, 0, 1)),
        YA: (r, col(0, 1)),
        YB: (row(0, 1), col(0, 1)),
        YY: (row(0, 1), c),
        ZP: (r, col(1, 0)),
        ZM: (r, col(-1, 0)),
        XP: (row(1, 0), c),
        XM: (row(-1, 0), c),
    }

    fetches = [
        pltpu.make_async_copy(src, dst, local.at[k])
        for k, (src, dst) in enumerate(((pat_in, pat), (dens_in, dens), (keep_in, keep), (owner_in, owner)))
    ]
    for fetch in fetches:
        fetch.start()
    barrier = pltpu.get_barrier_semaphore()
    for dev in ways.values():
        pl.semaphore_signal(barrier, inc=1, device_id=dev, device_id_type=MESH)

    started = [0, 0]
    arriving = {}
    expected = [0] * GROUPS

    def piece(buf, slot, q):
        h, first, end = QUARTERS[q]
        return buf.at[slot, h, pl.ds(first, end - first)]

    def find(kind, d, f, q):
        if kind == LEFT:
            return piece(left, col(d, f), q)
        if kind == SIBLING:
            return piece(left, col(d, f, 1), q)
        return piece(right if kind == RIGHT else sq, row(d, f), q)

    def start(kind, d, f, q, from_kind, from_d, from_f, way):
        k = group_of(kind, d, f, q)
        if k is None:
            k = GROUPS + len(arriving)
        else:
            _, first, end = QUARTERS[q]
            expected[k] += end - first
        group = 0 if kind in (LEFT, SIBLING) else 1
        if kind == RIGHT:
            src = piece(left, c, q) if (from_d, from_f) == (0, 0) else find(from_kind, from_d, from_f, q)
            dst = piece(right, r if from_kind == LEFT else row(from_d, from_f), q)
        else:
            src = dst = find(from_kind, from_d, from_f, q)
        op = pltpu.make_async_remote_copy(
            src_ref=src, dst_ref=dst, send_sem=send.at[group], recv_sem=recv.at[k],
            device_id=ways[way], device_id_type=MESH)
        op.start()
        started[group] += QUARTERS[q][2] - QUARTERS[q][1]
        if k < GROUPS:
            return
        here = find(kind, d, f, q)
        arriving[kind, d, f, q] = pltpu.make_async_remote_copy(
            src_ref=here, dst_ref=here, send_sem=send.at[group], recv_sem=recv.at[k],
            device_id=ways[way], device_id_type=MESH)

    def join(group):
        rows = expected[group]
        if rows == 0:
            return
        all_rows = left.at[pl.ds(0, rows // (2 * W))] if rows % (2 * W) == 0 else outgoing.at[pl.ds(0, rows)]
        pltpu.make_async_remote_copy(
            src_ref=all_rows, dst_ref=all_rows, send_sem=send.at[0], recv_sem=recv.at[group],
            device_id=ways[CORE], device_id_type=MESH).wait_recv()

    def follow(table, own, work):
        for op, *what in table:
            if op == OWN:
                own(what[0])
            elif op == SEND:
                start(*what)
            elif op == WAIT:
                if group_of(*what) is None:
                    arriving[tuple(what)].wait_recv()
            else:
                join(what[0])
                work[what[0]]()

    def multiply(p, buf, h):
        if h is None:
            two = [left[2 * p + k].reshape(2 * W, WP) for k in range(2)]
            at = pl.ds(0, 2 * W)
        else:
            two = [left[2 * p + k, h] for k in range(2)]
            at = pl.ds(h * W, W)
        rows = buf[pl.ds(lax.rem(2 * p, NROW), 2), lax.div(p, 4)].reshape(2 * WP, WP)
        acc[at, :] += jnp.dot(jnp.concatenate(two, axis=1), rows, preferred_element_type=F32)

    def is_last_left(p):
        return (lax.div(p, 2) == lax.rem(z + 2, 4)) & (lax.rem(p, 2) == 1 - yl)

    def is_late(p):
        zp, yp = lax.div(p, 2), lax.rem(p, 2)
        in_left = is_last_left(p)
        in_right = (lax.rem(zp, 2) == 1 - yh) & (yp == lax.div(lax.rem(x + 2, 4), 2))
        return in_left | in_right

    def own_density(h):
        m = grow(pat[h]).astype(BF16)
        left[c, h, :, pl.ds(256, 128)] = jnp.zeros((W, 128), BF16)
        left[c, h, :, pl.ds(0, W)] = dens[h] * m[:, :W]
        mask[h] = m
        if h == 0:
            pl.semaphore_wait(barrier, len(ways))

    def prepare():
        for h in range(2):
            right[r, h, pl.ds(0, W)] = left[c, h]
        zero = jnp.zeros((2, WP - W, WP), BF16)

        def clear(k, carry):
            right[k, :, pl.ds(W, WP - W)] = zero
            sq[k, :, pl.ds(W, WP - W)] = zero
            return carry

        lax.fori_loop(0, NROW, clear, 0)
        acc[...] = jnp.zeros_like(acc)
        fetches[2].wait()
        fetches[3].wait()
        for h in range(2):
            kept[h] = grow(keep[h]).astype(BF16)
        routing_tables(owner, place, hot, hot_tail, rank_at, tail_at)

    def is_first(p):
        zp, yp = lax.div(p, 2), lax.rem(p, 2)
        return (lax.rem(zp, 2) == yh) & ((yp == yl) | (zp == z)) & jnp.logical_not(is_late(p))

    def pairs(chosen, group):
        def add(p, carry):
            @pl.when(chosen(p))
            def _():
                multiply(p, right, None)
            return carry

        join(7 + group)
        lax.fori_loop(0, NCOL // 2, add, 0)

    fetches[0].wait()
    fetches[1].wait()
    follow(FIRST_GATHER, own_density, {
        PREPARE: prepare,
        FIRST_PAIRS: lambda: pairs(is_first, FIRST_PAIRS),
        EARLY: lambda: pairs(lambda p: jnp.logical_not(is_first(p) | is_late(p)), EARLY),
    })

    def own_square(h):
        def add(p, carry):
            @pl.when(is_late(p) & jnp.logical_not(is_last_left(p)))
            def _():
                multiply(p, right, h)
            return carry

        if h == 0:
            join(LATE)
        lax.fori_loop(0, NCOL // 2, add, 0)
        if h == 0:
            join(7 + LATE)
        multiply(lax.rem(z + 2, 4) * 2 + 1 - yl, right, h)
        half = pl.ds(h * W, W)
        sq[r, h, pl.ds(0, W)] = (acc[half, :] / ORDER * mask[h].astype(F32)).astype(BF16)
        acc[half, :] = jnp.zeros((W, WP), F32)

    near = lax.div(x, 2)

    def second(yhp, pair):
        def add(h, carry):
            multiply((2 * h + yhp) * 2 + pair, sq, None)
            return carry

        lax.fori_loop(0, 2, add, 0)

    follow(SECOND_GATHER, own_square, {
        NEAR_OWN: lambda: second(yh, near),
        FAR_OWN: lambda: second(yh, 1 - near),
        NEAR_OTHER: lambda: second(1 - yh, near),
        FAR_OTHER: lambda: second(1 - yh, 1 - near),
    })

    for h in range(2):
        mat = left[c, h].astype(F32)
        new = kept[h].astype(F32) * (1.5 * mat - 0.5 * acc[pl.ds(h * W, W), :])
        for k in range(WP // 128):
            update[h, k] = new[:, k * 128 : k * 128 + 128]

    def rows_of(buf, device):
        return buf.at[pl.ds(pl.multiple_of(device * ROWS, ROWS), ROWS)]

    def messages(yhp, xp, first):
        at = pl.ds(pl.multiple_of((yhp * 2 + xp) * 512, 512), 512)
        outgoing[at, :] = jnp.dot(hot[at, :], blocks[...], preferred_element_type=F32).astype(BF16)

        def start_message(i, carry):
            i = lax.rem(i * 13, 32)
            dz, dyl, dcore, dx = lax.div(i, 8), lax.rem(lax.div(i, 4), 2), lax.rem(lax.div(i, 2), 2), lax.rem(i, 2)
            to_row = yhp * 4 + xp * 2 + lax.rem(x + dx, 2)
            to_col = lax.rem(z + dz, 4) * 4 + lax.rem(yl + dyl, 2) * 2 + lax.rem(core + dcore, 2)
            pltpu.make_async_remote_copy(
                src_ref=rows_of(outgoing, to_row * NCOL + to_col), dst_ref=rows_of(arrived, me),
                send_sem=exchange_send, recv_sem=exchange_recv, device_id=(to_row, to_col), device_id_type=MESH).start()
            return carry

        lax.fori_loop(first, 32, start_message, 0)

    line, in_line = r * 2 + yl, z * 2 + core

    def other_line(i):
        dyl, dyh, dx = i % 2, i // 2 % 2, i // 4
        return row(dx, dyh), yl if dyl == 0 else 1 - yl

    def line_copy(to, here, device):
        return pltpu.make_async_remote_copy(
            src_ref=to, dst_ref=here, send_sem=tail_send.at[0], recv_sem=tail_recv.at[0],
            device_id=device, device_id_type=MESH)

    def pass_on(to, here, device):
        return pltpu.make_async_remote_copy(
            src_ref=to, dst_ref=here, send_sem=tail_send.at[1], recv_sem=tail_recv.at[1],
            device_id=device, device_id_type=MESH)

    all_lines = line_copy(tails.at[pl.ds(0, (2 * NROW - 1) * ROWS)], relay_in.at[pl.ds(0, (2 * NROW - 1) * ROWS)],
                          ways[CORE])
    keep_line = pltpu.make_async_copy(rows_of(tails, line), rows_of(relay_in, line), local.at[5])

    def send_tails():
        for i in range(1, 2 * NROW):
            to_row, to_yl = other_line(i)
            line_copy(rows_of(tails, to_row * 2 + to_yl), rows_of(relay_in, line),
                      (to_row, z * 4 + to_yl * 2 + core)).start()
        keep_line.start()

    fill(update, rank_at, tail_at, place, hot_tail, blocks, tails, send_tails)

    messages(1 - yh, 1 - near, 0)
    messages(yh, 1 - near, 0)
    keep_line.wait()
    all_lines.wait_recv()
    relay_wide[...] = relay_in[...].astype(F32)
    for j in range(2 * 4):
        for k in range(2):
            part = relay_wide[pl.ds(2 * j + k, 2 * NROW, stride=ROWS), :]
            relay_out[pl.ds(j * ROWS, ROWS), pl.ds(128 * k, 128)] = part.astype(BF16)
    for i in range(1, 2 * 4):
        to_core = core if i % 2 == 0 else 1 - core
        to_z = lax.rem(z + i // 2, 4)
        pass_on(rows_of(relay_out, to_z * 2 + to_core), rows_of(tails_arrived, in_line),
                (r, to_z * 4 + yl * 2 + to_core)).start()
    all_passed = pass_on(relay_out.at[pl.ds(0, 7 * ROWS)], tails_arrived.at[pl.ds(0, 7 * ROWS)], ways[CORE])
    keep_tails = pltpu.make_async_copy(rows_of(relay_out, in_line), rows_of(tails_arrived, in_line), local.at[6])
    keep_tails.start()
    messages(1 - yh, near, 0)
    messages(yh, near, 1)
    own = pltpu.make_async_copy(rows_of(outgoing, me), rows_of(arrived, me), local.at[4])
    own.start()
    for group, rows in enumerate(started):
        sent = left.at[pl.ds(0, rows // (2 * W))]
        pltpu.make_async_remote_copy(
            src_ref=sent, dst_ref=sent, send_sem=send.at[group], recv_sem=recv.at[group],
            device_id=ways[CORE], device_id_type=MESH).wait_send()
    own.wait()
    keep_tails.wait()
    all_lines.wait_send()
    all_passed.wait_send()
    most = pl.ds(0, (DEVICES - 1) * ROWS)
    others = pltpu.make_async_remote_copy(
        src_ref=outgoing.at[most], dst_ref=arrived.at[most],
        send_sem=exchange_send, recv_sem=exchange_recv, device_id=ways[CORE], device_id_type=MESH)
    others.wait_send()
    others.wait_recv()
    all_passed.wait_recv()


N_BLOCKS = 2 * PB * PB


WINDOWS = [
    (w, i) for w in range(3) for i in range(BS) if i * BS + BS > w * 256 and i * BS < w * 256 + 256
]


def ranks(owner_row):
    owner = jnp.broadcast_to(owner_row.astype(F32), (8, N_BLOCKS))
    same = owner.T[:, :1] == owner[:1]
    one = lax.broadcasted_iota(jnp.int32, (N_BLOCKS, N_BLOCKS), 0)
    two = lax.broadcasted_iota(jnp.int32, (N_BLOCKS, N_BLOCKS), 1)
    rank = jnp.sum(jnp.where(same & (one < two), 1.0, 0.0), axis=0, keepdims=True).astype(jnp.int32)
    rank_col = jnp.sum(jnp.where(same & (two < one), 1.0, 0.0), axis=1, keepdims=True).astype(jnp.int32)
    return rank, rank_col


def routing_tables(owner, place, hot, hot_tail, rank_at, tail_at):
    lane = lax.broadcasted_iota(jnp.int32, (WP, 256), 0)
    at = lax.broadcasted_iota(jnp.int32, (WP, 256), 1)
    entry = lane - lax.div(lane, BS) * BS
    slot = lax.div(at, TAIL)
    def spread(k, carry):
        w = lax.div(k, 12)
        place[k] = jnp.where(at - entry == (k - w) * BS - w * 256, 1.0, 0.0).astype(BF16)
        return carry

    lax.fori_loop(0, 24, spread, 0)
    offset = at - slot * TAIL
    fits = (slot < 6) & (offset - entry == (BS - 1) * BS - 512) & (offset < ENT - 512)
    place[24] = jnp.where(fits, 1.0, 0.0).astype(BF16)
    rank, rank_col = ranks(owner[...])
    rank_at[...] = jnp.broadcast_to(rank_col, rank_at.shape)
    group = lax.div(lax.broadcasted_iota(jnp.int32, tail_at.shape, 1), TAIL)
    tail_at[...] = jnp.where(rank_col - lax.div(rank_col, 6) * 6 == group, 1.0, 0.0)
    own = owner[...]
    key = own * ROWS + rank
    last_key = own * ROWS + CAP + rank - lax.div(rank, 4) * 4
    to_row, to_col = lax.div(own, NCOL), lax.rem(own, NCOL)
    line = to_row * 2 + lax.rem(lax.div(to_col, 2), 2)
    in_line = lax.div(to_col, 4) * 2 + lax.rem(to_col, 2)
    tail_key = line * ROWS + in_line * 2 + lax.div(rank, 6)
    step = 256

    def compare(k, carry):
        rows = pl.ds(pl.multiple_of(k * step, step), step)
        at = lax.broadcasted_iota(jnp.int32, (step, N_BLOCKS), 0) + k * step
        hot[rows, pl.ds(0, N_BLOCKS)] = jnp.where(at == key, 1.0, 0.0).astype(BF16)
        hot[rows, pl.ds(N_BLOCKS, N_BLOCKS)] = jnp.where(at == last_key, 1.0, 0.0).astype(BF16)
        return carry

    lax.fori_loop(0, DEVICES * ROWS // step, compare, 0)
    at = lax.broadcasted_iota(jnp.int32, hot_tail.shape, 0)
    hot_tail[...] = jnp.where(at == tail_key, 1.0, 0.0).astype(BF16)


def fill(update, rank_at, tail_at, place, hot_tail, blocks, tails, send_tails):
    n = N_BLOCKS
    half = PB // 2
    picks = []
    for g in range(2):
        bc = lax.broadcasted_iota(jnp.int32, (half, 256), 0) + g * half
        entry = lax.broadcasted_iota(jnp.int32, (half, 256), 1) + g * 128
        picks.append(jnp.where((entry >= bc * BS) & (entry < bc * BS + BS), 1.0, 0.0)[None])
    for w in (2, 0, 1):
        total = [None, None]
        for k, (wk, i) in enumerate(WINDOWS):
            if wk != w:
                continue
            u = [[update[h, j, pl.ds(i, PB, stride=BS), :] for j in range(WP // 128)] for h in range(2)]
            for g in range(2):
                rows = [
                    (jnp.concatenate(u[h][g : g + 2], axis=1)[:, None, :] * picks[g]).astype(BF16)
                    .reshape(PB * half, 256)
                    for h in range(2)
                ]
                term = jnp.dot(jnp.concatenate(rows, axis=0), place[k, pl.ds(128 * g, 256), :],
                               preferred_element_type=F32)
                total[g] = term if total[g] is None else total[g] + term
        both = [t.reshape(2 * PB, 1, half, 256) for t in total]
        both = jnp.concatenate(both, axis=1).reshape(n, 256)
        if w == 2:
            tail = (both[:, :128] * tail_at[...]).astype(BF16)
            tails[...] = jnp.dot(hot_tail[...], tail, preferred_element_type=F32).astype(BF16)
            send_tails()
        elif w == 0:
            blocks[pl.ds(0, n), pl.ds(0, 256)] = both.astype(BF16)
        else:
            blocks[pl.ds(0, n), pl.ds(256, 128)] = both[:, :128].astype(BF16)
            rank = rank_at[...]
            for j in range(3):
                mine = (rank >= 4 * j) & (rank < 4 * j + 4)
                blocks[pl.ds(n, n), pl.ds(128 * j, 128)] = jnp.where(mine, both[:, 128:], 0.0).astype(BF16)


N_ARRIVALS = GROUPS + sum(
    op[0] == SEND and group_of(*op[1:5]) is None for op in FIRST_GATHER + SECOND_GATHER)


def stepped(density, pattern, keep, owner):
    anywhere = pl.BlockSpec(memory_space=pl.ANY)
    owner = owner.reshape(1, N_BLOCKS)
    return pl.pallas_call(
        whole_step,
        out_shape=(
            jax.ShapeDtypeStruct((DEVICES * ROWS, LANES), BF16),
            jax.ShapeDtypeStruct((DEVICES, 256), BF16),
        ),
        in_specs=[anywhere] * 4,
        out_specs=(anywhere, anywhere),
        scratch_shapes=[
            pltpu.VMEM(density.shape, BF16),
            pltpu.VMEM(pattern.shape, jnp.int32),
            pltpu.VMEM(keep.shape, jnp.int32),
            pltpu.VMEM(owner.shape, jnp.int32),
            pltpu.VMEM((NCOL, 2, W, WP), BF16),
            pltpu.VMEM((NROW, 2, WP, WP), BF16),
            pltpu.VMEM((NROW, 2, WP, WP), BF16),
            pltpu.VMEM((2, W, WP), BF16),
            pltpu.VMEM((2, W, WP), BF16),
            pltpu.VMEM((2 * W, WP), F32),
            pltpu.VMEM((2, WP // 128, W, 128), F32),
            pltpu.VMEM((25, WP, 256), BF16),
            pltpu.VMEM((DEVICES * ROWS, 2 * N_BLOCKS), BF16),
            pltpu.VMEM((2 * NROW * ROWS, N_BLOCKS), BF16),
            pltpu.VMEM((N_BLOCKS, 128), jnp.int32),
            pltpu.VMEM((N_BLOCKS, 128), F32),
            pltpu.VMEM((2 * N_BLOCKS, LANES), BF16),
            pltpu.VMEM((DEVICES * ROWS, LANES), BF16),
            pltpu.VMEM((2 * NROW * ROWS, 128), BF16),
            pltpu.VMEM((2 * NROW * ROWS, 128), BF16),
            pltpu.VMEM((2 * NROW * ROWS, 128), F32),
            pltpu.VMEM((DEVICES, 256), BF16),
            pltpu.SemaphoreType.DMA((2,)),
            pltpu.SemaphoreType.DMA((N_ARRIVALS,)),
            pltpu.SemaphoreType.DMA,
            pltpu.SemaphoreType.DMA,
            pltpu.SemaphoreType.DMA((2,)),
            pltpu.SemaphoreType.DMA((2,)),
            pltpu.SemaphoreType.DMA((7,)),
        ],
        compiler_params=pltpu.CompilerParams(
            collective_id=0, has_side_effects=True, vmem_limit_bytes=56 * 1024 * 1024),
        name="whole_step",
    )(density, pattern, keep, owner)


def unpack(messages, tails, out, arrived, tails_in, tails_wide, by_source, ready, sem):
    chunks = [pl.ds(128 * k, 128) for k in range(LANES // 128)]
    fetches = [
        pltpu.make_async_copy(messages.at[:, at], arrived.at[:, at], sem.at[CAP + k])
        for k, at in enumerate(chunks)
    ]
    fetch_tails = pltpu.make_async_copy(tails, tails_in, sem.at[CAP + len(chunks)])
    fetch_tails.start()
    for fetch in fetches:
        fetch.start()

    fetch_tails.wait()
    for k in range(2):
        tails_wide[k] = tails_in[:, pl.ds(128 * k, 128)].astype(F32)
        for j in range(8):
            for yl in range(2):
                source = j // 2 * 4 + yl * 2 + j % 2
                by_source[k, pl.ds(source, NROW, stride=NCOL), :] = tails_wide[k, pl.ds(j * ROWS + yl, NROW, stride=2), :]
        rows = by_source[k].T.astype(BF16)
        for s in range(6):
            ready[6 * k + s, pl.ds(512, ENT - 512), :] = rows[s * TAIL : s * TAIL + ENT - 512]
    copies = []
    for k, at in enumerate(chunks):
        fetches[k].wait()
        wide = jnp.transpose(arrived[:, at].astype(F32).reshape(DEVICES, ROWS, 128), (1, 0, 2))
        for s in range(4):
            ready[4 * k + s, pl.ds(384, 128), :] = wide[CAP + s].T.astype(BF16)
        for s in range(CAP):
            ready[s, at, :] = wide[s].T.astype(BF16)
            if k == len(chunks) - 1:
                copies.append(pltpu.make_async_copy(ready.at[s], out.at[s], sem.at[s]))
                copies[-1].start()
    for copy in copies:
        copy.wait()


def unpacked(messages, tails):
    anywhere = pl.BlockSpec(memory_space=pl.ANY)
    out = pl.pallas_call(
        unpack,
        out_shape=jax.ShapeDtypeStruct((CAP, ENT, DEVICES), BF16),
        in_specs=[anywhere] * 2,
        out_specs=anywhere,
        scratch_shapes=[
            pltpu.VMEM((DEVICES * ROWS, LANES), BF16),
            pltpu.VMEM((DEVICES, 256), BF16),
            pltpu.VMEM((2, DEVICES, 128), F32),
            pltpu.VMEM((2, DEVICES, 128), F32),
            pltpu.VMEM((CAP, ENT, DEVICES), BF16),
            pltpu.SemaphoreType.DMA((CAP + 4,)),
        ],
        compiler_params=pltpu.CompilerParams(vmem_limit_bytes=58 * 1024 * 1024),
        name="unpack",
    )(messages, tails)
    return out.transpose(2, 0, 1)[None]


def per_device(density, pattern, keep, owner):
    return unpacked(*stepped(density, pattern, keep, owner))


def solution(mesh):
    placed = (
        P(None, "row", "col"),
        P(None, "row", "col"),
        P(None, "row", "col"),
        P(("row", "col"), None, None),
    )
    return jax.shard_map(
        per_device,
        mesh=mesh,
        in_specs=placed,
        out_specs=P(("row", "col"), None, None, None),
        check_vma=False,
    )
```

```python
import jax
import jax.numpy as jnp
from jax import lax
from jax.experimental import pallas as pl
from jax.experimental.pallas import tpu as pltpu
from jax.sharding import PartitionSpec as P

BS = 23
PB = 16
W = BS * PB
WP = 384
ORDER = 5888
NROW = 8
NCOL = 16
DEVICES = NROW * NCOL
CAP = 12
ENT = BS * BS
ROWS = 16
LANES = 384
TAIL = 21
MESH = pl.DeviceIdType.MESH
F32 = jnp.float32
BF16 = jnp.bfloat16


QUARTERS = ((0, 0, 240), (0, 240, W), (1, 0, 240), (1, 240, W))

OWN, SEND, WAIT, DO = range(4)
LEFT, SIBLING, RIGHT, SQUARE = range(4)
CORE, YA, YB, YY, ZP, ZM, XP, XM = range(8)
PREPARE, FIRST_PAIRS, EARLY, LATE, NEAR_OWN, FAR_OWN, NEAR_OTHER, FAR_OTHER = range(8)
FIRST_GATHER = (
    (OWN, 0), (SEND, LEFT, 0, 1, 0, LEFT, 0, 0, YA), (SEND, LEFT, -1, 0, 0, LEFT, 0, 0, ZP), (WAIT, SIBLING, 0, 0, 0),
    (SEND, SIBLING, 0, 0, 0, LEFT, 0, 0, CORE), (SEND, LEFT, 1, 0, 1, LEFT, 0, 0, ZM),
    (SEND, RIGHT, -1, 0, 1, RIGHT, 0, 0, XP), (WAIT, RIGHT, 1, 0, 0), (SEND, RIGHT, 1, 0, 0, RIGHT, 0, 0, XM),
    (SEND, RIGHT, -1, 0, 0, RIGHT, 0, 0, XP), (SEND, LEFT, -1, 0, 1, LEFT, 0, 0, ZP),
    (SEND, LEFT, 1, 0, 0, LEFT, 0, 0, ZM), (WAIT, SIBLING, 0, 0, 1), (SEND, SIBLING, 0, 0, 1, LEFT, 0, 0, CORE),
    (OWN, 1), (SEND, LEFT, 0, 1, 1, LEFT, 0, 0, YA), (WAIT, SIBLING, 0, 0, 2),
    (SEND, SIBLING, 0, 0, 2, LEFT, 0, 0, CORE), (SEND, RIGHT, 1, 0, 3, RIGHT, 0, 0, XM), (WAIT, SIBLING, 0, 0, 3),
    (SEND, SIBLING, 0, 0, 3, LEFT, 0, 0, CORE), (DO, PREPARE), (SEND, LEFT, -1, 0, 3, LEFT, 0, 0, ZP),
    (SEND, LEFT, 0, 1, 2, LEFT, 0, 0, YA), (SEND, LEFT, 1, 0, 2, LEFT, 0, 0, ZM), (WAIT, RIGHT, 1, 0, 1),
    (SEND, RIGHT, 1, 0, 1, RIGHT, 0, 0, XM), (SEND, RIGHT, -1, 0, 2, RIGHT, 0, 0, XP), (WAIT, LEFT, 1, 0, 1),
    (WAIT, SIBLING, 1, 0, 1), (SEND, SIBLING, 1, 0, 1, LEFT, 1, 0, CORE), (SEND, LEFT, -1, 0, 2, LEFT, 0, 0, ZP),
    (WAIT, RIGHT, -1, 0, 1), (WAIT, LEFT, 0, 1, 0), (SEND, RIGHT, 0, 1, 0, LEFT, 0, 1, YB), (WAIT, SIBLING, 0, 1, 0),
    (SEND, SIBLING, 0, 1, 0, LEFT, 0, 1, CORE), (SEND, LEFT, 0, 1, 3, LEFT, 0, 0, YA), (WAIT, RIGHT, 1, 0, 2),
    (SEND, RIGHT, 1, 0, 2, RIGHT, 0, 0, XM), (WAIT, LEFT, -1, 0, 0), (WAIT, SIBLING, -1, 0, 0),
    (SEND, SIBLING, -1, 0, 0, LEFT, -1, 0, CORE), (SEND, LEFT, 1, 0, 3, LEFT, 0, 0, ZM), (WAIT, RIGHT, 2, 0, 1),
    (SEND, RIGHT, 2, 0, 1, RIGHT, -1, 0, XP), (WAIT, LEFT, 0, 1, 1), (WAIT, SIBLING, 0, 1, 1),
    (SEND, SIBLING, 0, 1, 1, LEFT, 0, 1, CORE), (SEND, RIGHT, 0, 1, 1, LEFT, 0, 1, YB), (WAIT, LEFT, -1, 0, 1),
    (SEND, LEFT, -1, 1, 0, LEFT, -1, 0, YA), (WAIT, SIBLING, -1, 0, 1), (SEND, SIBLING, -1, 0, 1, LEFT, -1, 0, CORE),
    (SEND, LEFT, 2, 0, 1, LEFT, -1, 0, ZP), (WAIT, LEFT, 1, 0, 0), (SEND, LEFT, 1, 1, 0, LEFT, 0, 1, ZM),
    (WAIT, SIBLING, 1, 0, 0), (SEND, SIBLING, 1, 0, 0, LEFT, 1, 0, CORE), (SEND, RIGHT, -1, 0, 3, RIGHT, 0, 0, XP),
    (WAIT, RIGHT, -1, 0, 0), (WAIT, RIGHT, 1, 0, 3), (WAIT, RIGHT, 2, 0, 3), (SEND, RIGHT, 2, 0, 3, RIGHT, 1, 0, XM),
    (WAIT, LEFT, -1, 0, 3), (WAIT, SIBLING, -1, 0, 3), (SEND, SIBLING, -1, 0, 3, LEFT, -1, 0, CORE),
    (WAIT, LEFT, 0, 1, 2), (SEND, LEFT, 2, 0, 0, LEFT, -1, 0, ZP), (WAIT, SIBLING, 0, 1, 2),
    (SEND, SIBLING, 0, 1, 2, LEFT, 0, 1, CORE), (SEND, RIGHT, 0, 1, 2, LEFT, 0, 1, YB),
    (SEND, LEFT, -1, 1, 3, LEFT, -1, 0, YA), (SEND, RIGHT, 2, 0, 0, RIGHT, -1, 0, XP), (WAIT, RIGHT, 0, 1, 0),
    (SEND, LEFT, 1, 1, 2, LEFT, 0, 1, ZM), (WAIT, RIGHT, 1, 1, 0), (SEND, RIGHT, 1, 1, 0, RIGHT, 0, 1, XM),
    (WAIT, LEFT, 1, 0, 2), (WAIT, SIBLING, 1, 0, 2), (SEND, SIBLING, 1, 0, 2, LEFT, 1, 0, CORE),
    (WAIT, RIGHT, -1, 0, 2), (WAIT, LEFT, 0, 1, 3), (WAIT, SIBLING, 0, 1, 3),
    (SEND, SIBLING, 0, 1, 3, LEFT, 0, 1, CORE), (SEND, RIGHT, 0, 1, 3, LEFT, 0, 1, YB), (WAIT, LEFT, -1, 0, 2),
    (SEND, LEFT, 1, 1, 1, LEFT, 1, 0, YA), (WAIT, SIBLING, -1, 0, 2), (SEND, SIBLING, -1, 0, 2, LEFT, -1, 0, CORE),
    (SEND, LEFT, 2, 0, 3, LEFT, -1, 0, ZP), (WAIT, RIGHT, 0, 1, 1), (WAIT, RIGHT, 2, 0, 2),
    (SEND, RIGHT, 2, 0, 2, RIGHT, -1, 0, XP), (WAIT, LEFT, 1, 0, 3), (SEND, RIGHT, 1, 1, 1, RIGHT, 0, 1, XM),
    (WAIT, SIBLING, 1, 0, 3), (SEND, SIBLING, 1, 0, 3, LEFT, 1, 0, CORE), (WAIT, LEFT, 2, 0, 1),
    (WAIT, SIBLING, 2, 0, 1), (SEND, SIBLING, 2, 0, 1, LEFT, 2, 0, CORE), (WAIT, RIGHT, -1, 1, 1),
    (SEND, RIGHT, -1, 1, 1, RIGHT, -1, 0, YY), (SEND, LEFT, 2, 0, 2, LEFT, 1, 0, ZM), (WAIT, RIGHT, -1, 0, 3),
    (SEND, LEFT, -1, 1, 1, LEFT, 0, 1, ZP), (WAIT, LEFT, -1, 1, 0), (WAIT, SIBLING, -1, 1, 0),
    (SEND, SIBLING, -1, 1, 0, LEFT, -1, 1, CORE), (WAIT, LEFT, 1, 1, 0), (WAIT, SIBLING, 1, 1, 0),
    (SEND, SIBLING, 1, 1, 0, LEFT, 1, 1, CORE), (WAIT, RIGHT, 0, 1, 2), (SEND, RIGHT, -1, 1, 3, RIGHT, -1, 0, YY),
    (SEND, LEFT, 2, 1, 0, LEFT, -1, 1, ZP), (SEND, RIGHT, 1, 1, 2, RIGHT, 0, 1, XM), (WAIT, LEFT, -1, 1, 3),
    (WAIT, SIBLING, -1, 1, 3), (SEND, SIBLING, -1, 1, 3, LEFT, -1, 1, CORE), (WAIT, RIGHT, -1, 1, 2),
    (SEND, RIGHT, -1, 1, 2, RIGHT, 0, 1, XP), (WAIT, LEFT, 2, 0, 0), (WAIT, SIBLING, 2, 0, 0),
    (SEND, SIBLING, 2, 0, 0, LEFT, 2, 0, CORE), (SEND, LEFT, 1, 1, 3, LEFT, 0, 1, ZM),
    (SEND, LEFT, -1, 1, 2, LEFT, -1, 0, YA), (WAIT, RIGHT, 2, 0, 0), (WAIT, RIGHT, 0, 1, 3), (WAIT, RIGHT, 1, 1, 3),
    (SEND, RIGHT, 1, 1, 3, RIGHT, 0, 1, XM), (WAIT, LEFT, 1, 1, 1), (WAIT, SIBLING, 1, 1, 1),
    (SEND, SIBLING, 1, 1, 1, LEFT, 1, 1, CORE), (WAIT, LEFT, 1, 1, 2), (WAIT, SIBLING, 1, 1, 2),
    (SEND, SIBLING, 1, 1, 2, LEFT, 1, 1, CORE), (WAIT, LEFT, 2, 0, 3), (SEND, LEFT, 2, 1, 2, LEFT, 1, 1, ZM),
    (SEND, LEFT, 2, 1, 3, LEFT, -1, 1, ZP), (WAIT, RIGHT, -1, 1, 0), (SEND, RIGHT, -1, 1, 0, RIGHT, 0, 1, XP),
    (WAIT, SIBLING, 2, 0, 3), (SEND, SIBLING, 2, 0, 3, LEFT, 2, 0, CORE), (WAIT, RIGHT, 1, 1, 1),
    (WAIT, RIGHT, 2, 1, 1), (SEND, RIGHT, 2, 1, 1, RIGHT, 1, 1, XM), (WAIT, LEFT, -1, 1, 1),
    (WAIT, SIBLING, -1, 1, 1), (SEND, SIBLING, -1, 1, 1, LEFT, -1, 1, CORE), (WAIT, RIGHT, 2, 1, 0),
    (SEND, RIGHT, 2, 1, 0, RIGHT, 2, 0, YY), (SEND, LEFT, 2, 1, 1, LEFT, -1, 1, ZP), (WAIT, LEFT, 2, 0, 2),
    (WAIT, SIBLING, 2, 0, 2), (SEND, SIBLING, 2, 0, 2, LEFT, 2, 0, CORE), (WAIT, RIGHT, 1, 1, 2),
    (WAIT, RIGHT, 2, 1, 2), (SEND, RIGHT, 2, 1, 2, RIGHT, 1, 1, XM), (WAIT, RIGHT, -1, 1, 3), (WAIT, RIGHT, 2, 1, 3),
    (SEND, RIGHT, 2, 1, 3, RIGHT, -1, 1, XP), (DO, FIRST_PAIRS), (WAIT, LEFT, 1, 1, 3), (WAIT, SIBLING, 1, 1, 3),
    (SEND, SIBLING, 1, 1, 3, LEFT, 1, 1, CORE), (WAIT, LEFT, 2, 1, 0), (WAIT, SIBLING, 2, 1, 0),
    (SEND, SIBLING, 2, 1, 0, LEFT, 2, 1, CORE), (WAIT, LEFT, -1, 1, 2), (WAIT, SIBLING, -1, 1, 2),
    (SEND, SIBLING, -1, 1, 2, LEFT, -1, 1, CORE), (WAIT, LEFT, 2, 1, 3), (WAIT, SIBLING, 2, 1, 3),
    (SEND, SIBLING, 2, 1, 3, LEFT, 2, 1, CORE), (WAIT, LEFT, 2, 1, 2), (WAIT, SIBLING, 2, 1, 2),
    (SEND, SIBLING, 2, 1, 2, LEFT, 2, 1, CORE), (WAIT, LEFT, 2, 1, 1), (WAIT, SIBLING, 2, 1, 1),
    (SEND, SIBLING, 2, 1, 1, LEFT, 2, 1, CORE), (DO, EARLY),
)

SECOND_GATHER = (
    (OWN, 0), (SEND, SQUARE, 0, 1, 1, SQUARE, 0, 0, YY), (WAIT, SQUARE, 1, 0, 0),
    (SEND, SQUARE, 1, 0, 0, SQUARE, 0, 0, XM), (SEND, SQUARE, 0, 1, 0, SQUARE, 0, 0, YY),
    (SEND, SQUARE, -1, 0, 1, SQUARE, 0, 0, XP), (SEND, SQUARE, -1, 0, 0, SQUARE, 0, 0, XP), (OWN, 1),
    (SEND, SQUARE, 1, 0, 3, SQUARE, 0, 0, XM), (WAIT, SQUARE, -1, 0, 1), (SEND, SQUARE, 0, 1, 3, SQUARE, 0, 0, YY),
    (WAIT, SQUARE, -1, 0, 3), (SEND, SQUARE, -1, 0, 3, SQUARE, 0, 0, XP), (WAIT, SQUARE, 2, 0, 1),
    (SEND, SQUARE, 2, 0, 1, SQUARE, -1, 0, XP), (WAIT, SQUARE, 1, 0, 1), (SEND, SQUARE, 1, 0, 1, SQUARE, 0, 0, XM),
    (SEND, SQUARE, 1, 0, 2, SQUARE, 0, 0, XM), (WAIT, SQUARE, 0, 1, 2), (SEND, SQUARE, 0, 1, 2, SQUARE, 0, 0, YY),
    (WAIT, SQUARE, 0, 1, 1), (WAIT, SQUARE, 1, 0, 3), (SEND, SQUARE, -1, 0, 2, SQUARE, 0, 0, XP),
    (WAIT, SQUARE, -1, 0, 0), (SEND, SQUARE, -1, 1, 0, SQUARE, -1, 0, YY), (WAIT, SQUARE, 1, 1, 1),
    (SEND, SQUARE, 1, 1, 1, SQUARE, 0, 1, XM), (WAIT, SQUARE, 0, 1, 0), (WAIT, SQUARE, 0, 1, 3),
    (WAIT, SQUARE, -1, 1, 3), (SEND, SQUARE, -1, 1, 3, SQUARE, 0, 1, XP), (WAIT, SQUARE, 2, 0, 3),
    (SEND, SQUARE, 2, 0, 3, SQUARE, 1, 0, XM), (WAIT, SQUARE, 1, 0, 2), (SEND, SQUARE, 2, 0, 2, SQUARE, 1, 0, XM),
    (WAIT, SQUARE, 1, 1, 2), (SEND, SQUARE, 1, 1, 2, SQUARE, 1, 0, YY), (SEND, SQUARE, -1, 1, 1, SQUARE, 0, 1, XP),
    (WAIT, SQUARE, -1, 0, 2), (SEND, SQUARE, 1, 1, 3, SQUARE, 0, 1, XM), (WAIT, SQUARE, -1, 1, 2),
    (SEND, SQUARE, -1, 1, 2, SQUARE, -1, 0, YY), (WAIT, SQUARE, 2, 0, 0), (SEND, SQUARE, 2, 0, 0, SQUARE, -1, 0, XP),
    (DO, NEAR_OWN), (WAIT, SQUARE, -1, 1, 0), (WAIT, SQUARE, 2, 1, 0), (SEND, SQUARE, 2, 1, 0, SQUARE, -1, 1, XP),
    (WAIT, SQUARE, 1, 1, 0), (SEND, SQUARE, 1, 1, 0, SQUARE, 0, 1, XM), (WAIT, SQUARE, -1, 1, 1),
    (WAIT, SQUARE, 2, 0, 2), (WAIT, SQUARE, 2, 1, 2), (SEND, SQUARE, 2, 1, 2, SQUARE, 2, 0, YY),
    (WAIT, SQUARE, 1, 1, 3), (WAIT, SQUARE, 2, 1, 3), (SEND, SQUARE, 2, 1, 3, SQUARE, 1, 1, XM),
    (WAIT, SQUARE, 2, 1, 1), (SEND, SQUARE, 2, 1, 1, SQUARE, -1, 1, XP), (DO, FAR_OWN), (DO, NEAR_OTHER),
    (DO, FAR_OTHER),
)


FORWARDED = {(*op[5:8], op[4]) for op in FIRST_GATHER + SECOND_GATHER if op[0] == SEND}
GROUPS = 11


def group_of(kind, d, f, q):
    if (kind, d, f, q) in FORWARDED:
        return None
    if kind == SQUARE:
        return (NEAR_OTHER if d < 2 else FAR_OTHER) if f else (NEAR_OWN if d < 2 else FAR_OWN)
    work = LATE if (d, f) == (2, 1) else EARLY if f and (d or kind == RIGHT) else FIRST_PAIRS
    return 7 + work if kind == SIBLING else work


def grow_columns(mask):
    block = lax.broadcasted_iota(jnp.int32, (PB, WP), 0)
    col = lax.broadcasted_iota(jnp.int32, (PB, WP), 1)
    spread = jnp.where((col >= block * BS) & (col < block * BS + BS), 1.0, 0.0).astype(BF16)
    return jnp.dot(mask, spread, preferred_element_type=F32).astype(BF16)


def grow(mask):
    wide = grow_columns(mask.astype(F32).astype(BF16))
    row = lax.broadcasted_iota(jnp.int32, (W, PB), 0)
    block = lax.broadcasted_iota(jnp.int32, (W, PB), 1)
    spread = jnp.where((row >= block * BS) & (row < block * BS + BS), 1.0, 0.0).astype(BF16)
    return jnp.dot(spread, wide, preferred_element_type=F32)


def whole_step(
    dens_in, pat_in, keep_in, owner_in, arrived, tails_arrived,
    dens, pat, keep, owner, left, right, sq, mask, kept, acc, update, place, hot, hot_tail, rank_at, tail_at, blocks, outgoing,
    tails, relay_in, relay_wide, relay_out, send, recv, exchange_send, exchange_recv, tail_send, tail_recv, local,
):
    r = lax.axis_index("row")
    c = lax.axis_index("col")
    x, yh = lax.rem(r, 4), lax.div(r, 4)
    z, yl, core = lax.div(c, 4), lax.rem(lax.div(c, 2), 2), lax.rem(c, 2)
    me = r * NCOL + c

    def col(dz, dyl, dcore=0):
        ycol = (1 - yl) if dyl else yl
        ccol = (1 - core) if dcore else core
        return lax.rem(z + dz + 4, 4) * 4 + ycol * 2 + ccol

    def row(dx, dyh):
        yrow = (1 - yh) if dyh else yh
        return yrow * 4 + lax.rem(x + dx + 4, 4)

    ways = {
        CORE: (r, col(0, 0, 1)),
        YA: (r, col(0, 1)),
        YB: (row(0, 1), col(0, 1)),
        YY: (row(0, 1), c),
        ZP: (r, col(1, 0)),
        ZM: (r, col(-1, 0)),
        XP: (row(1, 0), c),
        XM: (row(-1, 0), c),
    }

    fetches = [
        pltpu.make_async_copy(src, dst, local.at[k])
        for k, (src, dst) in enumerate(((pat_in, pat), (dens_in, dens), (keep_in, keep), (owner_in, owner)))
    ]
    for fetch in fetches:
        fetch.start()
    barrier = pltpu.get_barrier_semaphore()
    for dev in ways.values():
        pl.semaphore_signal(barrier, inc=1, device_id=dev, device_id_type=MESH)

    started = [0, 0]
    arriving = {}
    expected = [0] * GROUPS

    def piece(buf, slot, q):
        h, first, end = QUARTERS[q]
        return buf.at[slot, h, pl.ds(first, end - first)]

    def find(kind, d, f, q):
        if kind == LEFT:
            return piece(left, col(d, f), q)
        if kind == SIBLING:
            return piece(left, col(d, f, 1), q)
        return piece(right if kind == RIGHT else sq, row(d, f), q)

    def start(kind, d, f, q, from_kind, from_d, from_f, way):
        k = group_of(kind, d, f, q)
        if k is None:
            k = GROUPS + len(arriving)
        else:
            _, first, end = QUARTERS[q]
            expected[k] += end - first
        group = 0 if kind in (LEFT, SIBLING) else 1
        if kind == RIGHT:
            src = piece(left, c, q) if (from_d, from_f) == (0, 0) else find(from_kind, from_d, from_f, q)
            dst = piece(right, r if from_kind == LEFT else row(from_d, from_f), q)
        else:
            src = dst = find(from_kind, from_d, from_f, q)
        op = pltpu.make_async_remote_copy(
            src_ref=src, dst_ref=dst, send_sem=send.at[group], recv_sem=recv.at[k],
            device_id=ways[way], device_id_type=MESH)
        op.start()
        started[group] += QUARTERS[q][2] - QUARTERS[q][1]
        if k < GROUPS:
            return
        here = find(kind, d, f, q)
        arriving[kind, d, f, q] = pltpu.make_async_remote_copy(
            src_ref=here, dst_ref=here, send_sem=send.at[group], recv_sem=recv.at[k],
            device_id=ways[way], device_id_type=MESH)

    def join(group):
        rows = expected[group]
        if rows == 0:
            return
        all_rows = left.at[pl.ds(0, rows // (2 * W))] if rows % (2 * W) == 0 else outgoing.at[pl.ds(0, rows)]
        pltpu.make_async_remote_copy(
            src_ref=all_rows, dst_ref=all_rows, send_sem=send.at[0], recv_sem=recv.at[group],
            device_id=ways[CORE], device_id_type=MESH).wait_recv()

    def follow(table, own, work):
        for op, *what in table:
            if op == OWN:
                own(what[0])
            elif op == SEND:
                start(*what)
            elif op == WAIT:
                if group_of(*what) is None:
                    arriving[tuple(what)].wait_recv()
            else:
                join(what[0])
                work[what[0]]()

    def multiply(p, buf, h):
        if h is None:
            two = [left[2 * p + k].reshape(2 * W, WP) for k in range(2)]
            at = pl.ds(0, 2 * W)
        else:
            two = [left[2 * p + k, h] for k in range(2)]
            at = pl.ds(h * W, W)
        rows = buf[pl.ds(lax.rem(2 * p, NROW), 2), lax.div(p, 4)].reshape(2 * WP, WP)
        acc[at, :] += jnp.dot(jnp.concatenate(two, axis=1), rows, preferred_element_type=F32)

    def is_last_left(p):
        return (lax.div(p, 2) == lax.rem(z + 2, 4)) & (lax.rem(p, 2) == 1 - yl)

    def is_late(p):
        zp, yp = lax.div(p, 2), lax.rem(p, 2)
        in_left = is_last_left(p)
        in_right = (lax.rem(zp, 2) == 1 - yh) & (yp == lax.div(lax.rem(x + 2, 4), 2))
        return in_left | in_right

    def own_density(h):
        m = grow(pat[h]).astype(BF16)
        left[c, h, :, pl.ds(256, 128)] = jnp.zeros((W, 128), BF16)
        left[c, h, :, pl.ds(0, W)] = dens[h] * m[:, :W]
        mask[h] = m
        if h == 0:
            pl.semaphore_wait(barrier, len(ways))

    def prepare():
        for h in range(2):
            right[r, h, pl.ds(0, W)] = left[c, h]
        zero = jnp.zeros((2, WP - W, WP), BF16)

        def clear(k, carry):
            right[k, :, pl.ds(W, WP - W)] = zero
            sq[k, :, pl.ds(W, WP - W)] = zero
            return carry

        lax.fori_loop(0, NROW, clear, 0)
        acc[...] = jnp.zeros_like(acc)
        fetches[2].wait()
        fetches[3].wait()
        for h in range(2):
            kept[h] = grow(keep[h]).astype(BF16)
        routing_tables(owner, place, hot, hot_tail, rank_at, tail_at)

    def is_first(p):
        zp, yp = lax.div(p, 2), lax.rem(p, 2)
        return (lax.rem(zp, 2) == yh) & ((yp == yl) | (zp == z)) & jnp.logical_not(is_late(p))

    def pairs(chosen, group):
        def add(p, carry):
            @pl.when(chosen(p))
            def _():
                multiply(p, right, None)
            return carry

        join(7 + group)
        lax.fori_loop(0, NCOL // 2, add, 0)

    fetches[0].wait()
    fetches[1].wait()
    follow(FIRST_GATHER, own_density, {
        PREPARE: prepare,
        FIRST_PAIRS: lambda: pairs(is_first, FIRST_PAIRS),
        EARLY: lambda: pairs(lambda p: jnp.logical_not(is_first(p) | is_late(p)), EARLY),
    })

    def own_square(h):
        def add(p, carry):
            @pl.when(is_late(p) & jnp.logical_not(is_last_left(p)))
            def _():
                multiply(p, right, h)
            return carry

        if h == 0:
            join(LATE)
        lax.fori_loop(0, NCOL // 2, add, 0)
        if h == 0:
            join(7 + LATE)
        multiply(lax.rem(z + 2, 4) * 2 + 1 - yl, right, h)
        half = pl.ds(h * W, W)
        sq[r, h, pl.ds(0, W)] = (acc[half, :] / ORDER * mask[h].astype(F32)).astype(BF16)
        acc[half, :] = jnp.zeros((W, WP), F32)

    near = lax.div(x, 2)

    def second(yhp, pair):
        def add(h, carry):
            multiply((2 * h + yhp) * 2 + pair, sq, None)
            return carry

        lax.fori_loop(0, 2, add, 0)

    follow(SECOND_GATHER, own_square, {
        NEAR_OWN: lambda: second(yh, near),
        FAR_OWN: lambda: second(yh, 1 - near),
        NEAR_OTHER: lambda: second(1 - yh, near),
        FAR_OTHER: lambda: second(1 - yh, 1 - near),
    })

    for h in range(2):
        mat = left[c, h].astype(F32)
        new = kept[h].astype(F32) * (1.5 * mat - 0.5 * acc[pl.ds(h * W, W), :])
        for k in range(WP // 128):
            update[h, k] = new[:, k * 128 : k * 128 + 128]

    def rows_of(buf, device):
        return buf.at[pl.ds(pl.multiple_of(device * ROWS, ROWS), ROWS)]

    def messages(yhp, xp, first):
        at = pl.ds(pl.multiple_of((yhp * 2 + xp) * 512, 512), 512)
        outgoing[at, :] = jnp.dot(hot[at, :], blocks[...], preferred_element_type=F32).astype(BF16)

        def start_message(i, carry):
            i = lax.rem(i * 13, 32)
            dz, dyl, dcore, dx = lax.div(i, 8), lax.rem(lax.div(i, 4), 2), lax.rem(lax.div(i, 2), 2), lax.rem(i, 2)
            to_row = yhp * 4 + xp * 2 + lax.rem(x + dx, 2)
            to_col = lax.rem(z + dz, 4) * 4 + lax.rem(yl + dyl, 2) * 2 + lax.rem(core + dcore, 2)
            pltpu.make_async_remote_copy(
                src_ref=rows_of(outgoing, to_row * NCOL + to_col), dst_ref=rows_of(arrived, me),
                send_sem=exchange_send, recv_sem=exchange_recv, device_id=(to_row, to_col), device_id_type=MESH).start()
            return carry

        def start_two(i, carry):
            return start_message(i + 16, start_message(i, carry))

        if first == 1:
            start_message(16, 0)
        lax.fori_loop(first, 16, start_two, 0)

    line, in_line = r * 2 + yl, z * 2 + core

    def other_line(i):
        dyl, dyh, dx = i % 2, i // 2 % 2, i // 4
        return row(dx, dyh), yl if dyl == 0 else 1 - yl

    def line_copy(to, here, device):
        return pltpu.make_async_remote_copy(
            src_ref=to, dst_ref=here, send_sem=tail_send.at[0], recv_sem=tail_recv.at[0],
            device_id=device, device_id_type=MESH)

    def pass_on(to, here, device):
        return pltpu.make_async_remote_copy(
            src_ref=to, dst_ref=here, send_sem=tail_send.at[1], recv_sem=tail_recv.at[1],
            device_id=device, device_id_type=MESH)

    all_lines = line_copy(tails.at[pl.ds(0, (2 * NROW - 1) * ROWS)], relay_in.at[pl.ds(0, (2 * NROW - 1) * ROWS)],
                          ways[CORE])
    keep_line = pltpu.make_async_copy(rows_of(tails, line), rows_of(relay_in, line), local.at[5])

    def send_tails():
        for i in range(1, 2 * NROW):
            to_row, to_yl = other_line(i)
            line_copy(rows_of(tails, to_row * 2 + to_yl), rows_of(relay_in, line),
                      (to_row, z * 4 + to_yl * 2 + core)).start()
        keep_line.start()

    fill(update, rank_at, tail_at, place, hot_tail, blocks, tails, send_tails)

    messages(1 - yh, 1 - near, 0)
    messages(yh, 1 - near, 0)
    keep_line.wait()
    all_lines.wait_recv()
    relay_wide[...] = relay_in[...].astype(F32)
    for j in range(2 * 4):
        for k in range(2):
            part = relay_wide[pl.ds(2 * j + k, 2 * NROW, stride=ROWS), :]
            relay_out[pl.ds(j * ROWS, ROWS), pl.ds(128 * k, 128)] = part.astype(BF16)
    for i in range(1, 2 * 4):
        to_core = core if i % 2 == 0 else 1 - core
        to_z = lax.rem(z + i // 2, 4)
        pass_on(rows_of(relay_out, to_z * 2 + to_core), rows_of(tails_arrived, in_line),
                (r, to_z * 4 + yl * 2 + to_core)).start()
    all_passed = pass_on(relay_out.at[pl.ds(0, 7 * ROWS)], tails_arrived.at[pl.ds(0, 7 * ROWS)], ways[CORE])
    keep_tails = pltpu.make_async_copy(rows_of(relay_out, in_line), rows_of(tails_arrived, in_line), local.at[6])
    keep_tails.start()
    messages(1 - yh, near, 0)
    messages(yh, near, 1)
    own = pltpu.make_async_copy(rows_of(outgoing, me), rows_of(arrived, me), local.at[4])
    own.start()
    for group, rows in enumerate(started):
        sent = left.at[pl.ds(0, rows // (2 * W))]
        pltpu.make_async_remote_copy(
            src_ref=sent, dst_ref=sent, send_sem=send.at[group], recv_sem=recv.at[group],
            device_id=ways[CORE], device_id_type=MESH).wait_send()
    own.wait()
    keep_tails.wait()
    all_lines.wait_send()
    all_passed.wait_send()
    most = pl.ds(0, (DEVICES - 1) * ROWS)
    others = pltpu.make_async_remote_copy(
        src_ref=outgoing.at[most], dst_ref=arrived.at[most],
        send_sem=exchange_send, recv_sem=exchange_recv, device_id=ways[CORE], device_id_type=MESH)
    others.wait_send()
    others.wait_recv()
    all_passed.wait_recv()


N_BLOCKS = 2 * PB * PB


WINDOWS = [
    (w, i) for w in range(3) for i in range(BS) if i * BS + BS > w * 256 and i * BS < w * 256 + 256
]


def ranks(owner_row):
    owner = jnp.broadcast_to(owner_row.astype(F32), (8, N_BLOCKS))
    same = owner.T[:, :1] == owner[:1]
    one = lax.broadcasted_iota(jnp.int32, (N_BLOCKS, N_BLOCKS), 0)
    two = lax.broadcasted_iota(jnp.int32, (N_BLOCKS, N_BLOCKS), 1)
    rank = jnp.sum(jnp.where(same & (one < two), 1.0, 0.0), axis=0, keepdims=True).astype(jnp.int32)
    rank_col = jnp.sum(jnp.where(same & (two < one), 1.0, 0.0), axis=1, keepdims=True).astype(jnp.int32)
    return rank, rank_col


def routing_tables(owner, place, hot, hot_tail, rank_at, tail_at):
    lane = lax.broadcasted_iota(jnp.int32, (WP, 256), 0)
    at = lax.broadcasted_iota(jnp.int32, (WP, 256), 1)
    entry = lane - lax.div(lane, BS) * BS
    slot = lax.div(at, TAIL)
    def spread(k, carry):
        w = lax.div(k, 12)
        place[k] = jnp.where(at - entry == (k - w) * BS - w * 256, 1.0, 0.0).astype(BF16)
        return carry

    lax.fori_loop(0, 24, spread, 0)
    offset = at - slot * TAIL
    fits = (slot < 6) & (offset - entry == (BS - 1) * BS - 512) & (offset < ENT - 512)
    place[24] = jnp.where(fits, 1.0, 0.0).astype(BF16)
    rank, rank_col = ranks(owner[...])
    rank_at[...] = jnp.broadcast_to(rank_col, rank_at.shape)
    group = lax.div(lax.broadcasted_iota(jnp.int32, tail_at.shape, 1), TAIL)
    tail_at[...] = jnp.where(rank_col - lax.div(rank_col, 6) * 6 == group, 1.0, 0.0)
    own = owner[...]
    key = own * ROWS + rank
    last_key = own * ROWS + CAP + rank - lax.div(rank, 4) * 4
    to_row, to_col = lax.div(own, NCOL), lax.rem(own, NCOL)
    line = to_row * 2 + lax.rem(lax.div(to_col, 2), 2)
    in_line = lax.div(to_col, 4) * 2 + lax.rem(to_col, 2)
    tail_key = line * ROWS + in_line * 2 + lax.div(rank, 6)
    step = 256

    def compare(k, carry):
        rows = pl.ds(pl.multiple_of(k * step, step), step)
        at = lax.broadcasted_iota(jnp.int32, (step, N_BLOCKS), 0) + k * step
        hot[rows, pl.ds(0, N_BLOCKS)] = jnp.where(at == key, 1.0, 0.0).astype(BF16)
        hot[rows, pl.ds(N_BLOCKS, N_BLOCKS)] = jnp.where(at == last_key, 1.0, 0.0).astype(BF16)
        return carry

    lax.fori_loop(0, DEVICES * ROWS // step, compare, 0)
    at = lax.broadcasted_iota(jnp.int32, hot_tail.shape, 0)
    hot_tail[...] = jnp.where(at == tail_key, 1.0, 0.0).astype(BF16)


def fill(update, rank_at, tail_at, place, hot_tail, blocks, tails, send_tails):
    n = N_BLOCKS
    half = PB // 2
    picks = []
    for g in range(2):
        bc = lax.broadcasted_iota(jnp.int32, (half, 256), 0) + g * half
        entry = lax.broadcasted_iota(jnp.int32, (half, 256), 1) + g * 128
        picks.append(jnp.where((entry >= bc * BS) & (entry < bc * BS + BS), 1.0, 0.0)[None])
    for w in (2, 0, 1):
        total = [None, None]
        for k, (wk, i) in enumerate(WINDOWS):
            if wk != w:
                continue
            u = [[update[h, j, pl.ds(i, PB, stride=BS), :] for j in range(WP // 128)] for h in range(2)]
            for g in range(2):
                rows = [
                    (jnp.concatenate(u[h][g : g + 2], axis=1)[:, None, :] * picks[g]).astype(BF16)
                    .reshape(PB * half, 256)
                    for h in range(2)
                ]
                term = jnp.dot(jnp.concatenate(rows, axis=0), place[k, pl.ds(128 * g, 256), :],
                               preferred_element_type=F32)
                total[g] = term if total[g] is None else total[g] + term
        both = [t.reshape(2 * PB, 1, half, 256) for t in total]
        both = jnp.concatenate(both, axis=1).reshape(n, 256)
        if w == 2:
            tail = (both[:, :128] * tail_at[...]).astype(BF16)
            tails[...] = jnp.dot(hot_tail[...], tail, preferred_element_type=F32).astype(BF16)
            send_tails()
        elif w == 0:
            blocks[pl.ds(0, n), pl.ds(0, 256)] = both.astype(BF16)
        else:
            blocks[pl.ds(0, n), pl.ds(256, 128)] = both[:, :128].astype(BF16)
            rank = rank_at[...]
            for j in range(3):
                mine = (rank >= 4 * j) & (rank < 4 * j + 4)
                blocks[pl.ds(n, n), pl.ds(128 * j, 128)] = jnp.where(mine, both[:, 128:], 0.0).astype(BF16)


N_ARRIVALS = GROUPS + sum(
    op[0] == SEND and group_of(*op[1:5]) is None for op in FIRST_GATHER + SECOND_GATHER)


def stepped(density, pattern, keep, owner):
    anywhere = pl.BlockSpec(memory_space=pl.ANY)
    owner = owner.reshape(1, N_BLOCKS)
    return pl.pallas_call(
        whole_step,
        out_shape=(
            jax.ShapeDtypeStruct((DEVICES * ROWS, LANES), BF16),
            jax.ShapeDtypeStruct((DEVICES, 256), BF16),
        ),
        in_specs=[anywhere] * 4,
        out_specs=(anywhere, anywhere),
        scratch_shapes=[
            pltpu.VMEM(density.shape, BF16),
            pltpu.VMEM(pattern.shape, jnp.int32),
            pltpu.VMEM(keep.shape, jnp.int32),
            pltpu.VMEM(owner.shape, jnp.int32),
            pltpu.VMEM((NCOL, 2, W, WP), BF16),
            pltpu.VMEM((NROW, 2, WP, WP), BF16),
            pltpu.VMEM((NROW, 2, WP, WP), BF16),
            pltpu.VMEM((2, W, WP), BF16),
            pltpu.VMEM((2, W, WP), BF16),
            pltpu.VMEM((2 * W, WP), F32),
            pltpu.VMEM((2, WP // 128, W, 128), F32),
            pltpu.VMEM((25, WP, 256), BF16),
            pltpu.VMEM((DEVICES * ROWS, 2 * N_BLOCKS), BF16),
            pltpu.VMEM((2 * NROW * ROWS, N_BLOCKS), BF16),
            pltpu.VMEM((N_BLOCKS, 128), jnp.int32),
            pltpu.VMEM((N_BLOCKS, 128), F32),
            pltpu.VMEM((2 * N_BLOCKS, LANES), BF16),
            pltpu.VMEM((DEVICES * ROWS, LANES), BF16),
            pltpu.VMEM((2 * NROW * ROWS, 128), BF16),
            pltpu.VMEM((2 * NROW * ROWS, 128), BF16),
            pltpu.VMEM((2 * NROW * ROWS, 128), F32),
            pltpu.VMEM((DEVICES, 256), BF16),
            pltpu.SemaphoreType.DMA((2,)),
            pltpu.SemaphoreType.DMA((N_ARRIVALS,)),
            pltpu.SemaphoreType.DMA,
            pltpu.SemaphoreType.DMA,
            pltpu.SemaphoreType.DMA((2,)),
            pltpu.SemaphoreType.DMA((2,)),
            pltpu.SemaphoreType.DMA((7,)),
        ],
        compiler_params=pltpu.CompilerParams(
            collective_id=0, has_side_effects=True, vmem_limit_bytes=56 * 1024 * 1024),
        name="whole_step",
    )(density, pattern, keep, owner)


def unpack(messages, tails, out, arrived, tails_in, tails_wide, by_source, ready, sem):
    chunks = [pl.ds(128 * k, 128) for k in range(LANES // 128)]
    fetches = [
        pltpu.make_async_copy(messages.at[:, at], arrived.at[:, at], sem.at[CAP + k])
        for k, at in enumerate(chunks)
    ]
    fetch_tails = pltpu.make_async_copy(tails, tails_in, sem.at[CAP + len(chunks)])
    fetch_tails.start()
    for fetch in fetches:
        fetch.start()

    fetch_tails.wait()
    for k in range(2):
        tails_wide[k] = tails_in[:, pl.ds(128 * k, 128)].astype(F32)
        for j in range(8):
            for yl in range(2):
                source = j // 2 * 4 + yl * 2 + j % 2
                by_source[k, pl.ds(source, NROW, stride=NCOL), :] = tails_wide[k, pl.ds(j * ROWS + yl, NROW, stride=2), :]
        rows = by_source[k].T.astype(BF16)
        for s in range(6):
            ready[6 * k + s, pl.ds(512, ENT - 512), :] = rows[s * TAIL : s * TAIL + ENT - 512]
    copies = []
    for k, at in enumerate(chunks):
        fetches[k].wait()
        wide = jnp.transpose(arrived[:, at].astype(F32).reshape(DEVICES, ROWS, 128), (1, 0, 2))
        for s in range(4):
            ready[4 * k + s, pl.ds(384, 128), :] = wide[CAP + s].T.astype(BF16)
        for s in range(CAP):
            ready[s, at, :] = wide[s].T.astype(BF16)
            if k == len(chunks) - 1:
                copies.append(pltpu.make_async_copy(ready.at[s], out.at[s], sem.at[s]))
                copies[-1].start()
    for copy in copies:
        copy.wait()


def unpacked(messages, tails):
    anywhere = pl.BlockSpec(memory_space=pl.ANY)
    out = pl.pallas_call(
        unpack,
        out_shape=jax.ShapeDtypeStruct((CAP, ENT, DEVICES), BF16),
        in_specs=[anywhere] * 2,
        out_specs=anywhere,
        scratch_shapes=[
            pltpu.VMEM((DEVICES * ROWS, LANES), BF16),
            pltpu.VMEM((DEVICES, 256), BF16),
            pltpu.VMEM((2, DEVICES, 128), F32),
            pltpu.VMEM((2, DEVICES, 128), F32),
            pltpu.VMEM((CAP, ENT, DEVICES), BF16),
            pltpu.SemaphoreType.DMA((CAP + 4,)),
        ],
        compiler_params=pltpu.CompilerParams(vmem_limit_bytes=58 * 1024 * 1024),
        name="unpack",
    )(messages, tails)
    return out.transpose(2, 0, 1)[None]


def per_device(density, pattern, keep, owner):
    return unpacked(*stepped(density, pattern, keep, owner))


def solution(mesh):
    placed = (
        P(None, "row", "col"),
        P(None, "row", "col"),
        P(None, "row", "col"),
        P(("row", "col"), None, None),
    )
    return jax.shard_map(
        per_device,
        mesh=mesh,
        in_specs=placed,
        out_specs=P(("row", "col"), None, None, None),
        check_vma=False,
    )
```
